32 devices in a mesh: groups: 2 (over y), blk: 4 (over x, core), sub: 4 (over z).
Axes of the slice: x: 2, y: 2, z: 4, core: 2. Of those that a mesh axis runs over, the one named last changes fastest.
Arguments:
- embeds: bfloat16 [32768, 1024], P(('groups', 'blk', 'sub')), parts along dimension 0, may hold values from -6 to 6
- pick_blk: int32 [32, 4], P(('groups', 'blk', 'sub')), parts along dimension 0, may hold values from 0 to 3
- mask_blk: int32 [32, 16], P(('groups', 'blk', 'sub')), parts along dimension 0, may hold values from 0 to 1, as said below
- pick_sub: int32 [32, 4], P(('groups', 'blk')), parts along dimension 0, may hold values from 0 to 3
- mask_sub: int32 [32, 16], P(('groups', 'blk', 'sub')), parts along dimension 0, may hold values from 0 to 1, as said below
Outputs:
- dup_frac: float32 [32768], P(('groups', 'blk', 'sub')), parts along dimension 0
The draws below stay inside these ranges and needn't reach their ends.
There are 2 independent parts, one for each index of `groups`. The reference program is written for one: setup_inputs(seed, part) draws one part's arguments, and reference() takes and returns one part's arrays. A program takes and returns all parts, laid end to end along the dimension named above; each array names one. Nothing has to cross between parts.
Inputs may be any that keep to these rules, and one draw needn't show every extreme that they name: mask_blk[e, p * 4 + i] is 0 where p is device e's own blk index. mask_sub[e, p * 4 + i] is 0 where p is device e's own sub index.
All inputs are finite; a program needn't handle non-finite values.
Results may differ from the reference program's by a relative error of at most 0.00086.
Values may be sent and summed in bfloat16 or wider, within the bound.
No kernel may reach another device: no remote copies, remote signals or barrier semaphores. Data moves between devices by JAX's collectives and lax.ppermute only.
A program may use at most 64 MiB of HBM per device.

```python
import jax
import jax.numpy as jnp
from jax import lax

D = 1024
BLOCK = 256
BPD = 4
BLK_PEERS = 4
SUB_PEERS = 4
DEVS = 16
ROWS = 16384


def live_pattern(key, slots, own_index):
    level_key, entry_key = jax.random.split(key)
    levels = jax.random.randint(level_key, (DEVS, 1, 1), 1, 9)
    levels = levels.at[0].set(8)
    entries = jax.random.randint(entry_key, (DEVS, slots, BPD), 0, 8)
    peer_ids = jnp.arange(slots, dtype=jnp.int32)[None, :, None]
    alive = (entries < levels) & (peer_ids != own_index[:, None, None])
    return alive.astype(jnp.int32).reshape(DEVS, slots * BPD)


def draw_mask_blk(key, part):
    key = jax.random.fold_in(key, 11)
    devices = jnp.arange(DEVS, dtype=jnp.int32)
    return live_pattern(key, BLK_PEERS, devices // SUB_PEERS)


def draw_mask_sub(key, part):
    key = jax.random.fold_in(key, 23)
    devices = jnp.arange(DEVS, dtype=jnp.int32)
    return live_pattern(key, SUB_PEERS, devices % SUB_PEERS)


def set_ends(array, rng, low, largest):
    longest = array.shape.index(max(array.shape))
    spots = []
    for shift in (0, 1):
        where = [jax.random.randint(jax.random.fold_in(rng, axis), (), 0, length) for axis, length in enumerate(array.shape)]
        where[longest] = (where[longest] + shift) % array.shape[longest]
        spots.append(tuple(where))
    return array.at[spots[0]].set(low).at[spots[1]].set(largest)


def steps_of(stream_key, dims, pieces, least, high):
    factor_of = 1.0
    for dim, blocks in pieces:
        steps = jax.random.uniform(jax.random.fold_in(jax.random.fold_in(stream_key, 6), dim), (blocks,), jnp.float32, least / len(pieces), high / len(pieces))
        factor_of = factor_of * jnp.repeat(jnp.exp(steps), dims[dim] // blocks).reshape((-1,) + (1,) * (len(dims) - 1 - dim))
    return factor_of


def gaussian(rng, dims, width, most, shards=(), kind=jnp.bfloat16):
    loudness = steps_of(rng, dims, shards, -0.22, 0.18) if shards else 1.0
    values = jax.random.normal(rng, dims, jnp.float32) * width * loudness
    return jnp.minimum(jnp.maximum(values, -most), most).astype(kind)


def setup_inputs(seed: int = 0, part: int = 0) -> dict:
    seeds = jax.random.split(jax.random.key(seed), 6)
    part_keys = jax.random.split(jax.random.fold_in(seeds[5], part), 6)
    embeds = gaussian(part_keys[0], (ROWS, D), 1.0, 6.0, ((0, 16),))
    pick_blk = set_ends(jax.random.randint(part_keys[1], (DEVS, BLK_PEERS), 0, BPD), jax.random.fold_in(part_keys[1], 1), 0, BPD - 1).astype(jnp.int32)
    mask_blk = draw_mask_blk(jax.random.fold_in(jax.random.fold_in(seeds[5], part), 71), part)
    pick_sub = set_ends(jax.random.randint(part_keys[3], (DEVS, SUB_PEERS), 0, BPD), jax.random.fold_in(part_keys[3], 1), 0, BPD - 1).astype(jnp.int32)
    mask_sub = draw_mask_sub(jax.random.fold_in(jax.random.fold_in(seeds[5], part), 71), part)
    return {"embeds": embeds, "pick_blk": pick_blk, "mask_blk": mask_blk, "pick_sub": pick_sub, "mask_sub": mask_sub}


cutoff = 0.05
sharpness = 100.0

def reference(embeds, pick_blk, mask_blk, pick_sub, mask_sub):
    wide = embeds.astype(jnp.float32)
    unit_rows = (wide * lax.rsqrt(lax.optimization_barrier(jnp.sum(wide * wide, axis=1, keepdims=True)) + 1e-06)).astype(jnp.bfloat16)
    blocks = unit_rows.reshape(DEVS, BPD, BLOCK, D)
    devices = jnp.arange(DEVS, dtype=jnp.int32)
    blk_index = devices // SUB_PEERS
    sub_index = devices % SUB_PEERS
    blk_slots = jnp.arange(BLK_PEERS, dtype=jnp.int32)
    sub_slots = jnp.arange(SUB_PEERS, dtype=jnp.int32)
    senders_blk = blk_slots[None, :] * SUB_PEERS + sub_index[:, None]
    picks_blk = pick_blk[senders_blk, blk_index[:, None]]
    senders_sub = blk_index[:, None] * SUB_PEERS + sub_slots[None, :]
    picks_sub = pick_sub[senders_sub, sub_index[:, None]]
    senders = jnp.concatenate([senders_blk, senders_sub], axis=1).reshape(-1).astype(jnp.int32)
    picked = jnp.concatenate([picks_blk, picks_sub], axis=1).reshape(-1).astype(jnp.int32)
    alive = jnp.concatenate([mask_blk.reshape(DEVS, BLK_PEERS, BPD), mask_sub.reshape(DEVS, SUB_PEERS, BPD)], axis=1).reshape(-1, BPD)
    slot_count = BLK_PEERS + SUB_PEERS

    def visit(slot_index, totals):
        receiver = slot_index // slot_count
        sender = senders[slot_index]
        chosen = picked[slot_index]
        arrived = blocks[sender, chosen]
        locals_flat = blocks[receiver].reshape(BPD * BLOCK, D)
        cosines = jnp.dot(arrived, locals_flat.T, preferred_element_type=jnp.float32)
        weight = jax.nn.sigmoid((cosines - cutoff) * sharpness).reshape(BLOCK, BPD, BLOCK)
        weight = weight * alive[slot_index].astype(jnp.float32)[None, :, None]
        totals = totals.at[receiver].add(lax.optimization_barrier(jnp.sum(weight, axis=0)))
        totals = totals.at[sender, chosen].add(lax.optimization_barrier(jnp.sum(weight, axis=(1, 2))))
        return totals
    totals = lax.fori_loop(0, DEVS * slot_count, visit, jnp.zeros((DEVS, BPD, BLOCK), jnp.float32))
    return (totals / BLOCK).reshape(-1)
```

```python
import jax
import jax.numpy as jnp
from jax import lax
from jax.sharding import PartitionSpec as P

BLOCK = 256

cutoff = 0.05
sharpness = 100.0


def normalize(embeds):
    wide = embeds.astype(jnp.float32)
    scale = lax.rsqrt(jnp.sum(wide * wide, axis=1, keepdims=True) + 1e-06)
    return (wide * scale).astype(jnp.bfloat16)


def partner(index, step, size):
    if size & (size - 1) == 0:
        return index ^ step, index ^ step
    return (index + step) % size, (index - step) % size


def pairs(step, size):
    return [(i, partner(i, step, size)[0]) for i in range(size)]


def sweep(arrived, unit_rows, live_mask):
    count = live_mask.shape[0]
    rows = arrived.shape[0]
    cosines = lax.dot_general(
        normalize(arrived), unit_rows, (((1,), (1,)), ((), ())), preferred_element_type=jnp.float32
    )
    weight = jax.nn.sigmoid((cosines - cutoff) * sharpness).reshape(rows, count, -1)
    weight = weight * live_mask.astype(jnp.float32)[None, :, None]
    return jnp.sum(weight, axis=0), jnp.sum(weight, axis=(1, 2))


def body(embeds, pick_blk, mask_blk, pick_sub, mask_sub):
    features = embeds.shape[1]
    blocks = embeds.reshape(-1, BLOCK, features)
    count = blocks.shape[0]
    sub_size, blk_size = lax.axis_size("sub"), lax.axis_size("blk")
    own_sub, own_blk = lax.axis_index("sub"), lax.axis_index("blk")
    picks = {"sub": lax.dynamic_index_in_dim(pick_sub, own_sub, 0, keepdims=False), "blk": pick_blk[0]}
    masks = {"sub": mask_sub[0].reshape(-1, count), "blk": mask_blk[0].reshape(-1, count)}
    own = {"sub": own_sub, "blk": own_blk}
    size = {"sub": sub_size, "blk": blk_size}

    slots = []
    rounds = [("sub", k) for k in range(sub_size - 1, 0, -1)] + [("blk", k) for k in range(blk_size - 1, 0, -1)]
    for axis, step in rounds:
        target, source = partner(own[axis], step, size[axis])
        pick = lax.dynamic_index_in_dim(picks[axis], target, 0, keepdims=False)
        outgoing = lax.dynamic_index_in_dim(blocks, pick, 0, keepdims=False)
        arrived = lax.ppermute(outgoing, axis, pairs(step, size[axis]))
        mask = lax.dynamic_index_in_dim(masks[axis], source, 0, keepdims=False)
        slots.append((axis, step, pick, arrived, mask))

    unit_rows = normalize(embeds)
    totals = jnp.zeros((count, BLOCK), jnp.float32)
    for axis, step, pick, arrived, mask in reversed(slots):
        local, back = sweep(arrived, unit_rows, mask)
        back_pairs = [(b, a) for a, b in pairs(step, size[axis])]
        returned = lax.ppermute(back, axis, back_pairs)
        mine = (jnp.arange(count, dtype=jnp.int32) == pick)[:, None]
        totals = totals + local + jnp.where(mine, returned[None, :], 0.0)
    return totals.reshape(-1) / BLOCK


def solution(mesh):
    return jax.shard_map(
        body,
        mesh=mesh,
        in_specs=(
            P(("groups", "blk", "sub"), None),
            P(("groups", "blk", "sub"), None),
            P(("groups", "blk", "sub"), None),
            P(("groups", "blk"), None),
            P(("groups", "blk", "sub"), None),
        ),
        out_specs=P(("groups", "blk", "sub")),
        check_vma=False,
    )
```

```python
import functools

import jax
import jax.numpy as jnp
from jax import lax
from jax.experimental import pallas as pl
from jax.experimental.pallas import tpu as pltpu
from jax.sharding import PartitionSpec as P

BLOCK = 256

cutoff = 0.05
sharpness = 100.0


def partner(index, step, size):
    if size & (size - 1) == 0:
        return index ^ step, index ^ step
    return lax.rem(index + step, size), lax.rem(index + size - step, size)


def pairs(step, size):
    if size & (size - 1) == 0:
        return [(i, i ^ step) for i in range(size)]
    return [(i, (i + step) % size) for i in range(size)]


def rounded_units(rows):
    wide = rows.astype(jnp.float32)
    scale = lax.rsqrt(jnp.sum(wide * wide, axis=1, keepdims=True) + 1e-06)
    return (wide * scale).astype(jnp.bfloat16)


def take_pick(rounds, sizes, pick_blk, pick_sub, place):
    axis, step = rounds[place]
    target, _ = partner(lax.axis_index(axis), step, sizes[axis])
    return pick_blk[0, target] if axis == "blk" else pick_sub[lax.axis_index("sub"), target]


def pick_kernel(rounds, sizes, pick_blk, pick_sub, embeds, *rest):
    outs, sems = rest[:-1], rest[-1]
    copies = []
    for place, out in enumerate(outs):
        pick = take_pick(rounds, sizes, pick_blk, pick_sub, place)
        rows = pl.ds(pl.multiple_of(pick * BLOCK, BLOCK), BLOCK)
        copies.append(pltpu.make_async_copy(embeds.at[rows], out, sems.at[place]))
    for copy in copies:
        copy.start()
    for copy in copies:
        copy.wait()


def pick_blocks(rounds, sizes, pick_blk, pick_sub, embeds):
    smem, any_space = pl.BlockSpec(memory_space=pltpu.SMEM), pl.BlockSpec(memory_space=pl.ANY)
    shape = jax.ShapeDtypeStruct((BLOCK, embeds.shape[1]), embeds.dtype)
    return pl.pallas_call(
        functools.partial(pick_kernel, rounds, sizes),
        out_shape=[shape] * len(rounds),
        in_specs=[smem, smem, any_space],
        out_specs=[any_space] * len(rounds),
        scratch_shapes=[pltpu.SemaphoreType.DMA((len(rounds),))],
    )(pick_blk, pick_sub, embeds)


def unit_kernel(embeds, units):
    for start in range(0, embeds.shape[0], BLOCK):
        units[start : start + BLOCK] = rounded_units(embeds[start : start + BLOCK])


def unit_rows(embeds):
    vmem = pl.BlockSpec(memory_space=pltpu.VMEM)
    return pl.pallas_call(
        unit_kernel,
        out_shape=jax.ShapeDtypeStruct(embeds.shape, embeds.dtype),
        in_specs=[vmem],
        out_specs=vmem,
        compiler_params=pltpu.CompilerParams(vmem_limit_bytes=32 * 2**20),
    )(embeds)


def add_returned(totals, pick, sums):
    totals[pl.ds(pick, 1)] = totals[pl.ds(pick, 1)] + sums[...]


def slot_kernel(rounds, sizes, place, back_place, mask, pick_blk, pick_sub, arrived, units, totals, *rest):
    axis, step = rounds[place]
    _, source = partner(lax.axis_index(axis), step, sizes[axis])
    count = units.shape[0] // BLOCK
    new_totals, back = rest[-2:]
    x = rounded_units(arrived[...])
    along_rows = jnp.zeros((BLOCK, 128), jnp.float32)
    for i in range(count):
        y = units[i * BLOCK : (i + 1) * BLOCK]
        cosines = lax.dot_general(x, y, (((1,), (1,)), ((), ())), preferred_element_type=jnp.float32)
        weights = jax.nn.sigmoid((cosines - cutoff) * sharpness)
        live = mask[0, source * count + i].astype(jnp.float32)
        new_totals[i : i + 1] = totals[i : i + 1] + live * jnp.sum(weights, axis=0, keepdims=True)
        for lane in range(0, BLOCK, 128):
            along_rows = along_rows + live * weights[:, lane : lane + 128]
    back[...] = jnp.sum(along_rows.T, axis=0, keepdims=True)
    if back_place is not None:
        add_returned(new_totals, take_pick(rounds, sizes, pick_blk, pick_sub, back_place), rest[0])


def slot(rounds, sizes, place, masks, pick_blk, pick_sub, arrived, units, totals, back_place, returned):
    smem, vmem = pl.BlockSpec(memory_space=pltpu.SMEM), pl.BlockSpec(memory_space=pltpu.VMEM)
    operands = [masks[rounds[place][0]], pick_blk, pick_sub, arrived, units, totals]
    if back_place is not None:
        operands.append(returned)
    return pl.pallas_call(
        functools.partial(slot_kernel, rounds, sizes, place, back_place),
        out_shape=[
            jax.ShapeDtypeStruct(totals.shape, jnp.float32),
            jax.ShapeDtypeStruct((1, BLOCK), jnp.float32),
        ],
        in_specs=[smem] * 3 + [vmem] * (len(operands) - 3),
        out_specs=[vmem, vmem],
        compiler_params=pltpu.CompilerParams(vmem_limit_bytes=32 * 2**20),
    )(*operands)


def credit_kernel(rounds, sizes, places, pick_blk, pick_sub, totals, *rest):
    returned, out = rest[:-1], rest[-1]
    out[...] = totals[...]
    for place, sums in zip(places, returned):
        add_returned(out, take_pick(rounds, sizes, pick_blk, pick_sub, place), sums)
    out[...] = out[...] / BLOCK


def credit(rounds, sizes, places, pick_blk, pick_sub, totals, returned):
    smem, vmem = pl.BlockSpec(memory_space=pltpu.SMEM), pl.BlockSpec(memory_space=pltpu.VMEM)
    return pl.pallas_call(
        functools.partial(credit_kernel, rounds, sizes, places),
        out_shape=jax.ShapeDtypeStruct(totals.shape, jnp.float32),
        in_specs=[smem, smem, vmem] + [vmem] * len(returned),
        out_specs=vmem,
    )(pick_blk, pick_sub, totals, *returned)


def interleave(sub_size, blk_size):
    sub = [("sub", k) for k in ([2, 3, 1] if sub_size == 4 else range(1, sub_size))]
    blk = [("blk", k) for k in range(2, blk_size)]
    order = [("blk", 1)]
    for place in range(max(len(sub), len(blk))):
        order += sub[place : place + 1] + blk[place : place + 1]
    return order


BEHIND = 2


def body(embeds, pick_blk, mask_blk, pick_sub, mask_sub):
    count = embeds.shape[0] // BLOCK
    sizes = {"sub": lax.axis_size("sub"), "blk": lax.axis_size("blk")}
    masks = {"sub": mask_sub, "blk": mask_blk}
    rounds = interleave(sizes["sub"], sizes["blk"])

    outgoing = pick_blocks(rounds, sizes, pick_blk, pick_sub, embeds)
    arrived = [lax.ppermute(sent, axis, pairs(step, sizes[axis])) for (axis, step), sent in zip(rounds, outgoing)]

    units = unit_rows(embeds)
    totals = jnp.zeros((count, BLOCK), jnp.float32)
    returned = []
    for place, (axis, step) in enumerate(rounds):
        back_place = place - BEHIND if place >= BEHIND else None
        came_back = None if back_place is None else returned[back_place]
        totals, back = slot(
            rounds, sizes, place, masks, pick_blk, pick_sub, arrived[place], units, totals, back_place, came_back
        )
        returned.append(lax.ppermute(back, axis, [(b, a) for a, b in pairs(step, sizes[axis])]))
    last = list(range(len(rounds) - BEHIND, len(rounds)))
    out = credit(rounds, sizes, last, pick_blk, pick_sub, totals, [returned[place] for place in last])
    return out.reshape(-1)


def solution(mesh):
    return jax.shard_map(
        body,
        mesh=mesh,
        in_specs=(
            P(("groups", "blk", "sub"), None),
            P(("groups", "blk", "sub"), None),
            P(("groups", "blk", "sub"), None),
            P(("groups", "blk"), None),
            P(("groups", "blk", "sub"), None),
        ),
        out_specs=P(("groups", "blk", "sub")),
        check_vma=False,
    )
```

```python
import functools

import jax
import jax.numpy as jnp
from jax import lax
from jax.experimental import pallas as pl
from jax.experimental.pallas import tpu as pltpu
from jax.sharding import PartitionSpec as P

BLOCK = 256

cutoff = 0.05
sharpness = 100.0


def partner(index, step, size):
    if size & (size - 1) == 0:
        return index ^ step, index ^ step
    return lax.rem(index + step, size), lax.rem(index + size - step, size)


def pairs(step, size):
    if size & (size - 1) == 0:
        return [(i, i ^ step) for i in range(size)]
    return [(i, (i + step) % size) for i in range(size)]


def rounded_units(rows):
    wide = rows.astype(jnp.float32)
    scale = lax.rsqrt(jnp.sum(wide * wide, axis=1, keepdims=True) + 1e-06)
    return (wide * scale).astype(jnp.bfloat16)


def take_pick(rounds, sizes, pick_blk, pick_sub, place):
    axis, step = rounds[place]
    target, _ = partner(lax.axis_index(axis), step, sizes[axis])
    return pick_blk[0, target] if axis == "blk" else pick_sub[lax.axis_index("sub"), target]


def pick_kernel(rounds, sizes, pick_blk, pick_sub, embeds, *outs):
    for place, out in enumerate(outs):
        pick = take_pick(rounds, sizes, pick_blk, pick_sub, place)
        out[...] = embeds[pl.ds(pl.multiple_of(pick * BLOCK, BLOCK), BLOCK)]


def pick_blocks(rounds, sizes, pick_blk, pick_sub, embeds):
    smem, vmem = pl.BlockSpec(memory_space=pltpu.SMEM), pl.BlockSpec(memory_space=pltpu.VMEM)
    shape = jax.ShapeDtypeStruct((BLOCK, embeds.shape[1]), embeds.dtype)
    return pl.pallas_call(
        functools.partial(pick_kernel, rounds, sizes),
        out_shape=[shape] * len(rounds),
        in_specs=[smem, smem, vmem],
        out_specs=[vmem] * len(rounds),
        compiler_params=pltpu.CompilerParams(vmem_limit_bytes=32 * 2**20),
    )(pick_blk, pick_sub, embeds)


def unit_kernel(embeds, units):
    for start in range(0, embeds.shape[0], BLOCK):
        units[start : start + BLOCK] = rounded_units(embeds[start : start + BLOCK])


def unit_rows(embeds):
    vmem = pl.BlockSpec(memory_space=pltpu.VMEM)
    return pl.pallas_call(
        unit_kernel,
        out_shape=jax.ShapeDtypeStruct(embeds.shape, embeds.dtype),
        in_specs=[vmem],
        out_specs=vmem,
        compiler_params=pltpu.CompilerParams(vmem_limit_bytes=32 * 2**20),
    )(embeds)


def add_returned(totals, pick, sums):
    totals[pl.ds(pick, 1)] = totals[pl.ds(pick, 1)] + sums[...]


def slot_kernel(rounds, sizes, place, back_place, mask, pick_blk, pick_sub, arrived, units, totals, *rest):
    axis, step = rounds[place]
    _, source = partner(lax.axis_index(axis), step, sizes[axis])
    count = units.shape[0] // BLOCK
    new_totals, back = rest[-2:]
    x = rounded_units(arrived[...])
    along_rows = jnp.zeros((BLOCK, 128), jnp.float32)
    for i in range(count):
        y = units[i * BLOCK : (i + 1) * BLOCK]
        cosines = lax.dot_general(x, y, (((1,), (1,)), ((), ())), preferred_element_type=jnp.float32)
        weights = jax.nn.sigmoid((cosines - cutoff) * sharpness)
        live = mask[0, source * count + i].astype(jnp.float32)
        new_totals[i : i + 1] = totals[i : i + 1] + live * jnp.sum(weights, axis=0, keepdims=True)
        for lane in range(0, BLOCK, 128):
            along_rows = along_rows + live * weights[:, lane : lane + 128]
    back[...] = jnp.sum(along_rows.T, axis=0, keepdims=True)
    if back_place is not None:
        add_returned(new_totals, take_pick(rounds, sizes, pick_blk, pick_sub, back_place), rest[0])


def slot(rounds, sizes, place, masks, pick_blk, pick_sub, arrived, units, totals, back_place, returned):
    smem, vmem = pl.BlockSpec(memory_space=pltpu.SMEM), pl.BlockSpec(memory_space=pltpu.VMEM)
    operands = [masks[rounds[place][0]], pick_blk, pick_sub, arrived, units, totals]
    if back_place is not None:
        operands.append(returned)
    return pl.pallas_call(
        functools.partial(slot_kernel, rounds, sizes, place, back_place),
        out_shape=[
            jax.ShapeDtypeStruct(totals.shape, jnp.float32),
            jax.ShapeDtypeStruct((1, BLOCK), jnp.float32),
        ],
        in_specs=[smem] * 3 + [vmem] * (len(operands) - 3),
        out_specs=[vmem, vmem],
        compiler_params=pltpu.CompilerParams(vmem_limit_bytes=32 * 2**20),
    )(*operands)


def credit_kernel(rounds, sizes, places, pick_blk, pick_sub, totals, *rest):
    returned, out, sum_all = rest[:-2], rest[-2], rest[-1]
    sum_all[...] = totals[...]
    for place, sums in zip(places, returned):
        add_returned(sum_all, take_pick(rounds, sizes, pick_blk, pick_sub, place), sums)
    for i in range(totals.shape[0]):
        for lane in range(0, BLOCK, 128):
            row = (i * BLOCK + lane) // 128
            out[row : row + 1] = sum_all[i : i + 1, lane : lane + 128] / BLOCK


def credit(rounds, sizes, places, pick_blk, pick_sub, totals, returned):
    smem, vmem = pl.BlockSpec(memory_space=pltpu.SMEM), pl.BlockSpec(memory_space=pltpu.VMEM)
    return pl.pallas_call(
        functools.partial(credit_kernel, rounds, sizes, places),
        out_shape=jax.ShapeDtypeStruct((totals.size // 128, 128), jnp.float32),
        in_specs=[smem, smem, vmem] + [vmem] * len(returned),
        out_specs=vmem,
        scratch_shapes=[pltpu.VMEM(totals.shape, jnp.float32)],
    )(pick_blk, pick_sub, totals, *returned)


def interleave(sub_size, blk_size):
    sub = [("sub", k) for k in ([2, 3, 1] if sub_size == 4 else range(1, sub_size))]
    blk = [("blk", k) for k in range(2, blk_size)]
    order = [("blk", 1)]
    for place in range(max(len(sub), len(blk))):
        order += sub[place : place + 1] + blk[place : place + 1]
    return order


BEHIND = 2


def body(embeds, pick_blk, mask_blk, pick_sub, mask_sub):
    count = embeds.shape[0] // BLOCK
    sizes = {"sub": lax.axis_size("sub"), "blk": lax.axis_size("blk")}
    masks = {"sub": mask_sub, "blk": mask_blk}
    rounds = interleave(sizes["sub"], sizes["blk"])

    outgoing = pick_blocks(rounds, sizes, pick_blk, pick_sub, embeds)
    arrived = [lax.ppermute(sent, axis, pairs(step, sizes[axis])) for (axis, step), sent in zip(rounds, outgoing)]

    units = unit_rows(embeds)
    totals = jnp.zeros((count, BLOCK), jnp.float32)
    returned = []
    for place, (axis, step) in enumerate(rounds):
        back_place = place - BEHIND if place >= BEHIND else None
        came_back = None if back_place is None else returned[back_place]
        totals, back = slot(
            rounds, sizes, place, masks, pick_blk, pick_sub, arrived[place], units, totals, back_place, came_back
        )
        returned.append(lax.ppermute(back, axis, [(b, a) for a, b in pairs(step, sizes[axis])]))
    last = list(range(len(rounds) - BEHIND, len(rounds)))
    out = credit(rounds, sizes, last, pick_blk, pick_sub, totals, [returned[place] for place in last])
    return out.reshape(-1)


def solution(mesh):
    return jax.shard_map(
        body,
        mesh=mesh,
        in_specs=(
            P(("groups", "blk", "sub"), None),
            P(("groups", "blk", "sub"), None),
            P(("groups", "blk", "sub"), None),
            P(("groups", "blk"), None),
            P(("groups", "blk", "sub"), None),
        ),
        out_specs=P(("groups", "blk", "sub")),
        check_vma=False,
    )
```

```python
import functools
import math

import jax
import jax.numpy as jnp
from jax import lax
from jax.experimental import pallas as pl
from jax.experimental.pallas import tpu as pltpu
from jax.sharding import PartitionSpec as P

BLOCK = 256
LANES = 128
ROWS = BLOCK // LANES

cutoff = 0.05
sharpness = 100.0

SMEM = pl.BlockSpec(memory_space=pltpu.SMEM)
VMEM = pl.BlockSpec(memory_space=pltpu.VMEM)
HBM = pl.BlockSpec(memory_space=pltpu.HBM)
PARAMS = pltpu.CompilerParams(vmem_limit_bytes=32 * 2**20)


def pairs(step, size):
    return [(i, i ^ step) for i in range(size)]


def rounded_units(rows):
    wide = rows.astype(jnp.float32)
    scale = lax.rsqrt(jnp.sum(wide * wide, axis=1, keepdims=True) + 1e-06)
    return (wide * scale).astype(jnp.bfloat16)


def soft_weights(cosines):
    rate = sharpness * math.log2(math.e)
    below = 1.0 + jnp.exp2(jnp.minimum(cutoff * rate - cosines * rate, 125.0))
    guess = pl.reciprocal(below, approx=True)
    return guess * (2.0 - below * guess)


def take_pick(axis, step, pick_blk, pick_sub):
    target = lax.axis_index(axis) ^ step
    return pick_blk[0, target] if axis == "blk" else pick_sub[lax.axis_index("sub"), target]


def pick_kernel(pieces, pick_blk, pick_sub, embeds, *rest):
    outs, (blk_scalars, sub_scalars, scalar_sems, block_sems) = rest[: len(pieces)], rest[-4:]
    scalars = [
        pltpu.make_async_copy(pick_blk, blk_scalars, scalar_sems.at[0]),
        pltpu.make_async_copy(pick_sub, sub_scalars, scalar_sems.at[1]),
    ]
    for copy in scalars:
        copy.start()
    for copy in scalars:
        copy.wait()
    copies = []
    for place, (out, (axis, step, first, rows)) in enumerate(zip(outs, pieces)):
        pick = take_pick(axis, step, blk_scalars, sub_scalars)
        start = pl.multiple_of(pick * BLOCK + first, math.gcd(BLOCK, first))
        copies.append(pltpu.make_async_copy(embeds.at[pl.ds(start, rows)], out, block_sems.at[place]))
    for copy in copies:
        copy.start()
    for copy in copies:
        copy.wait()


def pick_rows(pieces, pick_blk, pick_sub, embeds):
    return pl.pallas_call(
        functools.partial(pick_kernel, pieces),
        out_shape=[jax.ShapeDtypeStruct((rows, embeds.shape[1]), embeds.dtype) for _, _, _, rows in pieces],
        in_specs=[HBM] * 3,
        out_specs=[VMEM] * len(pieces),
        scratch_shapes=[
            pltpu.SMEM(pick_blk.shape, jnp.int32),
            pltpu.SMEM(pick_sub.shape, jnp.int32),
            pltpu.SemaphoreType.DMA((2,)),
            pltpu.SemaphoreType.DMA((len(pieces),)),
        ],
        compiler_params=PARAMS,
    )(pick_blk, pick_sub, embeds)


def prepare_kernel(slots, pick_blk, pick_sub, mask_blk, mask_sub, embeds, units, live, mine):
    for start in range(0, embeds.shape[0], BLOCK):
        units[start : start + BLOCK] = rounded_units(embeds[start : start + BLOCK])
    count = live.shape[1]
    block_of = lax.broadcasted_iota(jnp.int32, mine.shape[1:], 0) // ROWS
    for place, (axis, step, _, _) in enumerate(slots):
        source = lax.axis_index(axis) ^ step
        mask = mask_blk if axis == "blk" else mask_sub
        for i in range(count):
            value = mask[0, source * count + i].astype(jnp.float32)
            live[place, i : i + 1] = jnp.full((1, LANES), value, jnp.float32)
        pick = take_pick(axis, step, pick_blk, pick_sub)
        mine[place] = (block_of == pick).astype(jnp.float32)


def prepare(slots, pick_blk, pick_sub, mask_blk, mask_sub, embeds):
    count = embeds.shape[0] // BLOCK
    return pl.pallas_call(
        functools.partial(prepare_kernel, slots),
        out_shape=[
            jax.ShapeDtypeStruct(embeds.shape, embeds.dtype),
            jax.ShapeDtypeStruct((len(slots), count, LANES), jnp.float32),
            jax.ShapeDtypeStruct((len(slots), count * ROWS, LANES), jnp.float32),
        ],
        in_specs=[SMEM] * 4 + [VMEM],
        out_specs=[VMEM] * 3,
        compiler_params=PARAMS,
    )(pick_blk, pick_sub, mask_blk, mask_sub, embeds)


def slot_kernel(place, first, rows, back_place, arrived, units, live, mine, totals, *rest):
    new_totals, back = rest[-2:]
    count = live.shape[1]
    before = totals[...]
    if back_place is not None:
        before = before + mine[back_place] * rest[0][...]
    new_totals[...] = before
    x = rounded_units(arrived[...])
    along_rows = jnp.zeros((rows, LANES), jnp.float32)
    for i in range(count):
        y = units[i * BLOCK : (i + 1) * BLOCK]
        cosines = lax.dot_general(x, y, (((1,), (1,)), ((), ())), preferred_element_type=jnp.float32)
        weights = soft_weights(cosines)
        alive = live[place, i : i + 1]
        for part in range(ROWS):
            piece = alive * weights[:, part * LANES : (part + 1) * LANES]
            along_rows = along_rows + piece
            row = i * ROWS + part
            new_totals[row : row + 1] = new_totals[row : row + 1] + jnp.sum(piece, axis=0, keepdims=True)
    empty = [jnp.zeros((gap, LANES), jnp.float32) for gap in (first, BLOCK - first - rows)]
    along_rows = jnp.concatenate([part for part in (empty[0], along_rows, empty[1]) if part.shape[0]], axis=0)
    for part in range(ROWS):
        sums = jnp.sum(along_rows[part * LANES : (part + 1) * LANES].T, axis=0, keepdims=True)
        for i in range(count):
            row = i * ROWS + part
            back[row : row + 1] = sums


def work(place, slot, arrived, units, live, mine, totals, back_place, returned):
    operands = [arrived, units, live, mine, totals] + ([] if back_place is None else [returned])
    return pl.pallas_call(
        functools.partial(slot_kernel, place, *slot[2:], back_place),
        out_shape=[jax.ShapeDtypeStruct(totals.shape, jnp.float32)] * 2,
        in_specs=[VMEM] * len(operands),
        out_specs=[VMEM] * 2,
        compiler_params=PARAMS,
    )(*operands)


BEHIND = 2
EARLY_ROWS = 128


def plan_slots(sizes):
    slots = [("blk", 1, 0, BLOCK), ("blk", 2, 0, BLOCK), ("sub", 2, 0, EARLY_ROWS)]
    slots += [("blk", k, 0, BLOCK) for k in range(3, sizes["blk"])]
    slots += [("sub", 1, 0, BLOCK), ("sub", 2, EARLY_ROWS, BLOCK - EARLY_ROWS)]
    return slots + [("sub", k, 0, BLOCK) for k in range(3, sizes["sub"])]


AT_ONCE = 3


def body(embeds, pick_blk, mask_blk, pick_sub, mask_sub):
    count = embeds.shape[0] // BLOCK
    sizes = {"sub": lax.axis_size("sub"), "blk": lax.axis_size("blk")}
    slots = plan_slots(sizes)

    def send(array, slot):
        return lax.ppermute(array, slot[0], pairs(slot[1], sizes[slot[0]]))

    arrived = []
    for group in (slots[:AT_ONCE], slots[AT_ONCE:]):
        for rows, slot in zip(pick_rows(group, pick_blk, pick_sub, embeds), group):
            arrived.append(send(rows, slot))

    units, live, mine = prepare(slots, pick_blk, pick_sub, mask_blk, mask_sub, embeds)
    totals = jnp.zeros((count * ROWS, LANES), jnp.float32)
    returned = []
    for place, slot in enumerate(slots):
        back_place = place - BEHIND if place >= BEHIND else None
        came_back = None if back_place is None else returned[back_place]
        totals, back = work(place, slot, arrived[place], units, live, mine, totals, back_place, came_back)
        returned.append(send(back, slot))
    for place in range(len(slots) - BEHIND, len(slots)):
        totals = totals + mine[place] * returned[place]
    return (totals * (1.0 / BLOCK)).reshape(-1)


def solution(mesh):
    return jax.shard_map(
        body,
        mesh=mesh,
        in_specs=(
            P(("groups", "blk", "sub"), None),
            P(("groups", "blk", "sub"), None),
            P(("groups", "blk", "sub"), None),
            P(("groups", "blk"), None),
            P(("groups", "blk", "sub"), None),
        ),
        out_specs=P(("groups", "blk", "sub")),
        check_vma=False,
    )
```

```python
import functools
import math

import jax
import jax.numpy as jnp
from jax import lax
from jax.experimental import pallas as pl
from jax.experimental.pallas import tpu as pltpu
from jax.sharding import PartitionSpec as P

BLOCK = 256
LANES = 128
ROWS = BLOCK // LANES

cutoff = 0.05
sharpness = 100.0

SMEM = pl.BlockSpec(memory_space=pltpu.SMEM)
VMEM = pl.BlockSpec(memory_space=pltpu.VMEM)
HBM = pl.BlockSpec(memory_space=pltpu.HBM)
PARAMS = pltpu.CompilerParams(vmem_limit_bytes=32 * 2**20)


def pairs(step, size):
    return [(i, i ^ step) for i in range(size)]


def rounded_units(rows):
    wide = rows.astype(jnp.float32)
    scale = lax.rsqrt(jnp.sum(wide * wide, axis=1, keepdims=True) + 1e-06)
    return (wide * scale).astype(jnp.bfloat16)


def soft_weights(cosines):
    rate = sharpness * math.log2(math.e)
    below = 1.0 + jnp.exp2(jnp.minimum(cutoff * rate - cosines * rate, 125.0))
    guess = pl.reciprocal(below, approx=True)
    return guess * (2.0 - below * guess)


def take_pick(axis, step, pick_blk, pick_sub):
    target = lax.axis_index(axis) ^ step
    return pick_blk[0, target] if axis == "blk" else pick_sub[lax.axis_index("sub"), target]


def pick_kernel(pieces, pick_blk, pick_sub, embeds, *rest):
    outs, (blk_scalars, sub_scalars, scalar_sems, block_sems) = rest[: len(pieces)], rest[-4:]
    scalars = [
        pltpu.make_async_copy(pick_blk, blk_scalars, scalar_sems.at[0]),
        pltpu.make_async_copy(pick_sub, sub_scalars, scalar_sems.at[1]),
    ]
    for copy in scalars:
        copy.start()
    for copy in scalars:
        copy.wait()
    copies = []
    for place, (out, (axis, step, first, rows)) in enumerate(zip(outs, pieces)):
        pick = take_pick(axis, step, blk_scalars, sub_scalars)
        start = pl.multiple_of(pick * BLOCK + first, math.gcd(BLOCK, first))
        copies.append(pltpu.make_async_copy(embeds.at[pl.ds(start, rows)], out, block_sems.at[place]))
    for copy in copies:
        copy.start()
    for copy in copies:
        copy.wait()


def pick_rows(pieces, pick_blk, pick_sub, embeds):
    return pl.pallas_call(
        functools.partial(pick_kernel, pieces),
        out_shape=[jax.ShapeDtypeStruct((rows, embeds.shape[1]), embeds.dtype) for _, _, _, rows in pieces],
        in_specs=[HBM] * 3,
        out_specs=[VMEM] * len(pieces),
        scratch_shapes=[
            pltpu.SMEM(pick_blk.shape, jnp.int32),
            pltpu.SMEM(pick_sub.shape, jnp.int32),
            pltpu.SemaphoreType.DMA((2,)),
            pltpu.SemaphoreType.DMA((len(pieces),)),
        ],
        compiler_params=PARAMS,
    )(pick_blk, pick_sub, embeds)


def prepare_kernel(slots, pick_blk, pick_sub, mask_blk, mask_sub, embeds, units, live, mine):
    for start in range(0, embeds.shape[0], BLOCK):
        units[start : start + BLOCK] = rounded_units(embeds[start : start + BLOCK])
    count = live.shape[1]
    block_of = lax.broadcasted_iota(jnp.int32, mine.shape[1:], 0) // ROWS
    for place, (axis, step, _, _) in enumerate(slots):
        source = lax.axis_index(axis) ^ step
        mask = mask_blk if axis == "blk" else mask_sub
        for i in range(count):
            value = mask[0, source * count + i].astype(jnp.float32)
            live[place, i : i + 1] = jnp.full((1, LANES), value, jnp.float32)
        pick = take_pick(axis, step, pick_blk, pick_sub)
        mine[place] = (block_of == pick).astype(jnp.float32)


def prepare(slots, pick_blk, pick_sub, mask_blk, mask_sub, embeds):
    count = embeds.shape[0] // BLOCK
    return pl.pallas_call(
        functools.partial(prepare_kernel, slots),
        out_shape=[
            jax.ShapeDtypeStruct(embeds.shape, embeds.dtype),
            jax.ShapeDtypeStruct((len(slots), count, LANES), jnp.float32),
            jax.ShapeDtypeStruct((len(slots), count * ROWS, LANES), jnp.float32),
        ],
        in_specs=[SMEM] * 4 + [VMEM],
        out_specs=[VMEM] * 3,
        compiler_params=PARAMS,
    )(pick_blk, pick_sub, mask_blk, mask_sub, embeds)


def slot_kernel(place, first, rows, back_place, carries, arrived, units, live, mine, totals, *rest):
    new_totals, back = rest[-2:]
    count = live.shape[1]
    before = totals[...]
    if back_place is not None:
        before = before + mine[back_place] * rest[0][...]
    new_totals[...] = before
    x = rounded_units(arrived[...])
    along_rows = jnp.zeros((rows, LANES), jnp.float32)
    for i in range(count):
        y = units[i * BLOCK : (i + 1) * BLOCK]
        cosines = lax.dot_general(x, y, (((1,), (1,)), ((), ())), preferred_element_type=jnp.float32)
        weights = soft_weights(cosines)
        alive = live[place, i : i + 1]
        for part in range(ROWS):
            piece = alive * weights[:, part * LANES : (part + 1) * LANES]
            along_rows = along_rows + piece
            row = i * ROWS + part
            new_totals[row : row + 1] = new_totals[row : row + 1] + jnp.sum(piece, axis=0, keepdims=True)
    empty = [jnp.zeros((gap, LANES), jnp.float32) for gap in (first, BLOCK - first - rows)]
    along_rows = jnp.concatenate([part for part in (empty[0], along_rows, empty[1]) if part.shape[0]], axis=0)
    for part in range(ROWS):
        sums = jnp.sum(along_rows[part * LANES : (part + 1) * LANES].T, axis=0, keepdims=True)
        for i in range(count):
            row = i * ROWS + part
            back[row : row + 1] = sums + rest[-3][row : row + 1] if carries else sums


def work(place, slot, arrived, units, live, mine, totals, returned, carried):
    back_place, came_back = returned or (None, None)
    operands = [arrived, units, live, mine, totals] + [one for one in (came_back, carried) if one is not None]
    return pl.pallas_call(
        functools.partial(slot_kernel, place, *slot[2:], back_place, carried is not None),
        out_shape=[jax.ShapeDtypeStruct(totals.shape, jnp.float32)] * 2,
        in_specs=[VMEM] * len(operands),
        out_specs=[VMEM] * 2,
        compiler_params=PARAMS,
    )(*operands)


BEHIND = 2
EARLY_ROWS = 128


def plan_slots(sizes):
    slots = [("blk", 1, 0, BLOCK), ("blk", 2, 0, BLOCK), ("sub", 2, 0, EARLY_ROWS)]
    slots += [("blk", k, 0, BLOCK) for k in range(3, sizes["blk"])]
    slots += [("sub", 1, 0, BLOCK), ("sub", 2, EARLY_ROWS, BLOCK - EARLY_ROWS)]
    return slots + [("sub", k, 0, BLOCK) for k in range(3, sizes["sub"])]


AT_ONCE = 3


def body(embeds, pick_blk, mask_blk, pick_sub, mask_sub):
    count = embeds.shape[0] // BLOCK
    sizes = {"sub": lax.axis_size("sub"), "blk": lax.axis_size("blk")}
    slots = plan_slots(sizes)

    def send(array, slot):
        return lax.ppermute(array, slot[0], pairs(slot[1], sizes[slot[0]]))

    arrived = []
    for group in (slots[:AT_ONCE], slots[AT_ONCE:]):
        for rows, slot in zip(pick_rows(group, pick_blk, pick_sub, embeds), group):
            arrived.append(send(rows, slot))

    units, live, mine = prepare(slots, pick_blk, pick_sub, mask_blk, mask_sub, embeds)
    totals = jnp.zeros((count * ROWS, LANES), jnp.float32)
    carried = {}
    soon, late = [], []
    for place, slot in enumerate(slots):
        axis, step, first, rows = slot
        ready = soon.pop(0) if soon and soon[0][0] <= place - BEHIND else None
        totals, back = work(
            place, slot, arrived[place], units, live, mine, totals, ready, carried.pop((axis, step), None)
        )
        if first + rows < BLOCK:
            carried[axis, step] = back
        else:
            (soon if axis == "blk" else late).append((place, send(back, slot)))
    for place, sums in soon + late:
        totals = totals + mine[place] * sums
    return (totals * (1.0 / BLOCK)).reshape(-1)


def solution(mesh):
    return jax.shard_map(
        body,
        mesh=mesh,
        in_specs=(
            P(("groups", "blk", "sub"), None),
            P(("groups", "blk", "sub"), None),
            P(("groups", "blk", "sub"), None),
            P(("groups", "blk"), None),
            P(("groups", "blk", "sub"), None),
        ),
        out_specs=P(("groups", "blk", "sub")),
        check_vma=False,
    )
```

```python
import functools
import math

import jax
import jax.numpy as jnp
from jax import lax
from jax.experimental import pallas as pl
from jax.experimental.pallas import tpu as pltpu
from jax.sharding import PartitionSpec as P

BLOCK = 256
LANES = 128
ROWS = BLOCK // LANES

cutoff = 0.05
sharpness = 100.0

SMEM = pl.BlockSpec(memory_space=pltpu.SMEM)
VMEM = pl.BlockSpec(memory_space=pltpu.VMEM)
HBM = pl.BlockSpec(memory_space=pltpu.HBM)
ANY = pl.BlockSpec(memory_space=pl.ANY)
PARAMS = pltpu.CompilerParams(vmem_limit_bytes=32 * 2**20)


def pairs(step, size):
    return [(i, i ^ step) for i in range(size)]


def rounded_units(rows):
    wide = rows.astype(jnp.float32)
    scale = lax.rsqrt(jnp.sum(wide * wide, axis=1, keepdims=True) + 1e-06)
    return (wide * scale).astype(jnp.bfloat16)


def soft_weights(cosines):
    rate = sharpness * math.log2(math.e)
    below = 1.0 + jnp.exp2(jnp.minimum(cutoff * rate - cosines * rate, 125.0))
    guess = pl.reciprocal(below, approx=True)
    return guess * (2.0 - below * guess)


def take_pick(axis, step, pick_blk, pick_sub):
    target = lax.axis_index(axis) ^ step
    return pick_blk[0, target] if axis == "blk" else pick_sub[lax.axis_index("sub"), target]


def pick_kernel(pieces, pick_blk, pick_sub, embeds, *rest):
    outs, (blk_scalars, sub_scalars, scalar_sems, in_sems, out_sems, *staged) = rest[: len(pieces)], rest[len(pieces) :]
    scalars = [
        pltpu.make_async_copy(pick_blk, blk_scalars, scalar_sems.at[0]),
        pltpu.make_async_copy(pick_sub, sub_scalars, scalar_sems.at[1]),
    ]
    for copy in scalars:
        copy.start()
    for copy in scalars:
        copy.wait()
    copies = []
    for place, (axis, step, first, rows) in enumerate(pieces):
        pick = take_pick(axis, step, blk_scalars, sub_scalars)
        start = pl.multiple_of(pick * BLOCK + first, math.gcd(BLOCK, first))
        target = staged[place] if staged else outs[place]
        copies.append(pltpu.make_async_copy(embeds.at[pl.ds(start, rows)], target, in_sems.at[place]))
        copies[-1].start()
    leaving = []
    for place, copy in enumerate(copies):
        copy.wait()
        if staged:
            leaving.append(pltpu.make_async_copy(staged[place], outs[place], out_sems.at[place]))
            leaving[-1].start()
    for copy in leaving:
        copy.wait()


def pick_rows(pieces, pick_blk, pick_sub, embeds, staged):
    shapes = [(rows, embeds.shape[1]) for _, _, _, rows in pieces]
    return pl.pallas_call(
        functools.partial(pick_kernel, pieces),
        out_shape=[jax.ShapeDtypeStruct(shape, embeds.dtype) for shape in shapes],
        in_specs=[ANY if staged else HBM] * 3,
        out_specs=[ANY if staged else VMEM] * len(pieces),
        scratch_shapes=[
            pltpu.SMEM(pick_blk.shape, jnp.int32),
            pltpu.SMEM(pick_sub.shape, jnp.int32),
            pltpu.SemaphoreType.DMA((2,)),
            pltpu.SemaphoreType.DMA((len(pieces),)),
            pltpu.SemaphoreType.DMA((len(pieces),)),
        ]
        + [pltpu.VMEM(shape, embeds.dtype) for shape in shapes if staged],
        compiler_params=None if staged else PARAMS,
    )(pick_blk, pick_sub, embeds)


def prepare_kernel(slots, pick_blk, pick_sub, mask_blk, mask_sub, embeds, units, live, mine):
    for start in range(0, embeds.shape[0], BLOCK):
        units[start : start + BLOCK] = rounded_units(embeds[start : start + BLOCK])
    count = live.shape[1]
    block_of = lax.broadcasted_iota(jnp.int32, mine.shape[1:], 0) // ROWS
    for place, (axis, step, _, _) in enumerate(slots):
        source = lax.axis_index(axis) ^ step
        mask = mask_blk if axis == "blk" else mask_sub
        for i in range(count):
            value = mask[0, source * count + i].astype(jnp.float32)
            live[place, i : i + 1] = jnp.full((1, LANES), value, jnp.float32)
        pick = take_pick(axis, step, pick_blk, pick_sub)
        mine[place] = (block_of == pick).astype(jnp.float32)


def prepare(slots, pick_blk, pick_sub, mask_blk, mask_sub, embeds):
    count = embeds.shape[0] // BLOCK
    return pl.pallas_call(
        functools.partial(prepare_kernel, slots),
        out_shape=[
            jax.ShapeDtypeStruct(embeds.shape, embeds.dtype),
            jax.ShapeDtypeStruct((len(slots), count, LANES), jnp.float32),
            jax.ShapeDtypeStruct((len(slots), count * ROWS, LANES), jnp.float32),
        ],
        in_specs=[SMEM] * 4 + [VMEM],
        out_specs=[VMEM] * 3,
        compiler_params=PARAMS,
    )(pick_blk, pick_sub, mask_blk, mask_sub, embeds)


def slot_kernel(place, first, rows, back_place, carries, arrived, units, live, mine, totals, *rest):
    new_totals, back = rest[-2:]
    count = live.shape[1]
    before = totals[...]
    if back_place is not None:
        before = before + mine[back_place] * rest[0][...]
    new_totals[...] = before
    x = rounded_units(arrived[...])
    along_rows = jnp.zeros((rows, LANES), jnp.float32)
    for i in range(count):
        y = units[i * BLOCK : (i + 1) * BLOCK]
        cosines = lax.dot_general(x, y, (((1,), (1,)), ((), ())), preferred_element_type=jnp.float32)
        weights = soft_weights(cosines)
        alive = live[place, i : i + 1]
        for part in range(ROWS):
            piece = alive * weights[:, part * LANES : (part + 1) * LANES]
            along_rows = along_rows + piece
            row = i * ROWS + part
            new_totals[row : row + 1] = new_totals[row : row + 1] + jnp.sum(piece, axis=0, keepdims=True)
    empty = [jnp.zeros((gap, LANES), jnp.float32) for gap in (first, BLOCK - first - rows)]
    along_rows = jnp.concatenate([part for part in (empty[0], along_rows, empty[1]) if part.shape[0]], axis=0)
    for part in range(ROWS):
        sums = jnp.sum(along_rows[part * LANES : (part + 1) * LANES].T, axis=0, keepdims=True)
        for i in range(count):
            row = i * ROWS + part
            back[row : row + 1] = sums + rest[-3][row : row + 1] if carries else sums


def work(place, slot, arrived, units, live, mine, totals, returned, carried):
    back_place, came_back = returned or (None, None)
    operands = [arrived, units, live, mine, totals] + [one for one in (came_back, carried) if one is not None]
    return pl.pallas_call(
        functools.partial(slot_kernel, place, *slot[2:], back_place, carried is not None),
        out_shape=[jax.ShapeDtypeStruct(totals.shape, jnp.float32)] * 2,
        in_specs=[VMEM] * len(operands),
        out_specs=[VMEM] * 2,
        compiler_params=PARAMS,
    )(*operands)


BEHIND = 2
EARLY_ROWS = 192
HALF = BLOCK // 2


def plan_slots(sizes):
    slots = [("sub", 2, 0, EARLY_ROWS), ("blk", 1, 0, BLOCK), ("blk", 2, 0, BLOCK), ("sub", 1, 0, BLOCK)]
    slots += [("blk", k, first, HALF) for k in range(3, sizes["blk"]) for first in (0, HALF)]
    slots += [("sub", 2, EARLY_ROWS, BLOCK - EARLY_ROWS)]
    return slots + [("sub", k, 0, BLOCK) for k in range(3, sizes["sub"])]


AT_ONCE = 3


def body(embeds, pick_blk, mask_blk, pick_sub, mask_sub):
    count = embeds.shape[0] // BLOCK
    sizes = {"sub": lax.axis_size("sub"), "blk": lax.axis_size("blk")}
    slots = plan_slots(sizes)

    def send(array, slot):
        return lax.ppermute(array, slot[0], pairs(slot[1], sizes[slot[0]]))

    arrived = []
    for group, staged in ((slots[:AT_ONCE], True), (slots[AT_ONCE:], False)):
        for rows, slot in zip(pick_rows(group, pick_blk, pick_sub, embeds, staged), group):
            arrived.append(send(rows, slot))

    units, live, mine = prepare(slots, pick_blk, pick_sub, mask_blk, mask_sub, embeds)
    totals = jnp.zeros((count * ROWS, LANES), jnp.float32)
    carried = {}
    soon, late = [], []
    for place, slot in enumerate(slots):
        axis, step, first, rows = slot
        ready = soon.pop(0) if soon and soon[0][0] <= place - BEHIND else None
        totals, back = work(
            place, slot, arrived[place], units, live, mine, totals, ready, carried.pop((axis, step), None)
        )
        if first + rows < BLOCK:
            carried[axis, step] = back
        else:
            (soon if axis == "blk" else late).append((place, send(back, slot)))
    for place, sums in soon + late:
        totals = totals + mine[place] * sums
    return (totals * (1.0 / BLOCK)).reshape(-1)


def solution(mesh):
    return jax.shard_map(
        body,
        mesh=mesh,
        in_specs=(
            P(("groups", "blk", "sub"), None),
            P(("groups", "blk", "sub"), None),
            P(("groups", "blk", "sub"), None),
            P(("groups", "blk"), None),
            P(("groups", "blk", "sub"), None),
        ),
        out_specs=P(("groups", "blk", "sub")),
        check_vma=False,
    )
```

```python
import functools
import math

import jax
import jax.numpy as jnp
from jax import lax
from jax.experimental import pallas as pl
from jax.experimental.pallas import tpu as pltpu
from jax.sharding import PartitionSpec as P

BLOCK = 256
LANES = 128
ROWS = BLOCK // LANES

cutoff = 0.05
sharpness = 100.0

SMEM = pl.BlockSpec(memory_space=pltpu.SMEM)
VMEM = pl.BlockSpec(memory_space=pltpu.VMEM)
HBM = pl.BlockSpec(memory_space=pltpu.HBM)
ANY = pl.BlockSpec(memory_space=pl.ANY)
PARAMS = pltpu.CompilerParams(vmem_limit_bytes=32 * 2**20)


def pairs(step, size):
    return [(i, i ^ step) for i in range(size)]


def rounded_units(rows):
    wide = rows.astype(jnp.float32)
    scale = lax.rsqrt(jnp.sum(wide * wide, axis=1, keepdims=True) + 1e-06)
    return (wide * scale).astype(jnp.bfloat16)


def soft_weights(cosines):
    rate = sharpness * math.log2(math.e)
    below = 1.0 + jnp.exp2(jnp.minimum(cutoff * rate - cosines * rate, 125.0))
    guess = pl.reciprocal(below, approx=True)
    return guess * (2.0 - below * guess)


def take_pick(axis, step, pick_blk, pick_sub):
    target = lax.axis_index(axis) ^ step
    return pick_blk[0, target] if axis == "blk" else pick_sub[lax.axis_index("sub"), target]


def pick_kernel(pieces, pick_blk, pick_sub, embeds, *rest):
    outs, (blk_scalars, sub_scalars, scalar_sems, in_sems, out_sems, *staged) = rest[: len(pieces)], rest[len(pieces) :]
    scalars = [
        pltpu.make_async_copy(pick_blk, blk_scalars, scalar_sems.at[0]),
        pltpu.make_async_copy(pick_sub, sub_scalars, scalar_sems.at[1]),
    ]
    for copy in scalars:
        copy.start()
    for copy in scalars:
        copy.wait()
    copies = []
    for place, (axis, step, first, rows) in enumerate(pieces):
        pick = take_pick(axis, step, blk_scalars, sub_scalars)
        start = pl.multiple_of(pick * BLOCK + first, math.gcd(BLOCK, first))
        target = staged[place] if staged else outs[place]
        copies.append(pltpu.make_async_copy(embeds.at[pl.ds(start, rows)], target, in_sems.at[place]))
        copies[-1].start()
    leaving = []
    for place, copy in enumerate(copies):
        copy.wait()
        if staged:
            leaving.append(pltpu.make_async_copy(staged[place], outs[place], out_sems.at[place]))
            leaving[-1].start()
    for copy in leaving:
        copy.wait()


def pick_rows(pieces, pick_blk, pick_sub, embeds, staged):
    shapes = [(rows, embeds.shape[1]) for _, _, _, rows in pieces]
    return pl.pallas_call(
        functools.partial(pick_kernel, pieces),
        out_shape=[jax.ShapeDtypeStruct(shape, embeds.dtype) for shape in shapes],
        in_specs=[ANY if staged else HBM] * 3,
        out_specs=[ANY if staged else VMEM] * len(pieces),
        scratch_shapes=[
            pltpu.SMEM(pick_blk.shape, jnp.int32),
            pltpu.SMEM(pick_sub.shape, jnp.int32),
            pltpu.SemaphoreType.DMA((2,)),
            pltpu.SemaphoreType.DMA((len(pieces),)),
            pltpu.SemaphoreType.DMA((len(pieces),)),
        ]
        + [pltpu.VMEM(shape, embeds.dtype) for shape in shapes if staged],
        compiler_params=None if staged else PARAMS,
    )(pick_blk, pick_sub, embeds)


def prepare_kernel(slots, pick_blk, pick_sub, mask_blk, mask_sub, embeds, units, live, mine):
    for start in range(0, embeds.shape[0], BLOCK):
        units[start : start + BLOCK] = rounded_units(embeds[start : start + BLOCK])
    count = live.shape[1]
    block_of = lax.broadcasted_iota(jnp.int32, mine.shape[1:], 0) // ROWS
    for place, (axis, step, _, _) in enumerate(slots):
        source = lax.axis_index(axis) ^ step
        mask = mask_blk if axis == "blk" else mask_sub
        for i in range(count):
            value = mask[0, source * count + i].astype(jnp.float32)
            live[place, i : i + 1] = jnp.full((1, LANES), value, jnp.float32)
        pick = take_pick(axis, step, pick_blk, pick_sub)
        mine[place] = (block_of == pick).astype(jnp.float32)


def prepare(slots, pick_blk, pick_sub, mask_blk, mask_sub, embeds):
    count = embeds.shape[0] // BLOCK
    return pl.pallas_call(
        functools.partial(prepare_kernel, slots),
        out_shape=[
            jax.ShapeDtypeStruct(embeds.shape, embeds.dtype),
            jax.ShapeDtypeStruct((len(slots), count, LANES), jnp.float32),
            jax.ShapeDtypeStruct((len(slots), count * ROWS, LANES), jnp.float32),
        ],
        in_specs=[SMEM] * 4 + [VMEM],
        out_specs=[VMEM] * 3,
        compiler_params=PARAMS,
    )(pick_blk, pick_sub, mask_blk, mask_sub, embeds)


def slot_kernel(place, first, rows, back_places, carries, arrived, units, live, mine, totals, *rest):
    new_totals, back = rest[-2:]
    count = live.shape[1]
    before = totals[...]
    for back_place, sums in zip(back_places, rest):
        before = before + mine[back_place] * sums[...]
    new_totals[...] = before
    x = rounded_units(arrived[...])
    along_rows = jnp.zeros((rows, LANES), jnp.float32)
    for i in range(count):
        y = units[i * BLOCK : (i + 1) * BLOCK]
        cosines = lax.dot_general(x, y, (((1,), (1,)), ((), ())), preferred_element_type=jnp.float32)
        weights = soft_weights(cosines)
        alive = live[place, i : i + 1]
        for part in range(ROWS):
            piece = alive * weights[:, part * LANES : (part + 1) * LANES]
            along_rows = along_rows + piece
            row = i * ROWS + part
            new_totals[row : row + 1] = new_totals[row : row + 1] + jnp.sum(piece, axis=0, keepdims=True)
    empty = [jnp.zeros((gap, LANES), jnp.float32) for gap in (first, BLOCK - first - rows)]
    along_rows = jnp.concatenate([part for part in (empty[0], along_rows, empty[1]) if part.shape[0]], axis=0)
    for part in range(ROWS):
        sums = jnp.sum(along_rows[part * LANES : (part + 1) * LANES].T, axis=0, keepdims=True)
        for i in range(count):
            row = i * ROWS + part
            back[row : row + 1] = sums + rest[-3][row : row + 1] if carries else sums


def work(place, slot, arrived, units, live, mine, totals, returned, carried):
    operands = [arrived, units, live, mine, totals] + [sums for _, sums in returned]
    operands += [] if carried is None else [carried]
    return pl.pallas_call(
        functools.partial(slot_kernel, place, *slot[2:], [one for one, _ in returned], carried is not None),
        out_shape=[jax.ShapeDtypeStruct(totals.shape, jnp.float32)] * 2,
        in_specs=[VMEM] * len(operands),
        out_specs=[VMEM] * 2,
        compiler_params=PARAMS,
    )(*operands)


BEHIND = 2
EARLY_ROWS = 192
HALF = BLOCK // 2


def plan_slots(sizes):
    slots = [("sub", 2, 0, EARLY_ROWS), ("sub", 2, EARLY_ROWS, BLOCK - EARLY_ROWS)]
    slots += [("blk", 1, 0, BLOCK), ("blk", 2, 0, BLOCK), ("sub", 1, 0, BLOCK)]
    slots += [("blk", k, first, HALF) for k in range(3, sizes["blk"]) for first in (0, HALF)]
    return slots + [("sub", k, 0, BLOCK) for k in range(3, sizes["sub"])]


EARLY_ROWS = 160
HALF = BLOCK // 2
AT_ONCE = 3


def body(embeds, pick_blk, mask_blk, pick_sub, mask_sub):
    count = embeds.shape[0] // BLOCK
    sizes = {"sub": lax.axis_size("sub"), "blk": lax.axis_size("blk")}
    slots = plan_slots(sizes)

    def send(array, slot):
        return lax.ppermute(array, slot[0], pairs(slot[1], sizes[slot[0]]))

    arrived = []
    for group, staged in ((slots[:AT_ONCE], True), (slots[AT_ONCE:], False)):
        for rows, slot in zip(pick_rows(group, pick_blk, pick_sub, embeds, staged), group):
            arrived.append(send(rows, slot))

    units, live, mine = prepare(slots, pick_blk, pick_sub, mask_blk, mask_sub, embeds)
    totals = jnp.zeros((count * ROWS, LANES), jnp.float32)
    carried = {}
    soon, late = [], []
    for place, slot in enumerate(slots):
        axis, step, first, rows = slot
        if place == len(slots) - 1:
            ready, soon, late = soon + late, [], []
        else:
            done = sum(sent <= place - BEHIND for sent, _ in soon)
            ready, soon = soon[:done], soon[done:]
        totals, back = work(
            place, slot, arrived[place], units, live, mine, totals, ready, carried.pop((axis, step), None)
        )
        if first + rows < BLOCK:
            carried[axis, step] = back
        else:
            (soon if axis == "blk" else late).append((place, send(back, slot)))
    for place, sums in late:
        totals = totals + mine[place] * sums
    return (totals * (1.0 / BLOCK)).reshape(-1)


def solution(mesh):
    return jax.shard_map(
        body,
        mesh=mesh,
        in_specs=(
            P(("groups", "blk", "sub"), None),
            P(("groups", "blk", "sub"), None),
            P(("groups", "blk", "sub"), None),
            P(("groups", "blk"), None),
            P(("groups", "blk", "sub"), None),
        ),
        out_specs=P(("groups", "blk", "sub")),
        check_vma=False,
    )
```

```python
import functools
import math

import jax
import jax.numpy as jnp
from jax import lax
from jax.experimental import pallas as pl
from jax.experimental.pallas import tpu as pltpu
from jax.sharding import PartitionSpec as P

BLOCK = 256
LANES = 128
ROWS = BLOCK // LANES

cutoff = 0.05
sharpness = 100.0

SMEM = pl.BlockSpec(memory_space=pltpu.SMEM)
VMEM = pl.BlockSpec(memory_space=pltpu.VMEM)
HBM = pl.BlockSpec(memory_space=pltpu.HBM)
ANY = pl.BlockSpec(memory_space=pl.ANY)
PARAMS = pltpu.CompilerParams(vmem_limit_bytes=32 * 2**20)


def pairs(step, size):
    return [(i, i ^ step) for i in range(size)]


def rounded_units(rows):
    wide = rows.astype(jnp.float32)
    scale = lax.rsqrt(jnp.sum(wide * wide, axis=1, keepdims=True) + 1e-06)
    return (wide * scale).astype(jnp.bfloat16)


def soft_weights(cosines):
    rate = sharpness * math.log2(math.e)
    return pltpu.reciprocal(1.0 + jnp.exp2(cutoff * rate - cosines * rate), approx=True)


def take_pick(axis, step, pick_blk, pick_sub):
    target = lax.axis_index(axis) ^ step
    return pick_blk[0, target] if axis == "blk" else pick_sub[lax.axis_index("sub"), target]


def pick_kernel(pieces, pick_blk, pick_sub, embeds, *rest):
    outs, (blk_scalars, sub_scalars, scalar_sems, in_sems, out_sems, *staged) = rest[: len(pieces)], rest[len(pieces) :]
    scalars = [
        pltpu.make_async_copy(pick_blk, blk_scalars, scalar_sems.at[0]),
        pltpu.make_async_copy(pick_sub, sub_scalars, scalar_sems.at[1]),
    ]
    for copy in scalars:
        copy.start()
    for copy in scalars:
        copy.wait()
    copies = []
    for place, (axis, step, first, rows) in enumerate(pieces):
        pick = take_pick(axis, step, blk_scalars, sub_scalars)
        start = pl.multiple_of(pick * BLOCK + first, math.gcd(BLOCK, first))
        target = staged[place] if staged else outs[place]
        copies.append(pltpu.make_async_copy(embeds.at[pl.ds(start, rows)], target, in_sems.at[place]))
        copies[-1].start()
    leaving = []
    for place, copy in enumerate(copies):
        copy.wait()
        if staged:
            leaving.append(pltpu.make_async_copy(staged[place], outs[place], out_sems.at[place]))
            leaving[-1].start()
    for copy in leaving:
        copy.wait()


def pick_rows(pieces, pick_blk, pick_sub, embeds, staged):
    shapes = [(rows, embeds.shape[1]) for _, _, _, rows in pieces]
    return pl.pallas_call(
        functools.partial(pick_kernel, pieces),
        out_shape=[jax.ShapeDtypeStruct(shape, embeds.dtype) for shape in shapes],
        in_specs=[ANY if staged else HBM] * 3,
        out_specs=[ANY if staged else VMEM] * len(pieces),
        scratch_shapes=[
            pltpu.SMEM(pick_blk.shape, jnp.int32),
            pltpu.SMEM(pick_sub.shape, jnp.int32),
            pltpu.SemaphoreType.DMA((2,)),
            pltpu.SemaphoreType.DMA((len(pieces),)),
            pltpu.SemaphoreType.DMA((len(pieces),)),
        ]
        + [pltpu.VMEM(shape, embeds.dtype) for shape in shapes if staged],
        compiler_params=None if staged else PARAMS,
    )(pick_blk, pick_sub, embeds)


def prepare_kernel(slots, pick_blk, pick_sub, mask_blk, mask_sub, embeds, units, live, mine, rows, sems):
    count = live.shape[1]
    copies = [
        pltpu.make_async_copy(embeds.at[pl.ds(i * BLOCK, BLOCK)], rows.at[pl.ds(i * BLOCK, BLOCK)], sems.at[i])
        for i in range(count)
    ]
    for copy in copies:
        copy.start()
    block_of = lax.broadcasted_iota(jnp.int32, mine.shape[1:], 0) // ROWS
    for place, (axis, step, _, _) in enumerate(slots):
        source = lax.axis_index(axis) ^ step
        mask = mask_blk if axis == "blk" else mask_sub
        for i in range(count):
            value = mask[0, source * count + i].astype(jnp.float32)
            live[place, i : i + 1] = jnp.full((1, LANES), value, jnp.float32)
        pick = take_pick(axis, step, pick_blk, pick_sub)
        mine[place] = (block_of == pick).astype(jnp.float32)
    for i, copy in enumerate(copies):
        copy.wait()
        units[i * BLOCK : (i + 1) * BLOCK] = rounded_units(rows[i * BLOCK : (i + 1) * BLOCK])


def prepare(slots, pick_blk, pick_sub, mask_blk, mask_sub, embeds):
    count = embeds.shape[0] // BLOCK
    return pl.pallas_call(
        functools.partial(prepare_kernel, slots),
        out_shape=[
            jax.ShapeDtypeStruct(embeds.shape, embeds.dtype),
            jax.ShapeDtypeStruct((len(slots), count, LANES), jnp.float32),
            jax.ShapeDtypeStruct((len(slots), count * ROWS, LANES), jnp.float32),
        ],
        in_specs=[SMEM] * 4 + [ANY],
        out_specs=[VMEM] * 3,
        scratch_shapes=[pltpu.VMEM(embeds.shape, embeds.dtype), pltpu.SemaphoreType.DMA((count,))],
    )(pick_blk, pick_sub, mask_blk, mask_sub, embeds)


def slot_kernel(place, first, rows, back_places, carries, arrived, units, live, mine, totals, *rest):
    new_totals, back = rest[-2:]
    count = live.shape[1]
    before = totals[...]
    for back_place, sums in zip(back_places, rest):
        before = before + mine[back_place] * sums[...]
    new_totals[...] = before
    x = rounded_units(arrived[...])
    along_rows = jnp.zeros((rows, LANES), jnp.float32)
    for i in range(count):
        y = units[i * BLOCK : (i + 1) * BLOCK]
        cosines = lax.dot_general(x, y, (((1,), (1,)), ((), ())), preferred_element_type=jnp.float32)
        weights = soft_weights(cosines)
        alive = live[place, i : i + 1]
        parts = [weights[:, part * LANES : (part + 1) * LANES] for part in range(ROWS)]
        along_rows = along_rows + alive * sum(parts)
        for part, piece in enumerate(parts):
            row = i * ROWS + part
            new_totals[row : row + 1] = new_totals[row : row + 1] + alive * jnp.sum(piece, axis=0, keepdims=True)
    empty = [jnp.zeros((gap, LANES), jnp.float32) for gap in (first, BLOCK - first - rows)]
    along_rows = jnp.concatenate([part for part in (empty[0], along_rows, empty[1]) if part.shape[0]], axis=0)
    for part in range(ROWS):
        sums = jnp.sum(along_rows[part * LANES : (part + 1) * LANES].T, axis=0, keepdims=True)
        for i in range(count):
            row = i * ROWS + part
            back[row : row + 1] = sums + rest[-3][row : row + 1] if carries else sums


def work(place, slot, arrived, units, live, mine, totals, returned, carried):
    operands = [arrived, units, live, mine, totals] + [sums for _, sums in returned]
    operands += [] if carried is None else [carried]
    return pl.pallas_call(
        functools.partial(slot_kernel, place, *slot[2:], [one for one, _ in returned], carried is not None),
        out_shape=[jax.ShapeDtypeStruct(totals.shape, jnp.float32)] * 2,
        in_specs=[VMEM] * len(operands),
        out_specs=[VMEM] * 2,
        compiler_params=PARAMS,
    )(*operands)


BEHIND = 2
EARLY_ROWS = 192
HALF = BLOCK // 2


def plan_slots(sizes):
    slots = [("sub", 2, 0, EARLY_ROWS), ("sub", 2, EARLY_ROWS, BLOCK - EARLY_ROWS)]
    slots += [("blk", 1, 0, BLOCK), ("blk", 2, 0, BLOCK)]
    slots += [("blk", k, first, HALF) for k in range(3, sizes["blk"]) for first in (0, HALF)]
    return slots + [("sub", k, 0, BLOCK) for k in (1, *range(3, sizes["sub"]))]


EARLY_ROWS = 192
HALF = BLOCK // 2


def plan_slots(sizes):
    slots = [("sub", 2, 0, EARLY_ROWS), ("sub", 2, EARLY_ROWS, BLOCK - EARLY_ROWS)]
    slots += [("blk", 1, 0, BLOCK), ("blk", 2, 0, BLOCK), ("sub", 1, 0, BLOCK)]
    slots += [("blk", k, first, HALF) for k in range(3, sizes["blk"]) for first in (0, HALF)]
    return slots + [("sub", k, 0, BLOCK) for k in range(3, sizes["sub"])]


EARLY_ROWS = 160
HALF = BLOCK // 2
AT_ONCE = 3


def body(embeds, pick_blk, mask_blk, pick_sub, mask_sub):
    count = embeds.shape[0] // BLOCK
    sizes = {"sub": lax.axis_size("sub"), "blk": lax.axis_size("blk")}
    slots = plan_slots(sizes)

    def send(array, slot):
        return lax.ppermute(array, slot[0], pairs(slot[1], sizes[slot[0]]))

    arrived = []
    for group, staged in ((slots[:AT_ONCE], True), (slots[AT_ONCE:], False)):
        for rows, slot in zip(pick_rows(group, pick_blk, pick_sub, embeds, staged), group):
            arrived.append(send(rows, slot))

    units, live, mine = prepare(slots, pick_blk, pick_sub, mask_blk, mask_sub, embeds)
    totals = jnp.zeros((count * ROWS, LANES), jnp.float32)
    carried = {}
    soon, late = [], []
    for place, slot in enumerate(slots):
        axis, step, first, rows = slot
        if place == len(slots) - 1:
            ready, soon, late = soon + late, [], []
        else:
            done = sum(sent <= place - BEHIND for sent, _ in soon)
            ready, soon = soon[:done], soon[done:]
        totals, back = work(
            place, slot, arrived[place], units, live, mine, totals, ready, carried.pop((axis, step), None)
        )
        if first + rows < BLOCK:
            carried[axis, step] = back
        else:
            (soon if axis == "blk" else late).append((place, send(back, slot)))
    for place, sums in late:
        totals = totals + mine[place] * sums
    return (totals * (1.0 / BLOCK)).reshape(-1)


def solution(mesh):
    return jax.shard_map(
        body,
        mesh=mesh,
        in_specs=(
            P(("groups", "blk", "sub"), None),
            P(("groups", "blk", "sub"), None),
            P(("groups", "blk", "sub"), None),
            P(("groups", "blk"), None),
            P(("groups", "blk", "sub"), None),
        ),
        out_specs=P(("groups", "blk", "sub")),
        check_vma=False,
    )
```

```python
import functools
import math

import jax
import jax.numpy as jnp
from jax import lax
from jax.experimental import pallas as pl
from jax.experimental.pallas import tpu as pltpu
from jax.sharding import PartitionSpec as P

BLOCK = 256
LANES = 128
ROWS = BLOCK // LANES

cutoff = 0.05
sharpness = 100.0

SMEM = pl.BlockSpec(memory_space=pltpu.SMEM)
VMEM = pl.BlockSpec(memory_space=pltpu.VMEM)
HBM = pl.BlockSpec(memory_space=pltpu.HBM)
ANY = pl.BlockSpec(memory_space=pl.ANY)
PARAMS = pltpu.CompilerParams(vmem_limit_bytes=32 * 2**20)


def pairs(step, size):
    return [(i, i ^ step) for i in range(size)]


def rounded_units(rows):
    wide = rows.astype(jnp.float32)
    scale = lax.rsqrt(jnp.sum(wide * wide, axis=1, keepdims=True) + 1e-06)
    return (wide * scale).astype(jnp.bfloat16)


def soft_weights(cosines):
    rate = sharpness * math.log2(math.e)
    return pltpu.reciprocal(1.0 + jnp.exp2(cutoff * rate - cosines * rate), approx=True)


def take_pick(axis, step, pick_blk, pick_sub):
    target = lax.axis_index(axis) ^ step
    return pick_blk[0, target] if axis == "blk" else pick_sub[lax.axis_index("sub"), target]


def pick_kernel(pieces, pick_blk, pick_sub, embeds, *rest):
    outs, (blk_scalars, sub_scalars, scalar_sems, in_sems, out_sems, *staged) = rest[: len(pieces)], rest[len(pieces) :]
    scalars = [
        pltpu.make_async_copy(pick_blk, blk_scalars, scalar_sems.at[0]),
        pltpu.make_async_copy(pick_sub, sub_scalars, scalar_sems.at[1]),
    ]
    for copy in scalars:
        copy.start()
    for copy in scalars:
        copy.wait()
    copies = []
    for place, (axis, step, first, rows) in enumerate(pieces):
        pick = take_pick(axis, step, blk_scalars, sub_scalars)
        start = pl.multiple_of(pick * BLOCK + first, math.gcd(BLOCK, first))
        target = staged[place] if staged else outs[place]
        copies.append(pltpu.make_async_copy(embeds.at[pl.ds(start, rows)], target, in_sems.at[place]))
        copies[-1].start()
    leaving = []
    for place, copy in enumerate(copies):
        copy.wait()
        if staged:
            leaving.append(pltpu.make_async_copy(staged[place], outs[place], out_sems.at[place]))
            leaving[-1].start()
    for copy in leaving:
        copy.wait()


def pick_rows(pieces, pick_blk, pick_sub, embeds, staged):
    shapes = [(rows, embeds.shape[1]) for _, _, _, rows in pieces]
    return pl.pallas_call(
        functools.partial(pick_kernel, pieces),
        out_shape=[jax.ShapeDtypeStruct(shape, embeds.dtype) for shape in shapes],
        in_specs=[ANY if staged else HBM] * 3,
        out_specs=[ANY if staged else VMEM] * len(pieces),
        scratch_shapes=[
            pltpu.SMEM(pick_blk.shape, jnp.int32),
            pltpu.SMEM(pick_sub.shape, jnp.int32),
            pltpu.SemaphoreType.DMA((2,)),
            pltpu.SemaphoreType.DMA((len(pieces),)),
            pltpu.SemaphoreType.DMA((len(pieces),)),
        ]
        + [pltpu.VMEM(shape, embeds.dtype) for shape in shapes if staged],
        compiler_params=None if staged else PARAMS,
    )(pick_blk, pick_sub, embeds)


def prepare_kernel(slots, pick_blk, pick_sub, mask_blk, mask_sub, embeds, units, live, mine):
    for start in range(0, embeds.shape[0], BLOCK):
        units[start : start + BLOCK] = rounded_units(embeds[start : start + BLOCK])
    count = live.shape[1]
    block_of = lax.broadcasted_iota(jnp.int32, mine.shape[1:], 0) // ROWS
    for place, (axis, step, _, _) in enumerate(slots):
        source = lax.axis_index(axis) ^ step
        mask = mask_blk if axis == "blk" else mask_sub
        for i in range(count):
            value = mask[0, source * count + i].astype(jnp.float32)
            live[place, i : i + 1] = jnp.full((1, LANES), value, jnp.float32)
        pick = take_pick(axis, step, pick_blk, pick_sub)
        mine[place] = (block_of == pick).astype(jnp.float32)


def prepare(slots, pick_blk, pick_sub, mask_blk, mask_sub, embeds):
    count = embeds.shape[0] // BLOCK
    return pl.pallas_call(
        functools.partial(prepare_kernel, slots),
        out_shape=[
            jax.ShapeDtypeStruct(embeds.shape, embeds.dtype),
            jax.ShapeDtypeStruct((len(slots), count, LANES), jnp.float32),
            jax.ShapeDtypeStruct((len(slots), count * ROWS, LANES), jnp.float32),
        ],
        in_specs=[SMEM] * 4 + [VMEM],
        out_specs=[VMEM] * 3,
        compiler_params=PARAMS,
    )(pick_blk, pick_sub, mask_blk, mask_sub, embeds)


def slot_kernel(place, first, rows, back_places, carries, arrived, units, live, mine, totals, *rest):
    new_totals, back = rest[-2:]
    count = live.shape[1]
    before = totals[...]
    for back_place, sums in zip(back_places, rest):
        before = before + mine[back_place] * sums[...]
    new_totals[...] = before
    x = rounded_units(arrived[...])
    along_rows = jnp.zeros((rows, LANES), jnp.float32)
    for i in range(count):
        y = units[i * BLOCK : (i + 1) * BLOCK]
        cosines = lax.dot_general(x, y, (((1,), (1,)), ((), ())), preferred_element_type=jnp.float32)
        weights = soft_weights(cosines)
        alive = live[place, i : i + 1]
        parts = [weights[:, part * LANES : (part + 1) * LANES] for part in range(ROWS)]
        along_rows = along_rows + alive * sum(parts)
        for part, piece in enumerate(parts):
            row = i * ROWS + part
            new_totals[row : row + 1] = new_totals[row : row + 1] + alive * jnp.sum(piece, axis=0, keepdims=True)
    empty = [jnp.zeros((gap, LANES), jnp.float32) for gap in (first, BLOCK - first - rows)]
    along_rows = jnp.concatenate([part for part in (empty[0], along_rows, empty[1]) if part.shape[0]], axis=0)
    for part in range(ROWS):
        sums = jnp.sum(along_rows[part * LANES : (part + 1) * LANES].T, axis=0, keepdims=True)
        for i in range(count):
            row = i * ROWS + part
            back[row : row + 1] = sums + rest[-3][row : row + 1] if carries else sums


def work(place, slot, arrived, units, live, mine, totals, returned, carried):
    operands = [arrived, units, live, mine, totals] + [sums for _, sums in returned]
    operands += [] if carried is None else [carried]
    return pl.pallas_call(
        functools.partial(slot_kernel, place, *slot[2:], [one for one, _ in returned], carried is not None),
        out_shape=[jax.ShapeDtypeStruct(totals.shape, jnp.float32)] * 2,
        in_specs=[VMEM] * len(operands),
        out_specs=[VMEM] * 2,
        compiler_params=PARAMS,
    )(*operands)


BEHIND = 2
EARLY_ROWS = 192
HALF = BLOCK // 2


FIRST_CUT = 240


def plan_slots(sizes):
    slots = [("blk", 1, 0, BLOCK), ("sub", 2, 0, BLOCK), ("blk", 2, 0, BLOCK)]
    for k in range(3, sizes["blk"]):
        slots += [("blk", k, 0, FIRST_CUT), ("blk", k, FIRST_CUT, BLOCK - FIRST_CUT)]
    return slots + [("sub", k, 0, BLOCK) for k in (1, *range(3, sizes["sub"]))]


AT_ONCE = 2


def body(embeds, pick_blk, mask_blk, pick_sub, mask_sub):
    count = embeds.shape[0] // BLOCK
    sizes = {"sub": lax.axis_size("sub"), "blk": lax.axis_size("blk")}
    slots = plan_slots(sizes)

    def send(array, slot):
        return lax.ppermute(array, slot[0], pairs(slot[1], sizes[slot[0]]))

    arrived = []
    for group, staged in ((slots[:AT_ONCE], True), (slots[AT_ONCE:], False)):
        for rows, slot in zip(pick_rows(group, pick_blk, pick_sub, embeds, staged), group):
            arrived.append(send(rows, slot))

    units, live, mine = prepare(slots, pick_blk, pick_sub, mask_blk, mask_sub, embeds)
    totals = jnp.zeros((count * ROWS, LANES), jnp.float32)
    carried = {}
    soon, late = [], []
    for place, slot in enumerate(slots):
        axis, step, first, rows = slot
        if place == len(slots) - 1:
            ready, soon, late = soon + late, [], []
        else:
            done = sum(sent <= place - BEHIND for sent, _ in soon)
            ready, soon = soon[:done], soon[done:]
        totals, back = work(
            place, slot, arrived[place], units, live, mine, totals, ready, carried.pop((axis, step), None)
        )
        if first + rows < BLOCK:
            carried[axis, step] = back
        else:
            (soon if axis == "blk" else late).append((place, send(back, slot)))
    for place, sums in late:
        totals = totals + mine[place] * sums
    return (totals * (1.0 / BLOCK)).reshape(-1)


def solution(mesh):
    return jax.shard_map(
        body,
        mesh=mesh,
        in_specs=(
            P(("groups", "blk", "sub"), None),
            P(("groups", "blk", "sub"), None),
            P(("groups", "blk", "sub"), None),
            P(("groups", "blk"), None),
            P(("groups", "blk", "sub"), None),
        ),
        out_specs=P(("groups", "blk", "sub")),
        check_vma=False,
    )
```

```python
import functools
import math

import jax
import jax.numpy as jnp
from jax import lax
from jax.experimental import pallas as pl
from jax.experimental.pallas import tpu as pltpu
from jax.sharding import PartitionSpec as P

BLOCK = 256
LANES = 128
ROWS = BLOCK // LANES

cutoff = 0.05
sharpness = 100.0

SMEM = pl.BlockSpec(memory_space=pltpu.SMEM)
VMEM = pl.BlockSpec(memory_space=pltpu.VMEM)
HBM = pl.BlockSpec(memory_space=pltpu.HBM)
ANY = pl.BlockSpec(memory_space=pl.ANY)
PARAMS = pltpu.CompilerParams(vmem_limit_bytes=32 * 2**20)


def pairs(step, size):
    return [(i, i ^ step) for i in range(size)]


def rounded_units(rows):
    wide = rows.astype(jnp.float32)
    scale = lax.rsqrt(jnp.sum(wide * wide, axis=1, keepdims=True) + 1e-06)
    return (wide * scale).astype(jnp.bfloat16)


def soft_weights(cosines):
    rate = sharpness * math.log2(math.e)
    return pltpu.reciprocal(1.0 + jnp.exp2(cutoff * rate - cosines * rate), approx=True)


def take_pick(axis, step, pick_blk, pick_sub):
    target = lax.axis_index(axis) ^ step
    return pick_blk[0, target] if axis == "blk" else pick_sub[lax.axis_index("sub"), target]


def first_kernel(slot, pick_sub, embeds, out, scalars, staged, scalar_sem, in_sems, out_sems):
    axis, step, first, rows = slot
    copy = pltpu.make_async_copy(pick_sub, scalars, scalar_sem)
    copy.start()
    copy.wait()
    pick = take_pick(axis, step, None, scalars)
    part = rows // PARTS
    entering, leaving = [], []
    for i in range(PARTS):
        start = pl.multiple_of(pick * BLOCK + (first + i * part), part)
        here = staged.at[pl.ds(i * part, part)]
        entering.append(pltpu.make_async_copy(embeds.at[pl.ds(start, part)], here, in_sems.at[i]))
        leaving.append(pltpu.make_async_copy(here, out.at[pl.ds(i * part, part)], out_sems.at[i]))
        entering[i].start()
    for i in range(PARTS):
        entering[i].wait()
        leaving[i].start()
    for copy in leaving:
        copy.wait()


PARTS = 4


def first_rows(slot, pick_sub, embeds):
    shape = (slot[3], embeds.shape[1])
    return pl.pallas_call(
        functools.partial(first_kernel, slot),
        out_shape=jax.ShapeDtypeStruct(shape, embeds.dtype),
        in_specs=[ANY, ANY],
        out_specs=ANY,
        scratch_shapes=[
            pltpu.SMEM(pick_sub.shape, jnp.int32),
            pltpu.VMEM(shape, embeds.dtype),
            pltpu.SemaphoreType.DMA,
            pltpu.SemaphoreType.DMA((PARTS,)),
            pltpu.SemaphoreType.DMA((PARTS,)),
        ],
    )(pick_sub, embeds)


def pick_kernel(slots, pick_blk, pick_sub, embeds, *rest):
    outs, (blk_scalars, sub_scalars, scalar_sems, row_sems) = rest[: len(slots)], rest[len(slots) :]
    scalars = [
        pltpu.make_async_copy(pick_blk, blk_scalars, scalar_sems.at[0]),
        pltpu.make_async_copy(pick_sub, sub_scalars, scalar_sems.at[1]),
    ]
    for copy in scalars:
        copy.start()
    for copy in scalars:
        copy.wait()
    copies = []
    for place, (axis, step, first, rows) in enumerate(slots):
        pick = take_pick(axis, step, blk_scalars, sub_scalars)
        start = pl.multiple_of(pick * BLOCK + first, math.gcd(BLOCK, first))
        copies.append(pltpu.make_async_copy(embeds.at[pl.ds(start, rows)], outs[place], row_sems.at[place]))
        copies[-1].start()
    for copy in copies:
        copy.wait()


def pick_rows(slots, pick_blk, pick_sub, embeds):
    return pl.pallas_call(
        functools.partial(pick_kernel, slots),
        out_shape=[jax.ShapeDtypeStruct((rows, embeds.shape[1]), embeds.dtype) for _, _, _, rows in slots],
        in_specs=[HBM] * 3,
        out_specs=[VMEM] * len(slots),
        scratch_shapes=[
            pltpu.SMEM(pick_blk.shape, jnp.int32),
            pltpu.SMEM(pick_sub.shape, jnp.int32),
            pltpu.SemaphoreType.DMA((2,)),
            pltpu.SemaphoreType.DMA((len(slots),)),
        ],
        compiler_params=PARAMS,
    )(pick_blk, pick_sub, embeds)


def prepare_kernel(slots, pick_blk, pick_sub, mask_blk, mask_sub, embeds, units, live, mine):
    for start in range(0, embeds.shape[0], BLOCK):
        units[start : start + BLOCK] = rounded_units(embeds[start : start + BLOCK])
    count = live.shape[1]
    block_of = lax.broadcasted_iota(jnp.int32, mine.shape[1:], 0) // ROWS
    for place, (axis, step, _, _) in enumerate(slots):
        source = lax.axis_index(axis) ^ step
        mask = mask_blk if axis == "blk" else mask_sub
        for i in range(count):
            value = mask[0, source * count + i].astype(jnp.float32)
            live[place, i : i + 1] = jnp.full((1, LANES), value, jnp.float32)
        pick = take_pick(axis, step, pick_blk, pick_sub)
        mine[place] = (block_of == pick).astype(jnp.float32)


def prepare(slots, pick_blk, pick_sub, mask_blk, mask_sub, embeds):
    count = embeds.shape[0] // BLOCK
    return pl.pallas_call(
        functools.partial(prepare_kernel, slots),
        out_shape=[
            jax.ShapeDtypeStruct(embeds.shape, embeds.dtype),
            jax.ShapeDtypeStruct((len(slots), count, LANES), jnp.float32),
            jax.ShapeDtypeStruct((len(slots), count * ROWS, LANES), jnp.float32),
        ],
        in_specs=[SMEM] * 4 + [VMEM],
        out_specs=[VMEM] * 3,
        compiler_params=PARAMS,
    )(pick_blk, pick_sub, mask_blk, mask_sub, embeds)


def slot_kernel(place, first, rows, back_places, carries, arrived, units, live, mine, totals, *rest):
    new_totals, back = rest[-2:]
    count = live.shape[1]
    before = totals[...]
    for back_place, sums in zip(back_places, rest):
        before = before + mine[back_place] * sums[...]
    new_totals[...] = before
    x = rounded_units(arrived[...])
    along_rows = jnp.zeros((rows, LANES), jnp.float32)
    for i in range(count):
        y = units[i * BLOCK : (i + 1) * BLOCK]
        cosines = lax.dot_general(x, y, (((1,), (1,)), ((), ())), preferred_element_type=jnp.float32)
        weights = soft_weights(cosines)
        alive = live[place, i : i + 1]
        parts = [weights[:, part * LANES : (part + 1) * LANES] for part in range(ROWS)]
        along_rows = along_rows + alive * sum(parts)
        for part, piece in enumerate(parts):
            row = i * ROWS + part
            new_totals[row : row + 1] = new_totals[row : row + 1] + alive * jnp.sum(piece, axis=0, keepdims=True)
    empty = [jnp.zeros((gap, LANES), jnp.float32) for gap in (first, BLOCK - first - rows)]
    along_rows = jnp.concatenate([part for part in (empty[0], along_rows, empty[1]) if part.shape[0]], axis=0)
    for part in range(ROWS):
        sums = jnp.sum(along_rows[part * LANES : (part + 1) * LANES].T, axis=0, keepdims=True)
        for i in range(count):
            row = i * ROWS + part
            back[row : row + 1] = sums + rest[-3][row : row + 1] if carries else sums


def work(place, slot, arrived, units, live, mine, totals, returned, carried):
    operands = [arrived, units, live, mine, totals] + [sums for _, sums in returned]
    operands += [] if carried is None else [carried]
    return pl.pallas_call(
        functools.partial(slot_kernel, place, *slot[2:], [one for one, _ in returned], carried is not None),
        out_shape=[jax.ShapeDtypeStruct(totals.shape, jnp.float32)] * 2,
        in_specs=[VMEM] * len(operands),
        out_specs=[VMEM] * 2,
        compiler_params=PARAMS,
    )(*operands)


BEHIND = 2
EARLY_ROWS = 192
HALF = BLOCK // 2


FIRST_CUT = 240


def plan_slots(sizes):
    slots = [("sub", 2, 0, BLOCK), ("blk", 1, 0, BLOCK), ("blk", 2, 0, BLOCK)]
    for k in range(3, sizes["blk"]):
        slots += [("blk", k, 0, FIRST_CUT), ("blk", k, FIRST_CUT, BLOCK - FIRST_CUT)]
    return slots + [("sub", k, 0, BLOCK) for k in (1, *range(3, sizes["sub"]))]


def body(embeds, pick_blk, mask_blk, pick_sub, mask_sub):
    count = embeds.shape[0] // BLOCK
    sizes = {"sub": lax.axis_size("sub"), "blk": lax.axis_size("blk")}
    slots = plan_slots(sizes)

    def send(array, slot):
        return lax.ppermute(array, slot[0], pairs(slot[1], sizes[slot[0]]))

    outgoing = [first_rows(slots[0], pick_sub, embeds), *pick_rows(slots[1:], pick_blk, pick_sub, embeds)]
    arrived = [send(rows, slot) for rows, slot in zip(outgoing, slots)]

    units, live, mine = prepare(slots, pick_blk, pick_sub, mask_blk, mask_sub, embeds)
    totals = jnp.zeros((count * ROWS, LANES), jnp.float32)
    carried = {}
    soon, late = [], []
    for place, slot in enumerate(slots):
        axis, step, first, rows = slot
        done = len(soon) if place == len(slots) - 1 else sum(sent <= place - BEHIND for sent, _ in soon)
        ready, soon = soon[:done], soon[done:]
        totals, back = work(
            place, slot, arrived[place], units, live, mine, totals, ready, carried.pop((axis, step), None)
        )
        if first + rows < BLOCK:
            carried[axis, step] = back
        else:
            (soon if axis == "blk" else late).append((place, send(back, slot)))
    for place, sums in late:
        totals = totals + mine[place] * sums
    return (totals * (1.0 / BLOCK)).reshape(-1)


def solution(mesh):
    return jax.shard_map(
        body,
        mesh=mesh,
        in_specs=(
            P(("groups", "blk", "sub"), None),
            P(("groups", "blk", "sub"), None),
            P(("groups", "blk", "sub"), None),
            P(("groups", "blk"), None),
            P(("groups", "blk", "sub"), None),
        ),
        out_specs=P(("groups", "blk", "sub")),
        check_vma=False,
    )
```

```python
import functools
import math

import jax
import jax.numpy as jnp
from jax import lax
from jax.experimental import pallas as pl
from jax.experimental.pallas import tpu as pltpu
from jax.sharding import PartitionSpec as P

BLOCK = 256
LANES = 128
ROWS = BLOCK // LANES

cutoff = 0.05
sharpness = 100.0

SMEM = pl.BlockSpec(memory_space=pltpu.SMEM)
VMEM = pl.BlockSpec(memory_space=pltpu.VMEM)
HBM = pl.BlockSpec(memory_space=pltpu.HBM)
ANY = pl.BlockSpec(memory_space=pl.ANY)
PARAMS = pltpu.CompilerParams(vmem_limit_bytes=32 * 2**20)


def pairs(step, size):
    return [(i, i ^ step) for i in range(size)]


def rounded_units(rows):
    wide = rows.astype(jnp.float32)
    scale = lax.rsqrt(jnp.sum(wide * wide, axis=1, keepdims=True) + 1e-06)
    return (wide * scale).astype(jnp.bfloat16)


def soft_weights(cosines):
    rate = sharpness * math.log2(math.e)
    return pltpu.reciprocal(1.0 + jnp.exp2(cutoff * rate - cosines * rate), approx=True)


def take_pick(axis, step, pick_blk, pick_sub):
    target = lax.axis_index(axis) ^ step
    return pick_blk[0, target] if axis == "blk" else pick_sub[lax.axis_index("sub"), target]


def first_kernel(slots, pick_blk, pick_sub, embeds, *rest):
    outs, (blk_scalars, sub_scalars, staged, scalar_sems, in_sems, out_sems) = rest[: len(slots)], rest[len(slots) :]
    scalars = [
        pltpu.make_async_copy(pick_blk, blk_scalars, scalar_sems.at[0]),
        pltpu.make_async_copy(pick_sub, sub_scalars, scalar_sems.at[1]),
    ]
    for copy in scalars:
        copy.start()
    for copy in scalars:
        copy.wait()
    entering, leaving = [], []
    for place, (axis, step, first, rows) in enumerate(slots):
        pick = take_pick(axis, step, blk_scalars, sub_scalars)
        for start in range(0, rows, PART):
            source = pl.multiple_of(pick * BLOCK + (first + start), PART)
            here = staged.at[place, pl.ds(start, PART)]
            number = len(entering)
            entering.append(pltpu.make_async_copy(embeds.at[pl.ds(source, PART)], here, in_sems.at[number]))
            leaving.append(pltpu.make_async_copy(here, outs[place].at[pl.ds(start, PART)], out_sems.at[number]))
            entering[-1].start()
    for copy, onward in zip(entering, leaving):
        copy.wait()
        onward.start()
    for onward in leaving:
        onward.wait()


PART = 64


def first_rows(slots, pick_blk, pick_sub, embeds):
    shape = (BLOCK, embeds.shape[1])
    parts = len(slots) * (BLOCK // PART)
    return pl.pallas_call(
        functools.partial(first_kernel, slots),
        out_shape=[jax.ShapeDtypeStruct(shape, embeds.dtype)] * len(slots),
        in_specs=[ANY] * 3,
        out_specs=[ANY] * len(slots),
        scratch_shapes=[
            pltpu.SMEM(pick_blk.shape, jnp.int32),
            pltpu.SMEM(pick_sub.shape, jnp.int32),
            pltpu.VMEM((len(slots), *shape), embeds.dtype),
            pltpu.SemaphoreType.DMA((2,)),
            pltpu.SemaphoreType.DMA((parts,)),
            pltpu.SemaphoreType.DMA((parts,)),
        ],
    )(pick_blk, pick_sub, embeds)


def pick_kernel(slots, pick_blk, pick_sub, embeds, *rest):
    outs, (blk_scalars, sub_scalars, scalar_sems, row_sems) = rest[: len(slots)], rest[len(slots) :]
    scalars = [
        pltpu.make_async_copy(pick_blk, blk_scalars, scalar_sems.at[0]),
        pltpu.make_async_copy(pick_sub, sub_scalars, scalar_sems.at[1]),
    ]
    for copy in scalars:
        copy.start()
    for copy in scalars:
        copy.wait()
    copies = []
    for place, (axis, step, first, rows) in enumerate(slots):
        pick = take_pick(axis, step, blk_scalars, sub_scalars)
        start = pl.multiple_of(pick * BLOCK + first, math.gcd(BLOCK, first))
        copies.append(pltpu.make_async_copy(embeds.at[pl.ds(start, rows)], outs[place], row_sems.at[place]))
        copies[-1].start()
    for copy in copies:
        copy.wait()


def pick_rows(slots, pick_blk, pick_sub, embeds):
    return pl.pallas_call(
        functools.partial(pick_kernel, slots),
        out_shape=[jax.ShapeDtypeStruct((rows, embeds.shape[1]), embeds.dtype) for _, _, _, rows in slots],
        in_specs=[HBM] * 3,
        out_specs=[VMEM] * len(slots),
        scratch_shapes=[
            pltpu.SMEM(pick_blk.shape, jnp.int32),
            pltpu.SMEM(pick_sub.shape, jnp.int32),
            pltpu.SemaphoreType.DMA((2,)),
            pltpu.SemaphoreType.DMA((len(slots),)),
        ],
        compiler_params=PARAMS,
    )(pick_blk, pick_sub, embeds)


def prepare_kernel(slots, pick_blk, pick_sub, mask_blk, mask_sub, embeds, units, live, mine):
    for start in range(0, embeds.shape[0], BLOCK):
        units[start : start + BLOCK] = rounded_units(embeds[start : start + BLOCK])
    count = live.shape[1]
    block_of = lax.broadcasted_iota(jnp.int32, mine.shape[1:], 0) // ROWS
    for place, (axis, step, _, _) in enumerate(slots):
        source = lax.axis_index(axis) ^ step
        mask = mask_blk if axis == "blk" else mask_sub
        for i in range(count):
            value = mask[0, source * count + i].astype(jnp.float32)
            live[place, i : i + 1] = jnp.full((1, LANES), value, jnp.float32)
        pick = take_pick(axis, step, pick_blk, pick_sub)
        mine[place] = (block_of == pick).astype(jnp.float32)


def prepare(slots, pick_blk, pick_sub, mask_blk, mask_sub, embeds):
    count = embeds.shape[0] // BLOCK
    return pl.pallas_call(
        functools.partial(prepare_kernel, slots),
        out_shape=[
            jax.ShapeDtypeStruct(embeds.shape, embeds.dtype),
            jax.ShapeDtypeStruct((len(slots), count, LANES), jnp.float32),
            jax.ShapeDtypeStruct((len(slots), count * ROWS, LANES), jnp.float32),
        ],
        in_specs=[SMEM] * 4 + [VMEM],
        out_specs=[VMEM] * 3,
        compiler_params=PARAMS,
    )(pick_blk, pick_sub, mask_blk, mask_sub, embeds)


def slot_kernel(place, first, rows, back_places, carries, arrived, units, live, mine, totals, *rest):
    new_totals, back = rest[-2:]
    count = live.shape[1]
    before = totals[...]
    for back_place, sums in zip(back_places, rest):
        before = before + mine[back_place] * sums[...]
    new_totals[...] = before
    x = rounded_units(arrived[...])
    along_rows = jnp.zeros((rows, LANES), jnp.float32)
    for i in range(count):
        y = units[i * BLOCK : (i + 1) * BLOCK]
        cosines = lax.dot_general(x, y, (((1,), (1,)), ((), ())), preferred_element_type=jnp.float32)
        weights = soft_weights(cosines)
        alive = live[place, i : i + 1]
        parts = [weights[:, part * LANES : (part + 1) * LANES] for part in range(ROWS)]
        along_rows = along_rows + alive * sum(parts)
        for part, piece in enumerate(parts):
            row = i * ROWS + part
            new_totals[row : row + 1] = new_totals[row : row + 1] + alive * jnp.sum(piece, axis=0, keepdims=True)
    empty = [jnp.zeros((gap, LANES), jnp.float32) for gap in (first, BLOCK - first - rows)]
    along_rows = jnp.concatenate([part for part in (empty[0], along_rows, empty[1]) if part.shape[0]], axis=0)
    for part in range(ROWS):
        sums = jnp.sum(along_rows[part * LANES : (part + 1) * LANES].T, axis=0, keepdims=True)
        for i in range(count):
            row = i * ROWS + part
            back[row : row + 1] = sums + rest[-3][row : row + 1] if carries else sums


def work(place, slot, arrived, units, live, mine, totals, returned, carried):
    operands = [arrived, units, live, mine, totals] + [sums for _, sums in returned]
    operands += [] if carried is None else [carried]
    return pl.pallas_call(
        functools.partial(slot_kernel, place, *slot[2:], [one for one, _ in returned], carried is not None),
        out_shape=[jax.ShapeDtypeStruct(totals.shape, jnp.float32)] * 2,
        in_specs=[VMEM] * len(operands),
        out_specs=[VMEM] * 2,
        compiler_params=PARAMS,
    )(*operands)


BEHIND = 2
EARLY_ROWS = 192
HALF = BLOCK // 2


FIRST_CUT = 240


def plan_slots(sizes):
    slots = [("blk", 1, 0, BLOCK), ("sub", 2, 0, BLOCK), ("blk", 2, 0, BLOCK)]
    for k in range(3, sizes["blk"]):
        slots += [("blk", k, 0, FIRST_CUT), ("blk", k, FIRST_CUT, BLOCK - FIRST_CUT)]
    return slots + [("sub", k, 0, BLOCK) for k in (1, *range(3, sizes["sub"]))]


AT_ONCE = 2


def body(embeds, pick_blk, mask_blk, pick_sub, mask_sub):
    count = embeds.shape[0] // BLOCK
    sizes = {"sub": lax.axis_size("sub"), "blk": lax.axis_size("blk")}
    slots = plan_slots(sizes)

    def send(array, slot):
        return lax.ppermute(array, slot[0], pairs(slot[1], sizes[slot[0]]))

    outgoing = first_rows(slots[:AT_ONCE], pick_blk, pick_sub, embeds)
    outgoing += pick_rows(slots[AT_ONCE:], pick_blk, pick_sub, embeds)
    arrived = [send(rows, slot) for rows, slot in zip(outgoing, slots)]

    units, live, mine = prepare(slots, pick_blk, pick_sub, mask_blk, mask_sub, embeds)
    totals = jnp.zeros((count * ROWS, LANES), jnp.float32)
    carried = {}
    soon, late = [], []
    for place, slot in enumerate(slots):
        axis, step, first, rows = slot
        done = len(soon) if place == len(slots) - 1 else sum(sent <= place - BEHIND for sent, _ in soon)
        ready, soon = soon[:done], soon[done:]
        totals, back = work(
            place, slot, arrived[place], units, live, mine, totals, ready, carried.pop((axis, step), None)
        )
        if first + rows < BLOCK:
            carried[axis, step] = back
        else:
            (soon if axis == "blk" else late).append((place, send(back, slot)))
    for place, sums in late:
        totals = totals + mine[place] * sums
    return (totals * (1.0 / BLOCK)).reshape(-1)


def solution(mesh):
    return jax.shard_map(
        body,
        mesh=mesh,
        in_specs=(
            P(("groups", "blk", "sub"), None),
            P(("groups", "blk", "sub"), None),
            P(("groups", "blk", "sub"), None),
            P(("groups", "blk"), None),
            P(("groups", "blk", "sub"), None),
        ),
        out_specs=P(("groups", "blk", "sub")),
        check_vma=False,
    )
```

```python
import functools
import math

import jax
import jax.numpy as jnp
from jax import lax
from jax.experimental import pallas as pl
from jax.experimental.pallas import tpu as pltpu
from jax.sharding import PartitionSpec as P

BLOCK = 256
LANES = 128
ROWS = BLOCK // LANES

cutoff = 0.05
sharpness = 100.0

SMEM = pl.BlockSpec(memory_space=pltpu.SMEM)
VMEM = pl.BlockSpec(memory_space=pltpu.VMEM)
HBM = pl.BlockSpec(memory_space=pltpu.HBM)
ANY = pl.BlockSpec(memory_space=pl.ANY)
PARAMS = pltpu.CompilerParams(vmem_limit_bytes=32 * 2**20)


def pairs(step, size):
    return [(i, i ^ step) for i in range(size)]


def rounded_units(rows):
    wide = rows.astype(jnp.float32)
    scale = lax.rsqrt(jnp.sum(wide * wide, axis=1, keepdims=True) + 1e-06)
    return (wide * scale).astype(jnp.bfloat16)


def soft_weights(cosines):
    rate = sharpness * math.log2(math.e)
    return pltpu.reciprocal(1.0 + jnp.exp2(cutoff * rate - cosines * rate), approx=True)


def take_pick(axis, step, pick_blk, pick_sub):
    target = lax.axis_index(axis) ^ step
    return pick_blk[0, target] if axis == "blk" else pick_sub[lax.axis_index("sub"), target]


def first_kernel(slots, pick_blk, pick_sub, embeds, *rest):
    outs, (blk_scalars, sub_scalars, staged, scalar_sems, in_sems, out_sems) = rest[: len(slots)], rest[len(slots) :]
    scalars = [
        pltpu.make_async_copy(pick_blk, blk_scalars, scalar_sems.at[0]),
        pltpu.make_async_copy(pick_sub, sub_scalars, scalar_sems.at[1]),
    ]
    for copy in scalars:
        copy.start()
    for copy in scalars:
        copy.wait()
    entering, leaving = [], []
    for place, (axis, step, first, rows) in enumerate(slots):
        pick = take_pick(axis, step, blk_scalars, sub_scalars)
        for start in range(0, rows, PART):
            source = pl.multiple_of(pick * BLOCK + (first + start), PART)
            here = staged.at[place, pl.ds(start, PART)]
            number = len(entering)
            entering.append(pltpu.make_async_copy(embeds.at[pl.ds(source, PART)], here, in_sems.at[number]))
            leaving.append(pltpu.make_async_copy(here, outs[place].at[pl.ds(start, PART)], out_sems.at[number]))
            entering[-1].start()
    for copy, onward in zip(entering, leaving):
        copy.wait()
        onward.start()
    for onward in leaving:
        onward.wait()


PART = 64


def first_rows(slots, pick_blk, pick_sub, embeds):
    shape = (BLOCK, embeds.shape[1])
    parts = len(slots) * (BLOCK // PART)
    return pl.pallas_call(
        functools.partial(first_kernel, slots),
        out_shape=[jax.ShapeDtypeStruct(shape, embeds.dtype)] * len(slots),
        in_specs=[ANY] * 3,
        out_specs=[ANY] * len(slots),
        scratch_shapes=[
            pltpu.SMEM(pick_blk.shape, jnp.int32),
            pltpu.SMEM(pick_sub.shape, jnp.int32),
            pltpu.VMEM((len(slots), *shape), embeds.dtype),
            pltpu.SemaphoreType.DMA((2,)),
            pltpu.SemaphoreType.DMA((parts,)),
            pltpu.SemaphoreType.DMA((parts,)),
        ],
    )(pick_blk, pick_sub, embeds)


def pick_kernel(slots, pick_blk, pick_sub, embeds, *rest):
    outs, (blk_scalars, sub_scalars, scalar_sems, row_sems) = rest[: len(slots)], rest[len(slots) :]
    scalars = [
        pltpu.make_async_copy(pick_blk, blk_scalars, scalar_sems.at[0]),
        pltpu.make_async_copy(pick_sub, sub_scalars, scalar_sems.at[1]),
    ]
    for copy in scalars:
        copy.start()
    for copy in scalars:
        copy.wait()
    copies = []
    for place, (axis, step, first, rows) in enumerate(slots):
        pick = take_pick(axis, step, blk_scalars, sub_scalars)
        start = pl.multiple_of(pick * BLOCK + first, math.gcd(BLOCK, first))
        copies.append(pltpu.make_async_copy(embeds.at[pl.ds(start, rows)], outs[place], row_sems.at[place]))
        copies[-1].start()
    for copy in copies:
        copy.wait()


def pick_rows(slots, pick_blk, pick_sub, embeds):
    return pl.pallas_call(
        functools.partial(pick_kernel, slots),
        out_shape=[jax.ShapeDtypeStruct((rows, embeds.shape[1]), embeds.dtype) for _, _, _, rows in slots],
        in_specs=[HBM] * 3,
        out_specs=[VMEM] * len(slots),
        scratch_shapes=[
            pltpu.SMEM(pick_blk.shape, jnp.int32),
            pltpu.SMEM(pick_sub.shape, jnp.int32),
            pltpu.SemaphoreType.DMA((2,)),
            pltpu.SemaphoreType.DMA((len(slots),)),
        ],
        compiler_params=PARAMS,
    )(pick_blk, pick_sub, embeds)


def prepare_kernel(slots, pick_blk, pick_sub, mask_blk, mask_sub, embeds, units, live, mine):
    for start in range(0, embeds.shape[0], BLOCK):
        units[start : start + BLOCK] = rounded_units(embeds[start : start + BLOCK])
    count = live.shape[1]
    block_of = lax.broadcasted_iota(jnp.int32, mine.shape[1:], 0) // ROWS
    for place, (axis, step, _, _) in enumerate(slots):
        source = lax.axis_index(axis) ^ step
        mask = mask_blk if axis == "blk" else mask_sub
        for i in range(count):
            value = mask[0, source * count + i].astype(jnp.float32)
            live[place, i : i + 1] = jnp.full((1, LANES), value, jnp.float32)
        pick = take_pick(axis, step, pick_blk, pick_sub)
        mine[place] = (block_of == pick).astype(jnp.float32)


def prepare(slots, pick_blk, pick_sub, mask_blk, mask_sub, embeds):
    count = embeds.shape[0] // BLOCK
    return pl.pallas_call(
        functools.partial(prepare_kernel, slots),
        out_shape=[
            jax.ShapeDtypeStruct(embeds.shape, embeds.dtype),
            jax.ShapeDtypeStruct((len(slots), count, LANES), jnp.float32),
            jax.ShapeDtypeStruct((len(slots), count * ROWS, LANES), jnp.float32),
        ],
        in_specs=[SMEM] * 4 + [VMEM],
        out_specs=[VMEM] * 3,
        compiler_params=PARAMS,
    )(pick_blk, pick_sub, mask_blk, mask_sub, embeds)


def slot_kernel(place, first, rows, back_places, carries, arrived, units, live, mine, totals, *rest):
    new_totals, back = rest[-2:]
    count = live.shape[1]
    before = totals[...]
    for back_place, sums in zip(back_places, rest):
        before = before + mine[back_place] * sums[...]
    new_totals[...] = before
    x = rounded_units(arrived[...])
    along_rows = jnp.zeros((rows, LANES), jnp.float32)
    for i in range(count):
        y = units[i * BLOCK : (i + 1) * BLOCK]
        cosines = lax.dot_general(x, y, (((1,), (1,)), ((), ())), preferred_element_type=jnp.float32)
        weights = soft_weights(cosines)
        alive = live[place, i : i + 1]
        parts = [weights[:, part * LANES : (part + 1) * LANES] for part in range(ROWS)]
        along_rows = along_rows + alive * sum(parts)
        for part, piece in enumerate(parts):
            row = i * ROWS + part
            new_totals[row : row + 1] = new_totals[row : row + 1] + alive * jnp.sum(piece, axis=0, keepdims=True)
    empty = [jnp.zeros((gap, LANES), jnp.float32) for gap in (first, BLOCK - first - rows)]
    along_rows = jnp.concatenate([part for part in (empty[0], along_rows, empty[1]) if part.shape[0]], axis=0)
    for part in range(ROWS):
        sums = jnp.sum(along_rows[part * LANES : (part + 1) * LANES].T, axis=0, keepdims=True)
        for i in range(count):
            row = i * ROWS + part
            back[row : row + 1] = sums + rest[-3][row : row + 1] if carries else sums


def work(place, slot, arrived, units, live, mine, totals, returned, carried):
    operands = [arrived, units, live, mine, totals] + [sums for _, sums in returned]
    operands += [] if carried is None else [carried]
    return pl.pallas_call(
        functools.partial(slot_kernel, place, *slot[2:], [one for one, _ in returned], carried is not None),
        out_shape=[jax.ShapeDtypeStruct(totals.shape, jnp.float32)] * 2,
        in_specs=[VMEM] * len(operands),
        out_specs=[VMEM] * 2,
        compiler_params=PARAMS,
    )(*operands)


BEHIND = 2
EARLY_ROWS = 192
HALF = BLOCK // 2


FIRST_CUT = 128


def plan_slots(sizes):
    slots = [("blk", 1, 0, BLOCK), ("sub", 2, 0, BLOCK), ("sub", 1, 0, BLOCK)]
    slots += [("blk", k, 0, BLOCK) for k in range(2, sizes["blk"])]
    for k in range(3, sizes["sub"]):
        slots += [("sub", k, 0, FIRST_CUT), ("sub", k, FIRST_CUT, BLOCK - FIRST_CUT)]
    return slots


AT_ONCE = 2


def body(embeds, pick_blk, mask_blk, pick_sub, mask_sub):
    count = embeds.shape[0] // BLOCK
    sizes = {"sub": lax.axis_size("sub"), "blk": lax.axis_size("blk")}
    slots = plan_slots(sizes)

    def send(array, slot):
        return lax.ppermute(array, slot[0], pairs(slot[1], sizes[slot[0]]))

    outgoing = first_rows(slots[:AT_ONCE], pick_blk, pick_sub, embeds)
    outgoing += pick_rows(slots[AT_ONCE:], pick_blk, pick_sub, embeds)
    arrived = [send(rows, slot) for rows, slot in zip(outgoing, slots)]

    units, live, mine = prepare(slots, pick_blk, pick_sub, mask_blk, mask_sub, embeds)
    totals = jnp.zeros((count * ROWS, LANES), jnp.float32)
    carried = {}
    soon, late = [], []
    for place, slot in enumerate(slots):
        axis, step, first, rows = slot
        done = len(soon) if place == len(slots) - 1 else sum(sent <= place - BEHIND for sent, _ in soon)
        ready, soon = soon[:done], soon[done:]
        totals, back = work(
            place, slot, arrived[place], units, live, mine, totals, ready, carried.pop((axis, step), None)
        )
        if first + rows < BLOCK:
            carried[axis, step] = back
        else:
            (soon if axis == "blk" else late).append((place, send(back, slot)))
    for place, sums in late:
        totals = totals + mine[place] * sums
    return (totals * (1.0 / BLOCK)).reshape(-1)


def solution(mesh):
    return jax.shard_map(
        body,
        mesh=mesh,
        in_specs=(
            P(("groups", "blk", "sub"), None),
            P(("groups", "blk", "sub"), None),
            P(("groups", "blk", "sub"), None),
            P(("groups", "blk"), None),
            P(("groups", "blk", "sub"), None),
        ),
        out_specs=P(("groups", "blk", "sub")),
        check_vma=False,
    )
```

```python
import functools
import math

import jax
import jax.numpy as jnp
from jax import lax
from jax.experimental import pallas as pl
from jax.experimental.pallas import tpu as pltpu
from jax.sharding import PartitionSpec as P

BLOCK = 256
LANES = 128
ROWS = BLOCK // LANES

cutoff = 0.05
sharpness = 100.0

SMEM = pl.BlockSpec(memory_space=pltpu.SMEM)
VMEM = pl.BlockSpec(memory_space=pltpu.VMEM)
HBM = pl.BlockSpec(memory_space=pltpu.HBM)
ANY = pl.BlockSpec(memory_space=pl.ANY)
PARAMS = pltpu.CompilerParams(vmem_limit_bytes=32 * 2**20)


def pairs(step, size):
    return [(i, i ^ step) for i in range(size)]


def rounded_units(rows):
    wide = rows.astype(jnp.float32)
    scale = lax.rsqrt(jnp.sum(wide * wide, axis=1, keepdims=True) + 1e-06)
    return (wide * scale).astype(jnp.bfloat16)


def soft_weights(cosines):
    rate = sharpness * math.log2(math.e)
    return pltpu.reciprocal(1.0 + jnp.exp2(cutoff * rate - cosines * rate), approx=True)


def take_pick(axis, step, pick_blk, pick_sub):
    target = lax.axis_index(axis) ^ step
    return pick_blk[0, target] if axis == "blk" else pick_sub[lax.axis_index("sub"), target]


def first_kernel(slots, pick_blk, pick_sub, embeds, *rest):
    outs, (blk_scalars, sub_scalars, staged, scalar_sems, in_sems, out_sems) = rest[: len(slots)], rest[len(slots) :]
    scalars = [
        pltpu.make_async_copy(pick_blk, blk_scalars, scalar_sems.at[0]),
        pltpu.make_async_copy(pick_sub, sub_scalars, scalar_sems.at[1]),
    ]
    for copy in scalars:
        copy.start()
    for copy in scalars:
        copy.wait()
    entering, leaving = [], []
    for place, (axis, step, first, rows) in enumerate(slots):
        pick = take_pick(axis, step, blk_scalars, sub_scalars)
        for start in range(0, rows, PART):
            source = pl.multiple_of(pick * BLOCK + (first + start), PART)
            here = staged.at[place, pl.ds(start, PART)]
            number = len(entering)
            entering.append(pltpu.make_async_copy(embeds.at[pl.ds(source, PART)], here, in_sems.at[number]))
            leaving.append(pltpu.make_async_copy(here, outs[place].at[pl.ds(start, PART)], out_sems.at[number]))
            entering[-1].start()
    for copy, onward in zip(entering, leaving):
        copy.wait()
        onward.start()
    for onward in leaving:
        onward.wait()


PART = 64


def first_rows(slots, pick_blk, pick_sub, embeds):
    shape = (BLOCK, embeds.shape[1])
    parts = len(slots) * (BLOCK // PART)
    return pl.pallas_call(
        functools.partial(first_kernel, slots),
        out_shape=[jax.ShapeDtypeStruct(shape, embeds.dtype)] * len(slots),
        in_specs=[ANY] * 3,
        out_specs=[ANY] * len(slots),
        scratch_shapes=[
            pltpu.SMEM(pick_blk.shape, jnp.int32),
            pltpu.SMEM(pick_sub.shape, jnp.int32),
            pltpu.VMEM((len(slots), *shape), embeds.dtype),
            pltpu.SemaphoreType.DMA((2,)),
            pltpu.SemaphoreType.DMA((parts,)),
            pltpu.SemaphoreType.DMA((parts,)),
        ],
    )(pick_blk, pick_sub, embeds)


def pick_kernel(slots, pick_blk, pick_sub, embeds, *rest):
    outs, (blk_scalars, sub_scalars, scalar_sems, row_sems) = rest[: len(slots)], rest[len(slots) :]
    scalars = [
        pltpu.make_async_copy(pick_blk, blk_scalars, scalar_sems.at[0]),
        pltpu.make_async_copy(pick_sub, sub_scalars, scalar_sems.at[1]),
    ]
    for copy in scalars:
        copy.start()
    for copy in scalars:
        copy.wait()
    copies = []
    for place, (axis, step, first, rows) in enumerate(slots):
        pick = take_pick(axis, step, blk_scalars, sub_scalars)
        start = pl.multiple_of(pick * BLOCK + first, math.gcd(BLOCK, first))
        copies.append(pltpu.make_async_copy(embeds.at[pl.ds(start, rows)], outs[place], row_sems.at[place]))
        copies[-1].start()
    for copy in copies:
        copy.wait()


def pick_rows(slots, pick_blk, pick_sub, embeds):
    return pl.pallas_call(
        functools.partial(pick_kernel, slots),
        out_shape=[jax.ShapeDtypeStruct((rows, embeds.shape[1]), embeds.dtype) for _, _, _, rows in slots],
        in_specs=[HBM] * 3,
        out_specs=[VMEM] * len(slots),
        scratch_shapes=[
            pltpu.SMEM(pick_blk.shape, jnp.int32),
            pltpu.SMEM(pick_sub.shape, jnp.int32),
            pltpu.SemaphoreType.DMA((2,)),
            pltpu.SemaphoreType.DMA((len(slots),)),
        ],
        compiler_params=PARAMS,
    )(pick_blk, pick_sub, embeds)


def prepare_kernel(slots, pick_blk, pick_sub, mask_blk, mask_sub, embeds, units, live, mine):
    for start in range(0, embeds.shape[0], BLOCK):
        units[:, start : start + BLOCK] = rounded_units(embeds[start : start + BLOCK]).T
    count = live.shape[1]
    block_of = lax.broadcasted_iota(jnp.int32, mine.shape[1:], 0) // ROWS
    for place, (axis, step, _, _) in enumerate(slots):
        source = lax.axis_index(axis) ^ step
        mask = mask_blk if axis == "blk" else mask_sub
        for i in range(count):
            value = mask[0, source * count + i].astype(jnp.float32)
            live[place, i : i + 1] = jnp.full((1, LANES), value, jnp.float32)
        pick = take_pick(axis, step, pick_blk, pick_sub)
        mine[place] = (block_of == pick).astype(jnp.float32)


def prepare(slots, pick_blk, pick_sub, mask_blk, mask_sub, embeds):
    count = embeds.shape[0] // BLOCK
    return pl.pallas_call(
        functools.partial(prepare_kernel, slots),
        out_shape=[
            jax.ShapeDtypeStruct(embeds.shape[::-1], embeds.dtype),
            jax.ShapeDtypeStruct((len(slots), count, LANES), jnp.float32),
            jax.ShapeDtypeStruct((len(slots), count * ROWS, LANES), jnp.float32),
        ],
        in_specs=[SMEM] * 4 + [VMEM],
        out_specs=[VMEM] * 3,
        compiler_params=PARAMS,
    )(pick_blk, pick_sub, mask_blk, mask_sub, embeds)


def slot_kernel(place, first, rows, back_places, carries, arrived, units, live, mine, totals, *rest):
    new_totals, back = rest[-2:]
    count = live.shape[1]
    before = totals[...]
    for back_place, sums in zip(back_places, rest):
        before = before + mine[back_place] * sums[...]
    new_totals[...] = before
    x = rounded_units(arrived[...])
    along_rows = jnp.zeros((rows, LANES), jnp.float32)
    for i in range(count):
        cosines = jnp.dot(x, units[:, i * BLOCK : (i + 1) * BLOCK], preferred_element_type=jnp.float32)
        weights = soft_weights(cosines)
        alive = live[place, i : i + 1]
        parts = [weights[:, part * LANES : (part + 1) * LANES] for part in range(ROWS)]
        along_rows = along_rows + alive * sum(parts)
        for part, piece in enumerate(parts):
            row = i * ROWS + part
            new_totals[row : row + 1] = new_totals[row : row + 1] + alive * jnp.sum(piece, axis=0, keepdims=True)
    empty = [jnp.zeros((gap, LANES), jnp.float32) for gap in (first, BLOCK - first - rows)]
    along_rows = jnp.concatenate([part for part in (empty[0], along_rows, empty[1]) if part.shape[0]], axis=0)
    for part in range(ROWS):
        sums = jnp.sum(along_rows[part * LANES : (part + 1) * LANES].T, axis=0, keepdims=True)
        for i in range(count):
            row = i * ROWS + part
            back[row : row + 1] = sums + rest[-3][row : row + 1] if carries else sums


def work(place, slot, arrived, units, live, mine, totals, returned, carried):
    operands = [arrived, units, live, mine, totals] + [sums for _, sums in returned]
    operands += [] if carried is None else [carried]
    return pl.pallas_call(
        functools.partial(slot_kernel, place, *slot[2:], [one for one, _ in returned], carried is not None),
        out_shape=[jax.ShapeDtypeStruct(totals.shape, jnp.float32)] * 2,
        in_specs=[VMEM] * len(operands),
        out_specs=[VMEM] * 2,
        compiler_params=PARAMS,
    )(*operands)


BEHIND = 2
EARLY_ROWS = 192
HALF = BLOCK // 2


FIRST_CUT = 240


def plan_slots(sizes):
    slots = [("sub", 2, 0, BLOCK), ("blk", 1, 0, BLOCK), ("blk", 2, 0, BLOCK)]
    for k in range(3, sizes["blk"]):
        slots += [("blk", k, 0, FIRST_CUT), ("blk", k, FIRST_CUT, BLOCK - FIRST_CUT)]
    return slots + [("sub", k, 0, BLOCK) for k in (*range(3, sizes["sub"]), 1)]


AT_ONCE = 1


def body(embeds, pick_blk, mask_blk, pick_sub, mask_sub):
    count = embeds.shape[0] // BLOCK
    sizes = {"sub": lax.axis_size("sub"), "blk": lax.axis_size("blk")}
    slots = plan_slots(sizes)

    def send(array, slot):
        return lax.ppermute(array, slot[0], pairs(slot[1], sizes[slot[0]]))

    outgoing = first_rows(slots[:AT_ONCE], pick_blk, pick_sub, embeds)
    outgoing += pick_rows(slots[AT_ONCE:], pick_blk, pick_sub, embeds)
    arrived = [send(rows, slot) for rows, slot in zip(outgoing, slots)]

    units, live, mine = prepare(slots, pick_blk, pick_sub, mask_blk, mask_sub, embeds)
    totals = jnp.zeros((count * ROWS, LANES), jnp.float32)
    carried = {}
    soon, late = [], []
    for place, slot in enumerate(slots):
        axis, step, first, rows = slot
        done = len(soon) if place == len(slots) - 1 else sum(sent <= place - BEHIND for sent, _ in soon)
        ready, soon = soon[:done], soon[done:]
        totals, back = work(
            place, slot, arrived[place], units, live, mine, totals, ready, carried.pop((axis, step), None)
        )
        if first + rows < BLOCK:
            carried[axis, step] = back
        else:
            (soon if axis == "blk" else late).append((place, send(back, slot)))
    for place, sums in late:
        totals = totals + mine[place] * sums
    return (totals * (1.0 / BLOCK)).reshape(-1)


def solution(mesh):
    return jax.shard_map(
        body,
        mesh=mesh,
        in_specs=(
            P(("groups", "blk", "sub"), None),
            P(("groups", "blk", "sub"), None),
            P(("groups", "blk", "sub"), None),
            P(("groups", "blk"), None),
            P(("groups", "blk", "sub"), None),
        ),
        out_specs=P(("groups", "blk", "sub")),
        check_vma=False,
    )
```

```python
import functools
import math

import jax
import jax.numpy as jnp
from jax import lax
from jax.experimental import pallas as pl
from jax.experimental.pallas import tpu as pltpu
from jax.sharding import PartitionSpec as P

BLOCK = 256
LANES = 128
ROWS = BLOCK // LANES

cutoff = 0.05
sharpness = 100.0

SMEM = pl.BlockSpec(memory_space=pltpu.SMEM)
VMEM = pl.BlockSpec(memory_space=pltpu.VMEM)
HBM = pl.BlockSpec(memory_space=pltpu.HBM)
ANY = pl.BlockSpec(memory_space=pl.ANY)
PARAMS = pltpu.CompilerParams(vmem_limit_bytes=32 * 2**20)


def pairs(step, size):
    return [(i, i ^ step) for i in range(size)]


def rounded_units(rows):
    wide = rows.astype(jnp.float32)
    scale = lax.rsqrt(jnp.sum(wide * wide, axis=1, keepdims=True) + 1e-06)
    return (wide * scale).astype(jnp.bfloat16)


def soft_weights(cosines):
    rate = sharpness * math.log2(math.e)
    return pltpu.reciprocal(1.0 + jnp.exp2(cutoff * rate - cosines * rate), approx=True)


def take_pick(axis, step, pick_blk, pick_sub):
    target = lax.axis_index(axis) ^ step
    return pick_blk[0, target] if axis == "blk" else pick_sub[lax.axis_index("sub"), target]


def first_kernel(slots, pick_blk, pick_sub, embeds, *rest):
    outs, (blk_scalars, sub_scalars, staged, scalar_sems, in_sems, out_sems) = rest[: len(slots)], rest[len(slots) :]
    scalars = [
        pltpu.make_async_copy(pick_blk, blk_scalars, scalar_sems.at[0]),
        pltpu.make_async_copy(pick_sub, sub_scalars, scalar_sems.at[1]),
    ]
    for copy in scalars:
        copy.start()
    starts = range(0, BLOCK, PART)
    entering = []
    for start in starts:
        for top in range(start, embeds.shape[0], BLOCK):
            rows = pl.ds(top, PART)
            entering.append(pltpu.make_async_copy(embeds.at[rows], staged.at[rows], in_sems.at[len(entering)]))
            entering[-1].start()
    for copy in scalars:
        copy.wait()
    picks = [take_pick(axis, step, blk_scalars, sub_scalars) for axis, step, _, _ in slots]
    count = embeds.shape[0] // BLOCK
    leaving = []
    for turn, start in enumerate(starts):
        for copy in entering[turn * count : (turn + 1) * count]:
            copy.wait()
        for pick, out in zip(picks, outs):
            here = staged.at[pl.ds(pl.multiple_of(pick * BLOCK + start, PART), PART)]
            leaving.append(pltpu.make_async_copy(here, out.at[pl.ds(start, PART)], out_sems.at[len(leaving)]))
            leaving[-1].start()
    for copy in leaving:
        copy.wait()


PART = 64


def first_rows(slots, pick_blk, pick_sub, embeds):
    parts = BLOCK // PART
    return pl.pallas_call(
        functools.partial(first_kernel, slots),
        out_shape=[jax.ShapeDtypeStruct((BLOCK, embeds.shape[1]), embeds.dtype)] * len(slots),
        in_specs=[ANY] * 3,
        out_specs=[ANY] * len(slots),
        scratch_shapes=[
            pltpu.SMEM(pick_blk.shape, jnp.int32),
            pltpu.SMEM(pick_sub.shape, jnp.int32),
            pltpu.VMEM(embeds.shape, embeds.dtype),
            pltpu.SemaphoreType.DMA((2,)),
            pltpu.SemaphoreType.DMA((embeds.shape[0] // PART,)),
            pltpu.SemaphoreType.DMA((len(slots) * parts,)),
        ],
    )(pick_blk, pick_sub, embeds)


def pick_kernel(slots, pick_blk, pick_sub, embeds, *rest):
    outs, (blk_scalars, sub_scalars, scalar_sems, row_sems) = rest[: len(slots)], rest[len(slots) :]
    scalars = [
        pltpu.make_async_copy(pick_blk, blk_scalars, scalar_sems.at[0]),
        pltpu.make_async_copy(pick_sub, sub_scalars, scalar_sems.at[1]),
    ]
    for copy in scalars:
        copy.start()
    for copy in scalars:
        copy.wait()
    copies = []
    for place, (axis, step, first, rows) in enumerate(slots):
        pick = take_pick(axis, step, blk_scalars, sub_scalars)
        start = pl.multiple_of(pick * BLOCK + first, math.gcd(BLOCK, first))
        copies.append(pltpu.make_async_copy(embeds.at[pl.ds(start, rows)], outs[place], row_sems.at[place]))
        copies[-1].start()
    for copy in copies:
        copy.wait()


def pick_rows(slots, pick_blk, pick_sub, embeds):
    return pl.pallas_call(
        functools.partial(pick_kernel, slots),
        out_shape=[jax.ShapeDtypeStruct((rows, embeds.shape[1]), embeds.dtype) for _, _, _, rows in slots],
        in_specs=[HBM] * 3,
        out_specs=[VMEM] * len(slots),
        scratch_shapes=[
            pltpu.SMEM(pick_blk.shape, jnp.int32),
            pltpu.SMEM(pick_sub.shape, jnp.int32),
            pltpu.SemaphoreType.DMA((2,)),
            pltpu.SemaphoreType.DMA((len(slots),)),
        ],
        compiler_params=PARAMS,
    )(pick_blk, pick_sub, embeds)


def prepare_kernel(slots, pick_blk, pick_sub, mask_blk, mask_sub, embeds, units, live, mine):
    for start in range(0, embeds.shape[0], BLOCK):
        units[:, start : start + BLOCK] = rounded_units(embeds[start : start + BLOCK]).T
    count = live.shape[1]
    block_of = lax.broadcasted_iota(jnp.int32, mine.shape[1:], 0) // ROWS
    for place, (axis, step, _, _) in enumerate(slots):
        source = lax.axis_index(axis) ^ step
        mask = mask_blk if axis == "blk" else mask_sub
        for i in range(count):
            value = mask[0, source * count + i].astype(jnp.float32)
            live[place, i : i + 1] = jnp.full((1, LANES), value, jnp.float32)
        pick = take_pick(axis, step, pick_blk, pick_sub)
        mine[place] = (block_of == pick).astype(jnp.float32)


def prepare(slots, pick_blk, pick_sub, mask_blk, mask_sub, embeds):
    count = embeds.shape[0] // BLOCK
    return pl.pallas_call(
        functools.partial(prepare_kernel, slots),
        out_shape=[
            jax.ShapeDtypeStruct(embeds.shape[::-1], embeds.dtype),
            jax.ShapeDtypeStruct((len(slots), count, LANES), jnp.float32),
            jax.ShapeDtypeStruct((len(slots), count * ROWS, LANES), jnp.float32),
        ],
        in_specs=[SMEM] * 4 + [VMEM],
        out_specs=[VMEM] * 3,
        compiler_params=PARAMS,
    )(pick_blk, pick_sub, mask_blk, mask_sub, embeds)


def slot_kernel(place, first, rows, back_places, carries, arrived, units, live, mine, totals, *rest):
    new_totals, back = rest[-2:]
    count = live.shape[1]
    before = totals[...]
    for back_place, sums in zip(back_places, rest):
        before = before + mine[back_place] * sums[...]
    new_totals[...] = before
    x = rounded_units(arrived[...])
    along_rows = jnp.zeros((rows, LANES), jnp.float32)
    for i in range(count):
        cosines = jnp.dot(x, units[:, i * BLOCK : (i + 1) * BLOCK], preferred_element_type=jnp.float32)
        weights = soft_weights(cosines)
        alive = live[place, i : i + 1]
        parts = [weights[:, part * LANES : (part + 1) * LANES] for part in range(ROWS)]
        along_rows = along_rows + alive * sum(parts)
        for part, piece in enumerate(parts):
            row = i * ROWS + part
            new_totals[row : row + 1] = new_totals[row : row + 1] + alive * jnp.sum(piece, axis=0, keepdims=True)
    empty = [jnp.zeros((gap, LANES), jnp.float32) for gap in (first, BLOCK - first - rows)]
    along_rows = jnp.concatenate([part for part in (empty[0], along_rows, empty[1]) if part.shape[0]], axis=0)
    for part in range(ROWS):
        sums = jnp.sum(along_rows[part * LANES : (part + 1) * LANES].T, axis=0, keepdims=True)
        for i in range(count):
            row = i * ROWS + part
            back[row : row + 1] = sums + rest[-3][row : row + 1] if carries else sums


def work(place, slot, arrived, units, live, mine, totals, returned, carried):
    operands = [arrived, units, live, mine, totals] + [sums for _, sums in returned]
    operands += [] if carried is None else [carried]
    return pl.pallas_call(
        functools.partial(slot_kernel, place, *slot[2:], [one for one, _ in returned], carried is not None),
        out_shape=[jax.ShapeDtypeStruct(totals.shape, jnp.float32)] * 2,
        in_specs=[VMEM] * len(operands),
        out_specs=[VMEM] * 2,
        compiler_params=PARAMS,
    )(*operands)


BEHIND = 2
EARLY_ROWS = 192
HALF = BLOCK // 2


FIRST_CUT = 240


FIRST_CUT = 240


def plan_slots(sizes):
    slots = [("blk", 1, 0, BLOCK), ("sub", 2, 0, BLOCK)]
    slots += [("blk", k, 0, BLOCK) for k in range(2, sizes["blk"])]
    for k in (1, *range(3, sizes["sub"])):
        slots += [("sub", k, 0, FIRST_CUT), ("sub", k, FIRST_CUT, BLOCK - FIRST_CUT)]
    return slots


AT_ONCE = 2


def body(embeds, pick_blk, mask_blk, pick_sub, mask_sub):
    count = embeds.shape[0] // BLOCK
    sizes = {"sub": lax.axis_size("sub"), "blk": lax.axis_size("blk")}
    slots = plan_slots(sizes)

    def send(array, slot):
        return lax.ppermute(array, slot[0], pairs(slot[1], sizes[slot[0]]))

    outgoing = first_rows(slots[:AT_ONCE], pick_blk, pick_sub, embeds)
    outgoing += pick_rows(slots[AT_ONCE:], pick_blk, pick_sub, embeds)
    arrived = [send(rows, slot) for rows, slot in zip(outgoing, slots)]

    units, live, mine = prepare(slots, pick_blk, pick_sub, mask_blk, mask_sub, embeds)
    totals = jnp.zeros((count * ROWS, LANES), jnp.float32)
    carried = {}
    waiting, late = [], []
    for place, slot in enumerate(slots):
        axis, step, first, rows = slot
        last = place == len(slots) - 1
        ready = [one for one in waiting if last or one[0] <= place]
        waiting = [one for one in waiting if not last and one[0] > place]
        totals, back = work(
            place, slot, arrived[place], units, live, mine, totals, [one[1:] for one in ready], carried.pop(slot[:2], None)
        )
        if first + rows < BLOCK:
            carried[axis, step] = back
        elif axis == "blk":
            waiting.append((place + BEHIND, place, send(back, slot)))
        elif step == 1 and not last:
            waiting.append((len(slots), place, send(back, slot)))
        else:
            late.append((place, send(back, slot)))
    for place, sums in late:
        totals = totals + mine[place] * sums
    return (totals * (1.0 / BLOCK)).reshape(-1)


def solution(mesh):
    return jax.shard_map(
        body,
        mesh=mesh,
        in_specs=(
            P(("groups", "blk", "sub"), None),
            P(("groups", "blk", "sub"), None),
            P(("groups", "blk", "sub"), None),
            P(("groups", "blk"), None),
            P(("groups", "blk", "sub"), None),
        ),
        out_specs=P(("groups", "blk", "sub")),
        check_vma=False,
    )
```

```python
import functools
import math

import jax
import jax.numpy as jnp
from jax import lax
from jax.experimental import pallas as pl
from jax.experimental.pallas import tpu as pltpu
from jax.sharding import PartitionSpec as P

BLOCK = 256
LANES = 128
ROWS = BLOCK // LANES

cutoff = 0.05
sharpness = 100.0

SMEM = pl.BlockSpec(memory_space=pltpu.SMEM)
VMEM = pl.BlockSpec(memory_space=pltpu.VMEM)
HBM = pl.BlockSpec(memory_space=pltpu.HBM)
ANY = pl.BlockSpec(memory_space=pl.ANY)
PARAMS = pltpu.CompilerParams(vmem_limit_bytes=32 * 2**20)


def pairs(step, size):
    return [(i, i ^ step) for i in range(size)]


def rounded_units(rows):
    wide = rows.astype(jnp.float32)
    scale = lax.rsqrt(jnp.sum(wide * wide, axis=1, keepdims=True) + 1e-06)
    return (wide * scale).astype(jnp.bfloat16)


def soft_weights(cosines):
    rate = sharpness * math.log2(math.e)
    return pltpu.reciprocal(1.0 + jnp.exp2(cutoff * rate - cosines * rate), approx=True)


def take_pick(axis, step, pick_blk, pick_sub):
    target = lax.axis_index(axis) ^ step
    return pick_blk[0, target] if axis == "blk" else pick_sub[lax.axis_index("sub"), target]


def first_kernel(slots, pick_blk, pick_sub, embeds, *rest):
    outs, (blk_scalars, sub_scalars, staged, scalar_sems, in_sems, out_sems) = rest[: len(slots)], rest[len(slots) :]
    scalars = [
        pltpu.make_async_copy(pick_blk, blk_scalars, scalar_sems.at[0]),
        pltpu.make_async_copy(pick_sub, sub_scalars, scalar_sems.at[1]),
    ]
    for copy in scalars:
        copy.start()
    half = BLOCK // 2
    entering = []
    for start in range(0, half, PART):
        for top in range(start, embeds.shape[0], BLOCK):
            rows = pl.ds(top, PART)
            entering.append(pltpu.make_async_copy(embeds.at[rows], staged.at[rows], in_sems.at[len(entering)]))
            entering[-1].start()
    for copy in scalars:
        copy.wait()
    picks = [take_pick(axis, step, blk_scalars, sub_scalars) for axis, step, _, _ in slots]
    lower = []
    for start in range(half, BLOCK, PART):
        for place, pick in enumerate(picks):
            source = embeds.at[pl.ds(pl.multiple_of(pick * BLOCK + start, PART), PART)]
            here = staged.at[pl.ds(embeds.shape[0] + place * half + start - half, PART)]
            lower.append(pltpu.make_async_copy(source, here, in_sems.at[len(entering) + len(lower)]))
            lower[-1].start()
    for copy in entering:
        copy.wait()
    leaving = []

    def leave(place, here, start):
        target = outs[place].at[pl.ds(start, PART)]
        leaving.append(pltpu.make_async_copy(here, target, out_sems.at[len(leaving)]))
        leaving[-1].start()

    for start in range(0, half, PART):
        for place, pick in enumerate(picks):
            leave(place, staged.at[pl.ds(pl.multiple_of(pick * BLOCK + start, PART), PART)], start)
    for turn, copy in enumerate(lower):
        copy.wait()
        start, place = divmod(turn, len(slots))
        leave(place, staged.at[pl.ds(embeds.shape[0] + place * half + start * PART, PART)], half + start * PART)
    for copy in leaving:
        copy.wait()


PART = 64


def first_rows(slots, pick_blk, pick_sub, embeds):
    parts = BLOCK // PART
    lower_rows = len(slots) * (BLOCK // 2)
    return pl.pallas_call(
        functools.partial(first_kernel, slots),
        out_shape=[jax.ShapeDtypeStruct((BLOCK, embeds.shape[1]), embeds.dtype)] * len(slots),
        in_specs=[ANY] * 3,
        out_specs=[ANY] * len(slots),
        scratch_shapes=[
            pltpu.SMEM(pick_blk.shape, jnp.int32),
            pltpu.SMEM(pick_sub.shape, jnp.int32),
            pltpu.VMEM((embeds.shape[0] + lower_rows, embeds.shape[1]), embeds.dtype),
            pltpu.SemaphoreType.DMA((2,)),
            pltpu.SemaphoreType.DMA((embeds.shape[0] // 2 // PART + lower_rows // PART,)),
            pltpu.SemaphoreType.DMA((len(slots) * parts,)),
        ],
    )(pick_blk, pick_sub, embeds)


def pick_kernel(slots, pick_blk, pick_sub, embeds, *rest):
    outs, (blk_scalars, sub_scalars, scalar_sems, row_sems) = rest[: len(slots)], rest[len(slots) :]
    scalars = [
        pltpu.make_async_copy(pick_blk, blk_scalars, scalar_sems.at[0]),
        pltpu.make_async_copy(pick_sub, sub_scalars, scalar_sems.at[1]),
    ]
    for copy in scalars:
        copy.start()
    for copy in scalars:
        copy.wait()
    copies = []
    for place, (axis, step, first, rows) in enumerate(slots):
        pick = take_pick(axis, step, blk_scalars, sub_scalars)
        start = pl.multiple_of(pick * BLOCK + first, math.gcd(BLOCK, first))
        copies.append(pltpu.make_async_copy(embeds.at[pl.ds(start, rows)], outs[place], row_sems.at[place]))
        copies[-1].start()
    for copy in copies:
        copy.wait()


def pick_rows(slots, pick_blk, pick_sub, embeds):
    return pl.pallas_call(
        functools.partial(pick_kernel, slots),
        out_shape=[jax.ShapeDtypeStruct((rows, embeds.shape[1]), embeds.dtype) for _, _, _, rows in slots],
        in_specs=[HBM] * 3,
        out_specs=[VMEM] * len(slots),
        scratch_shapes=[
            pltpu.SMEM(pick_blk.shape, jnp.int32),
            pltpu.SMEM(pick_sub.shape, jnp.int32),
            pltpu.SemaphoreType.DMA((2,)),
            pltpu.SemaphoreType.DMA((len(slots),)),
        ],
        compiler_params=PARAMS,
    )(pick_blk, pick_sub, embeds)


def prepare_kernel(slots, pick_blk, pick_sub, mask_blk, mask_sub, embeds, units, live, mine):
    for start in range(0, embeds.shape[0], BLOCK):
        units[:, start : start + BLOCK] = rounded_units(embeds[start : start + BLOCK]).T
    count = live.shape[1]
    block_of = lax.broadcasted_iota(jnp.int32, mine.shape[1:], 0) // ROWS
    for place, (axis, step, _, _) in enumerate(slots):
        source = lax.axis_index(axis) ^ step
        mask = mask_blk if axis == "blk" else mask_sub
        for i in range(count):
            value = mask[0, source * count + i].astype(jnp.float32)
            live[place, i : i + 1] = jnp.full((1, LANES), value, jnp.float32)
        pick = take_pick(axis, step, pick_blk, pick_sub)
        mine[place] = (block_of == pick).astype(jnp.float32)


def prepare(slots, pick_blk, pick_sub, mask_blk, mask_sub, embeds):
    count = embeds.shape[0] // BLOCK
    return pl.pallas_call(
        functools.partial(prepare_kernel, slots),
        out_shape=[
            jax.ShapeDtypeStruct(embeds.shape[::-1], embeds.dtype),
            jax.ShapeDtypeStruct((len(slots), count, LANES), jnp.float32),
            jax.ShapeDtypeStruct((len(slots), count * ROWS, LANES), jnp.float32),
        ],
        in_specs=[SMEM] * 4 + [VMEM],
        out_specs=[VMEM] * 3,
        compiler_params=PARAMS,
    )(pick_blk, pick_sub, mask_blk, mask_sub, embeds)


def slot_kernel(place, first, rows, back_places, carries, arrived, units, live, mine, totals, *rest):
    new_totals, back = rest[-2:]
    count = live.shape[1]
    before = totals[...]
    for back_place, sums in zip(back_places, rest):
        before = before + mine[back_place] * sums[...]
    new_totals[...] = before
    x = rounded_units(arrived[...])
    along_rows = jnp.zeros((rows, LANES), jnp.float32)
    for i in range(count):
        cosines = jnp.dot(x, units[:, i * BLOCK : (i + 1) * BLOCK], preferred_element_type=jnp.float32)
        weights = soft_weights(cosines)
        alive = live[place, i : i + 1]
        parts = [weights[:, part * LANES : (part + 1) * LANES] for part in range(ROWS)]
        along_rows = along_rows + alive * sum(parts)
        for part, piece in enumerate(parts):
            row = i * ROWS + part
            new_totals[row : row + 1] = new_totals[row : row + 1] + alive * jnp.sum(piece, axis=0, keepdims=True)
    empty = [jnp.zeros((gap, LANES), jnp.float32) for gap in (first, BLOCK - first - rows)]
    along_rows = jnp.concatenate([part for part in (empty[0], along_rows, empty[1]) if part.shape[0]], axis=0)
    for part in range(ROWS):
        sums = jnp.sum(along_rows[part * LANES : (part + 1) * LANES].T, axis=0, keepdims=True)
        for i in range(count):
            row = i * ROWS + part
            back[row : row + 1] = sums + rest[-3][row : row + 1] if carries else sums


def work(place, slot, arrived, units, live, mine, totals, returned, carried):
    operands = [arrived, units, live, mine, totals] + [sums for _, sums in returned]
    operands += [] if carried is None else [carried]
    return pl.pallas_call(
        functools.partial(slot_kernel, place, *slot[2:], [one for one, _ in returned], carried is not None),
        out_shape=[jax.ShapeDtypeStruct(totals.shape, jnp.float32)] * 2,
        in_specs=[VMEM] * len(operands),
        out_specs=[VMEM] * 2,
        compiler_params=PARAMS,
    )(*operands)


BEHIND = 2
EARLY_ROWS = 192
HALF = BLOCK // 2


FIRST_CUT = 192


FIRST_CUT = 192


def plan_slots(sizes):
    slots = [("blk", 1, 0, BLOCK), ("sub", 2, 0, BLOCK), ("sub", 1, 0, BLOCK)]
    slots += [("blk", k, 0, BLOCK) for k in range(2, sizes["blk"])]
    for k in range(3, sizes["sub"]):
        slots += [("sub", k, 0, FIRST_CUT), ("sub", k, FIRST_CUT, BLOCK - FIRST_CUT)]
    return slots


AT_ONCE = 2


def body(embeds, pick_blk, mask_blk, pick_sub, mask_sub):
    count = embeds.shape[0] // BLOCK
    sizes = {"sub": lax.axis_size("sub"), "blk": lax.axis_size("blk")}
    slots = plan_slots(sizes)

    def send(array, slot):
        return lax.ppermute(array, slot[0], pairs(slot[1], sizes[slot[0]]))

    outgoing = first_rows(slots[:AT_ONCE], pick_blk, pick_sub, embeds)
    outgoing += pick_rows(slots[AT_ONCE:], pick_blk, pick_sub, embeds)
    arrived = [send(rows, slot) for rows, slot in zip(outgoing, slots)]

    units, live, mine = prepare(slots, pick_blk, pick_sub, mask_blk, mask_sub, embeds)
    totals = jnp.zeros((count * ROWS, LANES), jnp.float32)
    carried = {}
    waiting, late = [], []
    for place, slot in enumerate(slots):
        axis, step, first, rows = slot
        last = place == len(slots) - 1
        ready = [one for one in waiting if last or one[0] <= place]
        waiting = [one for one in waiting if not last and one[0] > place]
        totals, back = work(
            place, slot, arrived[place], units, live, mine, totals, [one[1:] for one in ready], carried.pop(slot[:2], None)
        )
        if first + rows < BLOCK:
            carried[axis, step] = back
        elif axis == "blk":
            waiting.append((place + BEHIND, place, send(back, slot)))
        else:
            late.append((place, send(back, slot)))
    for place, sums in late:
        totals = totals + mine[place] * sums
    return (totals * (1.0 / BLOCK)).reshape(-1)


def solution(mesh):
    return jax.shard_map(
        body,
        mesh=mesh,
        in_specs=(
            P(("groups", "blk", "sub"), None),
            P(("groups", "blk", "sub"), None),
            P(("groups", "blk", "sub"), None),
            P(("groups", "blk"), None),
            P(("groups", "blk", "sub"), None),
        ),
        out_specs=P(("groups", "blk", "sub")),
        check_vma=False,
    )
```

```python
import functools
import math

import jax
import jax.numpy as jnp
from jax import lax
from jax.experimental import pallas as pl
from jax.experimental.pallas import tpu as pltpu
from jax.sharding import PartitionSpec as P

BLOCK = 256
LANES = 128
ROWS = BLOCK // LANES

cutoff = 0.05
sharpness = 100.0

SMEM = pl.BlockSpec(memory_space=pltpu.SMEM)
VMEM = pl.BlockSpec(memory_space=pltpu.VMEM)
HBM = pl.BlockSpec(memory_space=pltpu.HBM)
ANY = pl.BlockSpec(memory_space=pl.ANY)
PARAMS = pltpu.CompilerParams(vmem_limit_bytes=32 * 2**20)


def pairs(step, size):
    return [(i, i ^ step) for i in range(size)]


def rounded_units(rows):
    wide = rows.astype(jnp.float32)
    scale = lax.rsqrt(jnp.sum(wide * wide, axis=1, keepdims=True) + 1e-06)
    return (wide * scale).astype(jnp.bfloat16)


def soft_weights(cosines):
    rate = sharpness * math.log2(math.e)
    return pltpu.reciprocal(1.0 + jnp.exp2(cutoff * rate - cosines * rate), approx=True)


def take_pick(axis, step, pick_blk, pick_sub):
    target = lax.axis_index(axis) ^ step
    return pick_blk[0, target] if axis == "blk" else pick_sub[lax.axis_index("sub"), target]


def first_kernel(slots, pick_blk, pick_sub, embeds, *rest):
    outs, (blk_scalars, sub_scalars, staged, scalar_sems, in_sems, out_sems) = rest[: len(slots)], rest[len(slots) :]
    scalars = [
        pltpu.make_async_copy(pick_blk, blk_scalars, scalar_sems.at[0]),
        pltpu.make_async_copy(pick_sub, sub_scalars, scalar_sems.at[1]),
    ]
    for copy in scalars:
        copy.start()
    starts = range(0, BLOCK, PART)
    entering = []
    for start in starts:
        for top in range(start, embeds.shape[0], BLOCK):
            rows = pl.ds(top, PART)
            entering.append(pltpu.make_async_copy(embeds.at[rows], staged.at[rows], in_sems.at[len(entering)]))
            entering[-1].start()
    for copy in scalars:
        copy.wait()
    picks = [take_pick(axis, step, blk_scalars, sub_scalars) for axis, step, _, _ in slots]
    count = embeds.shape[0] // BLOCK
    leaving = []
    for turn, start in enumerate(starts):
        for copy in entering[turn * count : (turn + 1) * count]:
            copy.wait()
        for pick, out in zip(picks, outs):
            here = staged.at[pl.ds(pl.multiple_of(pick * BLOCK + start, PART), PART)]
            leaving.append(pltpu.make_async_copy(here, out.at[pl.ds(start, PART)], out_sems.at[len(leaving)]))
            leaving[-1].start()
    for copy in leaving:
        copy.wait()


PART = 64


def first_rows(slots, pick_blk, pick_sub, embeds):
    parts = BLOCK // PART
    return pl.pallas_call(
        functools.partial(first_kernel, slots),
        out_shape=[jax.ShapeDtypeStruct((BLOCK, embeds.shape[1]), embeds.dtype)] * len(slots),
        in_specs=[ANY] * 3,
        out_specs=[ANY] * len(slots),
        scratch_shapes=[
            pltpu.SMEM(pick_blk.shape, jnp.int32),
            pltpu.SMEM(pick_sub.shape, jnp.int32),
            pltpu.VMEM(embeds.shape, embeds.dtype),
            pltpu.SemaphoreType.DMA((2,)),
            pltpu.SemaphoreType.DMA((embeds.shape[0] // PART,)),
            pltpu.SemaphoreType.DMA((len(slots) * parts,)),
        ],
    )(pick_blk, pick_sub, embeds)


def pick_kernel(slots, pick_blk, pick_sub, embeds, *rest):
    outs, (blk_scalars, sub_scalars, scalar_sems, row_sems) = rest[: len(slots)], rest[len(slots) :]
    scalars = [
        pltpu.make_async_copy(pick_blk, blk_scalars, scalar_sems.at[0]),
        pltpu.make_async_copy(pick_sub, sub_scalars, scalar_sems.at[1]),
    ]
    for copy in scalars:
        copy.start()
    for copy in scalars:
        copy.wait()
    copies = []
    for place, (axis, step, first, rows) in enumerate(slots):
        pick = take_pick(axis, step, blk_scalars, sub_scalars)
        start = pl.multiple_of(pick * BLOCK + first, math.gcd(BLOCK, first))
        copies.append(pltpu.make_async_copy(embeds.at[pl.ds(start, rows)], outs[place], row_sems.at[place]))
        copies[-1].start()
    for copy in copies:
        copy.wait()


def pick_rows(slots, pick_blk, pick_sub, embeds):
    return pl.pallas_call(
        functools.partial(pick_kernel, slots),
        out_shape=[jax.ShapeDtypeStruct((rows, embeds.shape[1]), embeds.dtype) for _, _, _, rows in slots],
        in_specs=[HBM] * 3,
        out_specs=[VMEM] * len(slots),
        scratch_shapes=[
            pltpu.SMEM(pick_blk.shape, jnp.int32),
            pltpu.SMEM(pick_sub.shape, jnp.int32),
            pltpu.SemaphoreType.DMA((2,)),
            pltpu.SemaphoreType.DMA((len(slots),)),
        ],
        compiler_params=PARAMS,
    )(pick_blk, pick_sub, embeds)


def prepare_kernel(slots, pick_blk, pick_sub, mask_blk, mask_sub, embeds, units, live, mine):
    for start in range(0, embeds.shape[0], BLOCK):
        units[:, start : start + BLOCK] = rounded_units(embeds[start : start + BLOCK]).T
    count = live.shape[1]
    block_of = lax.broadcasted_iota(jnp.int32, mine.shape[1:], 0) // ROWS
    for place, (axis, step, _, _) in enumerate(slots):
        source = lax.axis_index(axis) ^ step
        mask = mask_blk if axis == "blk" else mask_sub
        for i in range(count):
            value = mask[0, source * count + i].astype(jnp.float32)
            live[place, i : i + 1] = jnp.full((1, LANES), value, jnp.float32)
        pick = take_pick(axis, step, pick_blk, pick_sub)
        mine[place] = (block_of == pick).astype(jnp.float32)


def prepare(slots, pick_blk, pick_sub, mask_blk, mask_sub, embeds):
    count = embeds.shape[0] // BLOCK
    return pl.pallas_call(
        functools.partial(prepare_kernel, slots),
        out_shape=[
            jax.ShapeDtypeStruct(embeds.shape[::-1], embeds.dtype),
            jax.ShapeDtypeStruct((len(slots), count, LANES), jnp.float32),
            jax.ShapeDtypeStruct((len(slots), count * ROWS, LANES), jnp.float32),
        ],
        in_specs=[SMEM] * 4 + [VMEM],
        out_specs=[VMEM] * 3,
        compiler_params=PARAMS,
    )(pick_blk, pick_sub, mask_blk, mask_sub, embeds)


def slot_kernel(place, first, rows, back_places, carries, arrived, units, live, mine, totals, *rest):
    new_totals, back = rest[-2:]
    count = live.shape[1]
    before = totals[...]
    for back_place, sums in zip(back_places, rest):
        before = before + mine[back_place] * sums[...]
    new_totals[...] = before
    x = rounded_units(arrived[...])
    along_rows = jnp.zeros((rows, LANES), jnp.float32)
    for i in range(count):
        cosines = jnp.dot(x, units[:, i * BLOCK : (i + 1) * BLOCK], preferred_element_type=jnp.float32)
        weights = soft_weights(cosines)
        alive = live[place, i : i + 1]
        parts = [weights[:, part * LANES : (part + 1) * LANES] for part in range(ROWS)]
        along_rows = along_rows + alive * sum(parts)
        for part, piece in enumerate(parts):
            row = i * ROWS + part
            new_totals[row : row + 1] = new_totals[row : row + 1] + alive * jnp.sum(piece, axis=0, keepdims=True)
    empty = [jnp.zeros((gap, LANES), jnp.float32) for gap in (first, BLOCK - first - rows)]
    along_rows = jnp.concatenate([part for part in (empty[0], along_rows, empty[1]) if part.shape[0]], axis=0)
    for part in range(ROWS):
        sums = jnp.sum(along_rows[part * LANES : (part + 1) * LANES].T, axis=0, keepdims=True)
        for i in range(count):
            row = i * ROWS + part
            back[row : row + 1] = sums + rest[-3][row : row + 1] if carries else sums


def work(place, slot, arrived, units, live, mine, totals, returned, carried):
    operands = [arrived, units, live, mine, totals] + [sums for _, sums in returned]
    operands += [] if carried is None else [carried]
    return pl.pallas_call(
        functools.partial(slot_kernel, place, *slot[2:], [one for one, _ in returned], carried is not None),
        out_shape=[jax.ShapeDtypeStruct(totals.shape, jnp.float32)] * 2,
        in_specs=[VMEM] * len(operands),
        out_specs=[VMEM] * 2,
        compiler_params=PARAMS,
    )(*operands)


BEHIND = 2
EARLY_ROWS = 192
HALF = BLOCK // 2


FIRST_CUT = 128


def plan_slots(sizes):
    slots = [("blk", 1, 0, BLOCK), ("sub", 2, 0, BLOCK), ("sub", 1, 0, BLOCK)]
    slots += [("blk", k, 0, BLOCK) for k in range(2, sizes["blk"])]
    for k in range(3, sizes["sub"]):
        slots += [("sub", k, 0, FIRST_CUT), ("sub", k, FIRST_CUT, BLOCK - FIRST_CUT)]
    return slots


AT_ONCE = 2


def body(embeds, pick_blk, mask_blk, pick_sub, mask_sub):
    count = embeds.shape[0] // BLOCK
    sizes = {"sub": lax.axis_size("sub"), "blk": lax.axis_size("blk")}
    slots = plan_slots(sizes)

    def send(array, slot):
        return lax.ppermute(array, slot[0], pairs(slot[1], sizes[slot[0]]))

    outgoing = first_rows(slots[:AT_ONCE], pick_blk, pick_sub, embeds)
    outgoing += pick_rows(slots[AT_ONCE:], pick_blk, pick_sub, embeds)
    arrived = [send(rows, slot) for rows, slot in zip(outgoing, slots)]

    units, live, mine = prepare(slots, pick_blk, pick_sub, mask_blk, mask_sub, embeds)
    totals = jnp.zeros((count * ROWS, LANES), jnp.float32)
    carried = {}
    waiting, late = [], []
    for place, slot in enumerate(slots):
        axis, step, first, rows = slot
        last = place == len(slots) - 1
        ready = [one for one in waiting if last or one[0] <= place]
        waiting = [one for one in waiting if not last and one[0] > place]
        totals, back = work(
            place, slot, arrived[place], units, live, mine, totals, [one[1:] for one in ready], carried.pop(slot[:2], None)
        )
        if first + rows < BLOCK:
            carried[axis, step] = back
        elif axis == "blk":
            waiting.append((place + BEHIND, place, send(back, slot)))
        else:
            late.append((place, send(back, slot)))
    for place, sums in late:
        totals = totals + mine[place] * sums
    return (totals * (1.0 / BLOCK)).reshape(-1)


def solution(mesh):
    return jax.shard_map(
        body,
        mesh=mesh,
        in_specs=(
            P(("groups", "blk", "sub"), None),
            P(("groups", "blk", "sub"), None),
            P(("groups", "blk", "sub"), None),
            P(("groups", "blk"), None),
            P(("groups", "blk", "sub"), None),
        ),
        out_specs=P(("groups", "blk", "sub")),
        check_vma=False,
    )
```

```python
import functools
import math

import jax
import jax.numpy as jnp
from jax import lax
from jax.experimental import pallas as pl
from jax.experimental.pallas import tpu as pltpu
from jax.sharding import PartitionSpec as P

BLOCK = 256
LANES = 128
ROWS = BLOCK // LANES

cutoff = 0.05
sharpness = 100.0

SMEM = pl.BlockSpec(memory_space=pltpu.SMEM)
VMEM = pl.BlockSpec(memory_space=pltpu.VMEM)
ANY = pl.BlockSpec(memory_space=pl.ANY)
PARAMS = pltpu.CompilerParams(vmem_limit_bytes=32 * 2**20)


def pairs(step, size):
    return [(i, i ^ step) for i in range(size)]


def rounded_units(rows):
    wide = rows.astype(jnp.float32)
    scale = lax.rsqrt(jnp.sum(wide * wide, axis=1, keepdims=True) + 1e-06)
    return (wide * scale).astype(jnp.bfloat16)


def soft_weights(cosines):
    rate = sharpness * math.log2(math.e)
    return pltpu.reciprocal(1.0 + jnp.exp2(cutoff * rate - cosines * rate), approx=True)


def take_pick(axis, step, pick_blk, pick_sub):
    target = lax.axis_index(axis) ^ step
    return pick_blk[0, target] if axis == "blk" else pick_sub[lax.axis_index("sub"), target]


def pick_kernel(slots, pick_blk, pick_sub, embeds, *rest):
    outs, (blk_scalars, sub_scalars, staged, scalar_sems, in_sems, out_sems) = rest[: len(slots)], rest[len(slots) :]
    scalars = [
        pltpu.make_async_copy(pick_blk, blk_scalars, scalar_sems.at[0]),
        pltpu.make_async_copy(pick_sub, sub_scalars, scalar_sems.at[1]),
    ]
    for copy in scalars:
        copy.start()
    starts = range(0, BLOCK, PART)
    entering = []
    for start in starts:
        for top in range(start, embeds.shape[0], BLOCK):
            rows = pl.ds(top, PART)
            entering.append(pltpu.make_async_copy(embeds.at[rows], staged.at[rows], in_sems.at[len(entering)]))
            entering[-1].start()
    for copy in scalars:
        copy.wait()
    picks = [take_pick(axis, step, blk_scalars, sub_scalars) for axis, step, _, _ in slots]
    count = embeds.shape[0] // BLOCK
    leaving = []
    for turn, start in enumerate(starts):
        for copy in entering[turn * count : (turn + 1) * count]:
            copy.wait()
        for pick, out in zip(picks, outs):
            here = staged.at[pl.ds(pl.multiple_of(pick * BLOCK + start, PART), PART)]
            leaving.append(pltpu.make_async_copy(here, out.at[pl.ds(start, PART)], out_sems.at[len(leaving)]))
            leaving[-1].start()
    for copy in leaving:
        copy.wait()


PART = 128


def pick_rows(slots, pick_blk, pick_sub, embeds):
    parts = BLOCK // PART
    return pl.pallas_call(
        functools.partial(pick_kernel, slots),
        out_shape=[jax.ShapeDtypeStruct((BLOCK, embeds.shape[1]), embeds.dtype)] * len(slots),
        in_specs=[ANY] * 3,
        out_specs=[ANY] * len(slots),
        scratch_shapes=[
            pltpu.SMEM(pick_blk.shape, jnp.int32),
            pltpu.SMEM(pick_sub.shape, jnp.int32),
            pltpu.VMEM(embeds.shape, embeds.dtype),
            pltpu.SemaphoreType.DMA((2,)),
            pltpu.SemaphoreType.DMA((embeds.shape[0] // PART,)),
            pltpu.SemaphoreType.DMA((len(slots) * parts,)),
        ],
    )(pick_blk, pick_sub, embeds)


def prepare_kernel(slots, pick_blk, pick_sub, mask_blk, mask_sub, embeds, units, live, mine):
    for start in range(0, embeds.shape[0], BLOCK):
        units[:, start : start + BLOCK] = rounded_units(embeds[start : start + BLOCK]).T
    count = live.shape[1]
    block_of = lax.broadcasted_iota(jnp.int32, mine.shape[1:], 0) // ROWS
    for place, (axis, step, _, _) in enumerate(slots):
        source = lax.axis_index(axis) ^ step
        mask = mask_blk if axis == "blk" else mask_sub
        for i in range(count):
            value = mask[0, source * count + i].astype(jnp.float32)
            live[place, i : i + 1] = jnp.full((1, LANES), value, jnp.float32)
        pick = take_pick(axis, step, pick_blk, pick_sub)
        mine[place] = (block_of == pick).astype(jnp.float32)


def prepare(slots, pick_blk, pick_sub, mask_blk, mask_sub, embeds):
    count = embeds.shape[0] // BLOCK
    return pl.pallas_call(
        functools.partial(prepare_kernel, slots),
        out_shape=[
            jax.ShapeDtypeStruct(embeds.shape[::-1], embeds.dtype),
            jax.ShapeDtypeStruct((len(slots), count, LANES), jnp.float32),
            jax.ShapeDtypeStruct((len(slots), count * ROWS, LANES), jnp.float32),
        ],
        in_specs=[SMEM] * 4 + [VMEM],
        out_specs=[VMEM] * 3,
        compiler_params=PARAMS,
    )(pick_blk, pick_sub, mask_blk, mask_sub, embeds)


def slot_kernel(place, axis, step, first, rows, back_places, carries, arrived, units, live, mine, totals, *rest):
    new_totals, back = rest[-2:]
    count = live.shape[1]
    before = totals[...]
    for back_place, sums in zip(back_places, rest):
        before = before + mine[back_place] * sums[...]
    new_totals[...] = before
    top = 0
    if arrived.shape[0] != rows:
        own = lax.axis_index(axis)
        top = pl.multiple_of(jnp.where((own ^ step) > own, rows, 0), rows)
    x = rounded_units(arrived[pl.ds(top, rows)])
    along_rows = jnp.zeros((rows, LANES), jnp.float32)
    for i in range(count):
        cosines = jnp.dot(x, units[:, i * BLOCK : (i + 1) * BLOCK], preferred_element_type=jnp.float32)
        weights = soft_weights(cosines)
        alive = live[place, i : i + 1]
        parts = [weights[:, part * LANES : (part + 1) * LANES] for part in range(ROWS)]
        along_rows = along_rows + alive * sum(parts)
        for part, piece in enumerate(parts):
            row = i * ROWS + part
            new_totals[row : row + 1] = new_totals[row : row + 1] + alive * jnp.sum(piece, axis=0, keepdims=True)
    empty = [jnp.zeros((gap, LANES), jnp.float32) for gap in (first, BLOCK - first - rows)]
    along_rows = jnp.concatenate([part for part in (empty[0], along_rows, empty[1]) if part.shape[0]], axis=0)
    for part in range(ROWS):
        sums = jnp.sum(along_rows[part * LANES : (part + 1) * LANES].T, axis=0, keepdims=True)
        for i in range(count):
            row = i * ROWS + part
            back[row : row + 1] = sums + rest[-3][row : row + 1] if carries else sums


def work(place, slot, arrived, units, live, mine, totals, returned, carried):
    operands = [arrived, units, live, mine, totals] + [sums for _, sums in returned]
    operands += [] if carried is None else [carried]
    return pl.pallas_call(
        functools.partial(slot_kernel, place, *slot, [one for one, _ in returned], carried is not None),
        out_shape=[jax.ShapeDtypeStruct(totals.shape, jnp.float32)] * 2,
        in_specs=[VMEM] * len(operands),
        out_specs=[VMEM] * 2,
        compiler_params=PARAMS,
    )(*operands)


BEHIND = 2
def plan_slots(sizes):
    slots = [("sub", 2, 0, BLOCK), ("blk", 1, 0, BLOCK)]
    slots += [("blk", k, 0, BLOCK) for k in range(2, sizes["blk"])]
    return slots + [("sub", k, 0, BLOCK) for k in (1, *range(3, sizes["sub"]))]


def body(embeds, pick_blk, mask_blk, pick_sub, mask_sub):
    count = embeds.shape[0] // BLOCK
    sizes = {"sub": lax.axis_size("sub"), "blk": lax.axis_size("blk")}
    slots = plan_slots(sizes)

    def send(array, slot):
        return lax.ppermute(array, slot[0], pairs(slot[1], sizes[slot[0]]))

    def exchange(array, slot):
        if slot[0] == "sub":
            return send(array, slot)
        groups = [[a, b] for a, b in pairs(slot[1], sizes["blk"]) if a < b]
        return lax.all_gather(array, "blk", axis_index_groups=groups, axis=0, tiled=True)

    outgoing = pick_rows(slots, pick_blk, pick_sub, embeds)
    arrived = [exchange(rows, slot) for rows, slot in zip(outgoing, slots)]

    units, live, mine = prepare(slots, pick_blk, pick_sub, mask_blk, mask_sub, embeds)
    totals = jnp.zeros((count * ROWS, LANES), jnp.float32)
    carried = {}
    waiting, late = [], []
    for place, slot in enumerate(slots):
        axis, step, first, rows = slot
        last = place == len(slots) - 1
        ready = [one for one in waiting if last or one[0] <= place]
        waiting = [one for one in waiting if not last and one[0] > place]
        totals, back = work(
            place, slot, arrived[place], units, live, mine, totals, [one[1:] for one in ready], carried.pop(slot[:2], None)
        )
        if first + rows < BLOCK:
            carried[axis, step] = back
        elif axis == "blk":
            waiting.append((place + BEHIND, place, send(back, slot)))
        else:
            late.append((place, send(back, slot)))
    for place, sums in late:
        totals = totals + mine[place] * sums
    return (totals * (1.0 / BLOCK)).reshape(-1)


def solution(mesh):
    return jax.shard_map(
        body,
        mesh=mesh,
        in_specs=(
            P(("groups", "blk", "sub"), None),
            P(("groups", "blk", "sub"), None),
            P(("groups", "blk", "sub"), None),
            P(("groups", "blk"), None),
            P(("groups", "blk", "sub"), None),
        ),
        out_specs=P(("groups", "blk", "sub")),
        check_vma=False,
    )
```

```python
import functools
import math

import jax
import jax.numpy as jnp
from jax import lax
from jax.experimental import pallas as pl
from jax.experimental.pallas import tpu as pltpu
from jax.sharding import PartitionSpec as P

BLOCK = 256
LANES = 128
ROWS = BLOCK // LANES

cutoff = 0.05
sharpness = 100.0

SMEM = pl.BlockSpec(memory_space=pltpu.SMEM)
VMEM = pl.BlockSpec(memory_space=pltpu.VMEM)
HBM = pl.BlockSpec(memory_space=pltpu.HBM)
ANY = pl.BlockSpec(memory_space=pl.ANY)
PARAMS = pltpu.CompilerParams(vmem_limit_bytes=32 * 2**20)


def pairs(step, size):
    return [(i, i ^ step) for i in range(size)]


def rounded_units(rows):
    wide = rows.astype(jnp.float32)
    scale = lax.rsqrt(jnp.sum(wide * wide, axis=1, keepdims=True) + 1e-06)
    return (wide * scale).astype(jnp.bfloat16)


def soft_weights(cosines):
    rate = sharpness * math.log2(math.e)
    return pltpu.reciprocal(1.0 + jnp.exp2(cutoff * rate - cosines * rate), approx=True)


def take_pick(axis, step, pick_blk, pick_sub):
    target = lax.axis_index(axis) ^ step
    return pick_blk[0, target] if axis == "blk" else pick_sub[lax.axis_index("sub"), target]


def first_kernel(slots, pick_blk, pick_sub, embeds, *rest):
    outs, (blk_scalars, sub_scalars, staged, scalar_sems, in_sems, out_sems) = rest[: len(slots)], rest[len(slots) :]
    scalars = [
        pltpu.make_async_copy(pick_blk, blk_scalars, scalar_sems.at[0]),
        pltpu.make_async_copy(pick_sub, sub_scalars, scalar_sems.at[1]),
    ]
    for copy in scalars:
        copy.start()
    starts = range(0, BLOCK, PART)
    entering = []
    for start in starts:
        for top in range(start, embeds.shape[0], BLOCK):
            rows = pl.ds(top, PART)
            entering.append(pltpu.make_async_copy(embeds.at[rows], staged.at[rows], in_sems.at[len(entering)]))
            entering[-1].start()
    for copy in scalars:
        copy.wait()
    picks = [take_pick(axis, step, blk_scalars, sub_scalars) for axis, step, _, _ in slots]
    count = embeds.shape[0] // BLOCK
    leaving = []
    for turn, start in enumerate(starts):
        for copy in entering[turn * count : (turn + 1) * count]:
            copy.wait()
        for pick, out in zip(picks, outs):
            here = staged.at[pl.ds(pl.multiple_of(pick * BLOCK + start, PART), PART)]
            leaving.append(pltpu.make_async_copy(here, out.at[pl.ds(start, PART)], out_sems.at[len(leaving)]))
            leaving[-1].start()
    for copy in leaving:
        copy.wait()


PART = 64


def first_rows(slots, pick_blk, pick_sub, embeds):
    parts = BLOCK // PART
    return pl.pallas_call(
        functools.partial(first_kernel, slots),
        out_shape=[jax.ShapeDtypeStruct((BLOCK, embeds.shape[1]), embeds.dtype)] * len(slots),
        in_specs=[ANY] * 3,
        out_specs=[ANY] * len(slots),
        scratch_shapes=[
            pltpu.SMEM(pick_blk.shape, jnp.int32),
            pltpu.SMEM(pick_sub.shape, jnp.int32),
            pltpu.VMEM(embeds.shape, embeds.dtype),
            pltpu.SemaphoreType.DMA((2,)),
            pltpu.SemaphoreType.DMA((embeds.shape[0] // PART,)),
            pltpu.SemaphoreType.DMA((len(slots) * parts,)),
        ],
    )(pick_blk, pick_sub, embeds)


def pick_kernel(slots, pick_blk, pick_sub, embeds, *rest):
    outs, (blk_scalars, sub_scalars, scalar_sems, row_sems) = rest[: len(slots)], rest[len(slots) :]
    scalars = [
        pltpu.make_async_copy(pick_blk, blk_scalars, scalar_sems.at[0]),
        pltpu.make_async_copy(pick_sub, sub_scalars, scalar_sems.at[1]),
    ]
    for copy in scalars:
        copy.start()
    for copy in scalars:
        copy.wait()
    copies = []
    for place, (axis, step, first, rows) in enumerate(slots):
        pick = take_pick(axis, step, blk_scalars, sub_scalars)
        start = pl.multiple_of(pick * BLOCK + first, math.gcd(BLOCK, first))
        copies.append(pltpu.make_async_copy(embeds.at[pl.ds(start, rows)], outs[place], row_sems.at[place]))
        copies[-1].start()
    for copy in copies:
        copy.wait()


def pick_rows(slots, pick_blk, pick_sub, embeds):
    return pl.pallas_call(
        functools.partial(pick_kernel, slots),
        out_shape=[jax.ShapeDtypeStruct((rows, embeds.shape[1]), embeds.dtype) for _, _, _, rows in slots],
        in_specs=[HBM] * 3,
        out_specs=[VMEM] * len(slots),
        scratch_shapes=[
            pltpu.SMEM(pick_blk.shape, jnp.int32),
            pltpu.SMEM(pick_sub.shape, jnp.int32),
            pltpu.SemaphoreType.DMA((2,)),
            pltpu.SemaphoreType.DMA((len(slots),)),
        ],
        compiler_params=PARAMS,
    )(pick_blk, pick_sub, embeds)


def prepare_kernel(slots, pick_blk, pick_sub, mask_blk, mask_sub, embeds, units, live, mine):
    for start in range(0, embeds.shape[0], BLOCK):
        units[:, start : start + BLOCK] = rounded_units(embeds[start : start + BLOCK]).T
    count = live.shape[1]
    block_of = lax.broadcasted_iota(jnp.int32, mine.shape[1:], 0) // ROWS
    for place, (axis, step, _, _) in enumerate(slots):
        source = lax.axis_index(axis) ^ step
        mask = mask_blk if axis == "blk" else mask_sub
        for i in range(count):
            value = mask[0, source * count + i].astype(jnp.float32)
            live[place, i : i + 1] = jnp.full((1, LANES), value, jnp.float32)
        pick = take_pick(axis, step, pick_blk, pick_sub)
        mine[place] = (block_of == pick).astype(jnp.float32)


def prepare(slots, pick_blk, pick_sub, mask_blk, mask_sub, embeds):
    count = embeds.shape[0] // BLOCK
    return pl.pallas_call(
        functools.partial(prepare_kernel, slots),
        out_shape=[
            jax.ShapeDtypeStruct(embeds.shape[::-1], embeds.dtype),
            jax.ShapeDtypeStruct((len(slots), count, LANES), jnp.float32),
            jax.ShapeDtypeStruct((len(slots), count * ROWS, LANES), jnp.float32),
        ],
        in_specs=[SMEM] * 4 + [VMEM],
        out_specs=[VMEM] * 3,
        compiler_params=PARAMS,
    )(pick_blk, pick_sub, mask_blk, mask_sub, embeds)


def slot_kernel(place, first, rows, back_places, carries, arrived, units, live, mine, totals, *rest):
    new_totals, back = rest[-2:]
    count = live.shape[1]
    before = totals[...]
    for back_place, sums in zip(back_places, rest):
        before = before + mine[back_place] * sums[...]
    new_totals[...] = before
    x = rounded_units(arrived[...])
    along_rows = jnp.zeros((rows, LANES), jnp.float32)
    for i in range(count):
        cosines = jnp.dot(x, units[:, i * BLOCK : (i + 1) * BLOCK], preferred_element_type=jnp.float32)
        weights = soft_weights(cosines)
        alive = live[place, i : i + 1]
        parts = [weights[:, part * LANES : (part + 1) * LANES] for part in range(ROWS)]
        along_rows = along_rows + alive * sum(parts)
        for part, piece in enumerate(parts):
            row = i * ROWS + part
            new_totals[row : row + 1] = new_totals[row : row + 1] + alive * jnp.sum(piece, axis=0, keepdims=True)
    empty = [jnp.zeros((gap, LANES), jnp.float32) for gap in (first, BLOCK - first - rows)]
    along_rows = jnp.concatenate([part for part in (empty[0], along_rows, empty[1]) if part.shape[0]], axis=0)
    for part in range(ROWS):
        sums = jnp.sum(along_rows[part * LANES : (part + 1) * LANES].T, axis=0, keepdims=True)
        for i in range(count):
            row = i * ROWS + part
            back[row : row + 1] = sums + rest[-3][row : row + 1] if carries else sums


def work(place, slot, arrived, units, live, mine, totals, returned, carried):
    operands = [arrived, units, live, mine, totals] + [sums for _, sums in returned]
    operands += [] if carried is None else [carried]
    return pl.pallas_call(
        functools.partial(slot_kernel, place, *slot[2:], [one for one, _ in returned], carried is not None),
        out_shape=[jax.ShapeDtypeStruct(totals.shape, jnp.float32)] * 2,
        in_specs=[VMEM] * len(operands),
        out_specs=[VMEM] * 2,
        compiler_params=PARAMS,
    )(*operands)


BEHIND = 2
NEAR_CUT = 128
FAR_CUT = 160


def plan_slots(sizes):
    slots = [("blk", 1, 0, BLOCK), ("sub", 2, 0, BLOCK), ("sub", 1, 0, NEAR_CUT)]
    slots += [("blk", k, 0, BLOCK) for k in range(2, sizes["blk"])]
    slots += [("sub", k, 0, FAR_CUT) for k in range(3, sizes["sub"])] + [("sub", 1, NEAR_CUT, BLOCK - NEAR_CUT)]
    return slots + [("sub", k, FAR_CUT, BLOCK - FAR_CUT) for k in range(3, sizes["sub"])]


AT_ONCE = 2


def body(embeds, pick_blk, mask_blk, pick_sub, mask_sub):
    count = embeds.shape[0] // BLOCK
    sizes = {"sub": lax.axis_size("sub"), "blk": lax.axis_size("blk")}
    slots = plan_slots(sizes)

    def send(array, slot):
        return lax.ppermute(array, slot[0], pairs(slot[1], sizes[slot[0]]))

    outgoing = first_rows(slots[:AT_ONCE], pick_blk, pick_sub, embeds)
    outgoing += pick_rows(slots[AT_ONCE:], pick_blk, pick_sub, embeds)
    arrived = [send(rows, slot) for rows, slot in zip(outgoing, slots)]

    units, live, mine = prepare(slots, pick_blk, pick_sub, mask_blk, mask_sub, embeds)
    totals = jnp.zeros((count * ROWS, LANES), jnp.float32)
    carried = {}
    waiting, late = [], []
    for place, slot in enumerate(slots):
        axis, step, first, rows = slot
        last = place == len(slots) - 1
        ready = [one for one in waiting if last or one[0] <= place]
        waiting = [one for one in waiting if not last and one[0] > place]
        totals, back = work(
            place, slot, arrived[place], units, live, mine, totals, [one[1:] for one in ready], carried.pop(slot[:2], None)
        )
        if first + rows < BLOCK:
            carried[axis, step] = back
        elif axis == "blk":
            waiting.append((place + BEHIND, place, send(back, slot)))
        elif step == 1 and not last:
            waiting.append((len(slots), place, send(back, slot)))
        else:
            late.append((place, send(back, slot)))
    for place, sums in late:
        totals = totals + mine[place] * sums
    return (totals * (1.0 / BLOCK)).reshape(-1)


def solution(mesh):
    return jax.shard_map(
        body,
        mesh=mesh,
        in_specs=(
            P(("groups", "blk", "sub"), None),
            P(("groups", "blk", "sub"), None),
            P(("groups", "blk", "sub"), None),
            P(("groups", "blk"), None),
            P(("groups", "blk", "sub"), None),
        ),
        out_specs=P(("groups", "blk", "sub")),
        check_vma=False,
    )
```

```python
import functools
import math

import jax
import jax.numpy as jnp
from jax import lax
from jax.experimental import pallas as pl
from jax.experimental.pallas import tpu as pltpu
from jax.sharding import PartitionSpec as P

BLOCK = 256
LANES = 128
ROWS = BLOCK // LANES

cutoff = 0.05
sharpness = 100.0

SMEM = pl.BlockSpec(memory_space=pltpu.SMEM)
VMEM = pl.BlockSpec(memory_space=pltpu.VMEM)
HBM = pl.BlockSpec(memory_space=pltpu.HBM)
ANY = pl.BlockSpec(memory_space=pl.ANY)
PARAMS = pltpu.CompilerParams(vmem_limit_bytes=32 * 2**20)


def pairs(step, size):
    return [(i, i ^ step) for i in range(size)]


def rounded_units(rows):
    wide = rows.astype(jnp.float32)
    scale = lax.rsqrt(jnp.sum(wide * wide, axis=1, keepdims=True) + 1e-06)
    return (wide * scale).astype(jnp.bfloat16)


def soft_weights(cosines):
    rate = sharpness * math.log2(math.e)
    return pltpu.reciprocal(1.0 + jnp.exp2(cutoff * rate - cosines * rate), approx=True)


def take_pick(axis, step, pick_blk, pick_sub):
    target = lax.axis_index(axis) ^ step
    return pick_blk[0, target] if axis == "blk" else pick_sub[lax.axis_index("sub"), target]


def first_kernel(slots, pick_blk, pick_sub, embeds, *rest):
    outs, (blk_scalars, sub_scalars, staged, scalar_sems, in_sems, out_sems) = rest[: len(slots)], rest[len(slots) :]
    scalars = [
        pltpu.make_async_copy(pick_blk, blk_scalars, scalar_sems.at[0]),
        pltpu.make_async_copy(pick_sub, sub_scalars, scalar_sems.at[1]),
    ]
    for copy in scalars:
        copy.start()
    starts = range(0, BLOCK, PART)
    entering = []
    for start in starts:
        for top in range(start, embeds.shape[0], BLOCK):
            rows = pl.ds(top, PART)
            entering.append(pltpu.make_async_copy(embeds.at[rows], staged.at[rows], in_sems.at[len(entering)]))
            entering[-1].start()
    for copy in scalars:
        copy.wait()
    picks = [take_pick(axis, step, blk_scalars, sub_scalars) for axis, step, _, _ in slots]
    count = embeds.shape[0] // BLOCK
    leaving = []
    for turn, start in enumerate(starts):
        for copy in entering[turn * count : (turn + 1) * count]:
            copy.wait()
        for pick, out in zip(picks, outs):
            here = staged.at[pl.ds(pl.multiple_of(pick * BLOCK + start, PART), PART)]
            leaving.append(pltpu.make_async_copy(here, out.at[pl.ds(start, PART)], out_sems.at[len(leaving)]))
            leaving[-1].start()
    for copy in leaving:
        copy.wait()


PART = 128


def first_rows(slots, pick_blk, pick_sub, embeds):
    parts = BLOCK // PART
    return pl.pallas_call(
        functools.partial(first_kernel, slots),
        out_shape=[jax.ShapeDtypeStruct((BLOCK, embeds.shape[1]), embeds.dtype)] * len(slots),
        in_specs=[ANY] * 3,
        out_specs=[ANY] * len(slots),
        scratch_shapes=[
            pltpu.SMEM(pick_blk.shape, jnp.int32),
            pltpu.SMEM(pick_sub.shape, jnp.int32),
            pltpu.VMEM(embeds.shape, embeds.dtype),
            pltpu.SemaphoreType.DMA((2,)),
            pltpu.SemaphoreType.DMA((embeds.shape[0] // PART,)),
            pltpu.SemaphoreType.DMA((len(slots) * parts,)),
        ],
    )(pick_blk, pick_sub, embeds)


def pick_kernel(slots, pick_blk, pick_sub, embeds, *rest):
    outs, (blk_scalars, sub_scalars, scalar_sems, row_sems) = rest[: len(slots)], rest[len(slots) :]
    scalars = [
        pltpu.make_async_copy(pick_blk, blk_scalars, scalar_sems.at[0]),
        pltpu.make_async_copy(pick_sub, sub_scalars, scalar_sems.at[1]),
    ]
    for copy in scalars:
        copy.start()
    for copy in scalars:
        copy.wait()
    copies = []
    for place, (axis, step, first, rows) in enumerate(slots):
        pick = take_pick(axis, step, blk_scalars, sub_scalars)
        start = pl.multiple_of(pick * BLOCK + first, math.gcd(BLOCK, first))
        copies.append(pltpu.make_async_copy(embeds.at[pl.ds(start, rows)], outs[place], row_sems.at[place]))
        copies[-1].start()
    for copy in copies:
        copy.wait()


def pick_rows(slots, pick_blk, pick_sub, embeds):
    return pl.pallas_call(
        functools.partial(pick_kernel, slots),
        out_shape=[jax.ShapeDtypeStruct((rows, embeds.shape[1]), embeds.dtype) for _, _, _, rows in slots],
        in_specs=[HBM] * 3,
        out_specs=[VMEM] * len(slots),
        scratch_shapes=[
            pltpu.SMEM(pick_blk.shape, jnp.int32),
            pltpu.SMEM(pick_sub.shape, jnp.int32),
            pltpu.SemaphoreType.DMA((2,)),
            pltpu.SemaphoreType.DMA((len(slots),)),
        ],
        compiler_params=PARAMS,
    )(pick_blk, pick_sub, embeds)


def prepare_kernel(slots, pick_blk, pick_sub, mask_blk, mask_sub, embeds, units, live, mine):
    for start in range(0, embeds.shape[0], BLOCK):
        units[:, start : start + BLOCK] = rounded_units(embeds[start : start + BLOCK]).T
    count = live.shape[1]
    block_of = lax.broadcasted_iota(jnp.int32, mine.shape[1:], 0) // ROWS
    for place, (axis, step, _, _) in enumerate(slots):
        source = lax.axis_index(axis) ^ step
        mask = mask_blk if axis == "blk" else mask_sub
        for i in range(count):
            value = mask[0, source * count + i].astype(jnp.float32)
            live[place, i : i + 1] = jnp.full((1, LANES), value, jnp.float32)
        pick = take_pick(axis, step, pick_blk, pick_sub)
        mine[place] = (block_of == pick).astype(jnp.float32)


def prepare(slots, pick_blk, pick_sub, mask_blk, mask_sub, embeds):
    count = embeds.shape[0] // BLOCK
    return pl.pallas_call(
        functools.partial(prepare_kernel, slots),
        out_shape=[
            jax.ShapeDtypeStruct(embeds.shape[::-1], embeds.dtype),
            jax.ShapeDtypeStruct((len(slots), count, LANES), jnp.float32),
            jax.ShapeDtypeStruct((len(slots), count * ROWS, LANES), jnp.float32),
        ],
        in_specs=[SMEM] * 4 + [VMEM],
        out_specs=[VMEM] * 3,
        compiler_params=PARAMS,
    )(pick_blk, pick_sub, mask_blk, mask_sub, embeds)


def slot_kernel(place, first, rows, back_places, carries, arrived, units, live, mine, totals, *rest):
    new_totals, back = rest[-2:]
    count = live.shape[1]
    before = totals[...]
    for back_place, sums in zip(back_places, rest):
        before = before + mine[back_place] * sums[...]
    new_totals[...] = before
    x = rounded_units(arrived[...])
    along_rows = jnp.zeros((rows, LANES), jnp.float32)
    for i in range(count):
        cosines = jnp.dot(x, units[:, i * BLOCK : (i + 1) * BLOCK], preferred_element_type=jnp.float32)
        weights = soft_weights(cosines)
        alive = live[place, i : i + 1]
        parts = [weights[:, part * LANES : (part + 1) * LANES] for part in range(ROWS)]
        along_rows = along_rows + alive * sum(parts)
        for part, piece in enumerate(parts):
            row = i * ROWS + part
            new_totals[row : row + 1] = new_totals[row : row + 1] + alive * jnp.sum(piece, axis=0, keepdims=True)
    empty = [jnp.zeros((gap, LANES), jnp.float32) for gap in (first, BLOCK - first - rows)]
    along_rows = jnp.concatenate([part for part in (empty[0], along_rows, empty[1]) if part.shape[0]], axis=0)
    for part in range(ROWS):
        sums = jnp.sum(along_rows[part * LANES : (part + 1) * LANES].T, axis=0, keepdims=True)
        for i in range(count):
            row = i * ROWS + part
            back[row : row + 1] = sums + rest[-3][row : row + 1] if carries else sums


def work(place, slot, arrived, units, live, mine, totals, returned, carried):
    operands = [arrived, units, live, mine, totals] + [sums for _, sums in returned]
    operands += [] if carried is None else [carried]
    return pl.pallas_call(
        functools.partial(slot_kernel, place, *slot[2:], [one for one, _ in returned], carried is not None),
        out_shape=[jax.ShapeDtypeStruct(totals.shape, jnp.float32)] * 2,
        in_specs=[VMEM] * len(operands),
        out_specs=[VMEM] * 2,
        compiler_params=PARAMS,
    )(*operands)


BEHIND = 2
FIRST_CUT = 128


def plan_slots(sizes):
    slots = [("blk", 1, 0, BLOCK), ("sub", 2, 0, BLOCK), ("sub", 1, 0, BLOCK)]
    slots += [("blk", k, 0, BLOCK) for k in range(2, sizes["blk"])]
    for k in range(3, sizes["sub"]):
        slots += [("sub", k, 0, FIRST_CUT), ("sub", k, FIRST_CUT, BLOCK - FIRST_CUT)]
    return slots


AT_ONCE = 2


def body(embeds, pick_blk, mask_blk, pick_sub, mask_sub):
    count = embeds.shape[0] // BLOCK
    sizes = {"sub": lax.axis_size("sub"), "blk": lax.axis_size("blk")}
    slots = plan_slots(sizes)

    def send(array, slot):
        return lax.ppermute(array, slot[0], pairs(slot[1], sizes[slot[0]]))

    outgoing = first_rows(slots[:AT_ONCE], pick_blk, pick_sub, embeds)
    outgoing += pick_rows(slots[AT_ONCE:], pick_blk, pick_sub, embeds)
    arrived = [send(rows, slot) for rows, slot in zip(outgoing, slots)]

    units, live, mine = prepare(slots, pick_blk, pick_sub, mask_blk, mask_sub, embeds)
    totals = jnp.zeros((count * ROWS, LANES), jnp.float32)
    carried = {}
    waiting, late = [], []
    for place, slot in enumerate(slots):
        axis, step, first, rows = slot
        last = place == len(slots) - 1
        ready = [one for one in waiting if last or one[0] <= place]
        waiting = [one for one in waiting if not last and one[0] > place]
        totals, back = work(
            place, slot, arrived[place], units, live, mine, totals, [one[1:] for one in ready], carried.pop(slot[:2], None)
        )
        if first + rows < BLOCK:
            carried[axis, step] = back
        elif axis == "blk":
            waiting.append((place + BEHIND, place, send(back, slot)))
        else:
            late.append((place, send(back, slot)))
    for place, sums in late:
        totals = totals + mine[place] * sums
    return (totals * (1.0 / BLOCK)).reshape(-1)


def solution(mesh):
    return jax.shard_map(
        body,
        mesh=mesh,
        in_specs=(
            P(("groups", "blk", "sub"), None),
            P(("groups", "blk", "sub"), None),
            P(("groups", "blk", "sub"), None),
            P(("groups", "blk"), None),
            P(("groups", "blk", "sub"), None),
        ),
        out_specs=P(("groups", "blk", "sub")),
        check_vma=False,
    )
```

```python
import functools
import math

import jax
import jax.numpy as jnp
from jax import lax
from jax.experimental import pallas as pl
from jax.experimental.pallas import tpu as pltpu
from jax.sharding import PartitionSpec as P

BLOCK = 256
LANES = 128
ROWS = BLOCK // LANES

cutoff = 0.05
sharpness = 100.0

SMEM = pl.BlockSpec(memory_space=pltpu.SMEM)
VMEM = pl.BlockSpec(memory_space=pltpu.VMEM)
HBM = pl.BlockSpec(memory_space=pltpu.HBM)
ANY = pl.BlockSpec(memory_space=pl.ANY)
PARAMS = pltpu.CompilerParams(vmem_limit_bytes=32 * 2**20)


def pairs(axis, step, size):
    return [(i, i ^ step if axis == "blk" else (i + step) % size) for i in range(size)]


def target_and_source(axis, step, size):
    own = lax.axis_index(axis)
    if axis == "blk":
        return own ^ step, own ^ step
    return lax.rem(own + step, size), lax.rem(own + size - step, size)


def rounded_units(rows):
    wide = rows.astype(jnp.float32)
    scale = lax.rsqrt(jnp.sum(wide * wide, axis=1, keepdims=True) + 1e-06)
    return (wide * scale).astype(jnp.bfloat16)


def soft_weights(cosines):
    rate = sharpness * math.log2(math.e)
    return pltpu.reciprocal(1.0 + jnp.exp2(cutoff * rate - cosines * rate), approx=True)


def take_pick(axis, step, pick_blk, pick_sub):
    target, _ = target_and_source(axis, step, pick_sub.shape[1])
    return pick_blk[0, target] if axis == "blk" else pick_sub[lax.axis_index("sub"), target]


def first_kernel(slots, pick_blk, pick_sub, embeds, *rest):
    outs, (blk_scalars, sub_scalars, staged, scalar_sems, in_sems, out_sems) = rest[: len(slots)], rest[len(slots) :]
    scalars = [
        pltpu.make_async_copy(pick_blk, blk_scalars, scalar_sems.at[0]),
        pltpu.make_async_copy(pick_sub, sub_scalars, scalar_sems.at[1]),
    ]
    for copy in scalars:
        copy.start()
    starts = range(0, BLOCK, PART)
    entering = []
    for start in starts:
        for top in range(start, embeds.shape[0], BLOCK):
            rows = pl.ds(top, PART)
            entering.append(pltpu.make_async_copy(embeds.at[rows], staged.at[rows], in_sems.at[len(entering)]))
            entering[-1].start()
    for copy in scalars:
        copy.wait()
    picks = [take_pick(axis, step, blk_scalars, sub_scalars) for axis, step, _, _ in slots]
    count = embeds.shape[0] // BLOCK
    leaving = []
    for turn, start in enumerate(starts):
        for copy in entering[turn * count : (turn + 1) * count]:
            copy.wait()
        for pick, out in zip(picks, outs):
            here = staged.at[pl.ds(pl.multiple_of(pick * BLOCK + start, PART), PART)]
            leaving.append(pltpu.make_async_copy(here, out.at[pl.ds(start, PART)], out_sems.at[len(leaving)]))
            leaving[-1].start()
    for copy in leaving:
        copy.wait()


PART = 128


def first_rows(slots, pick_blk, pick_sub, embeds):
    parts = BLOCK // PART
    return pl.pallas_call(
        functools.partial(first_kernel, slots),
        out_shape=[jax.ShapeDtypeStruct((BLOCK, embeds.shape[1]), embeds.dtype)] * len(slots),
        in_specs=[ANY] * 3,
        out_specs=[ANY] * len(slots),
        scratch_shapes=[
            pltpu.SMEM(pick_blk.shape, jnp.int32),
            pltpu.SMEM(pick_sub.shape, jnp.int32),
            pltpu.VMEM(embeds.shape, embeds.dtype),
            pltpu.SemaphoreType.DMA((2,)),
            pltpu.SemaphoreType.DMA((embeds.shape[0] // PART,)),
            pltpu.SemaphoreType.DMA((len(slots) * parts,)),
        ],
    )(pick_blk, pick_sub, embeds)


def pick_kernel(slots, pick_blk, pick_sub, embeds, *rest):
    outs, (blk_scalars, sub_scalars, scalar_sems, row_sems) = rest[: len(slots)], rest[len(slots) :]
    scalars = [
        pltpu.make_async_copy(pick_blk, blk_scalars, scalar_sems.at[0]),
        pltpu.make_async_copy(pick_sub, sub_scalars, scalar_sems.at[1]),
    ]
    for copy in scalars:
        copy.start()
    for copy in scalars:
        copy.wait()
    copies = []
    for place, (axis, step, first, rows) in enumerate(slots):
        pick = take_pick(axis, step, blk_scalars, sub_scalars)
        start = pl.multiple_of(pick * BLOCK + first, math.gcd(BLOCK, first))
        copies.append(pltpu.make_async_copy(embeds.at[pl.ds(start, rows)], outs[place], row_sems.at[place]))
        copies[-1].start()
    for copy in copies:
        copy.wait()


def pick_rows(slots, pick_blk, pick_sub, embeds):
    return pl.pallas_call(
        functools.partial(pick_kernel, slots),
        out_shape=[jax.ShapeDtypeStruct((rows, embeds.shape[1]), embeds.dtype) for _, _, _, rows in slots],
        in_specs=[HBM] * 3,
        out_specs=[VMEM] * len(slots),
        scratch_shapes=[
            pltpu.SMEM(pick_blk.shape, jnp.int32),
            pltpu.SMEM(pick_sub.shape, jnp.int32),
            pltpu.SemaphoreType.DMA((2,)),
            pltpu.SemaphoreType.DMA((len(slots),)),
        ],
        compiler_params=PARAMS,
    )(pick_blk, pick_sub, embeds)


def prepare_kernel(slots, pick_blk, pick_sub, mask_blk, mask_sub, embeds, units, live, mine):
    for start in range(0, embeds.shape[0], BLOCK):
        units[:, start : start + BLOCK] = rounded_units(embeds[start : start + BLOCK]).T
    count = live.shape[1]
    block_of = lax.broadcasted_iota(jnp.int32, mine.shape[1:], 0) // ROWS
    for place, (axis, step, _, _) in enumerate(slots):
        mask = mask_blk if axis == "blk" else mask_sub
        _, source = target_and_source(axis, step, mask.shape[1] // count)
        for i in range(count):
            value = mask[0, source * count + i].astype(jnp.float32)
            live[place, i : i + 1] = jnp.full((1, LANES), value, jnp.float32)
        pick = take_pick(axis, step, pick_blk, pick_sub)
        mine[place] = (block_of == pick).astype(jnp.float32)


def prepare(slots, pick_blk, pick_sub, mask_blk, mask_sub, embeds):
    count = embeds.shape[0] // BLOCK
    return pl.pallas_call(
        functools.partial(prepare_kernel, slots),
        out_shape=[
            jax.ShapeDtypeStruct(embeds.shape[::-1], embeds.dtype),
            jax.ShapeDtypeStruct((len(slots), count, LANES), jnp.float32),
            jax.ShapeDtypeStruct((len(slots), count * ROWS, LANES), jnp.float32),
        ],
        in_specs=[SMEM] * 4 + [VMEM],
        out_specs=[VMEM] * 3,
        compiler_params=PARAMS,
    )(pick_blk, pick_sub, mask_blk, mask_sub, embeds)


def slot_kernel(place, first, rows, back_places, carries, arrived, units, live, mine, totals, *rest):
    new_totals, back = rest[-2:]
    count = live.shape[1]
    before = totals[...]
    for back_place, sums in zip(back_places, rest):
        before = before + mine[back_place] * sums[...]
    new_totals[...] = before
    x = rounded_units(arrived[...])
    along_rows = jnp.zeros((rows, LANES), jnp.float32)
    for i in range(count):
        cosines = jnp.dot(x, units[:, i * BLOCK : (i + 1) * BLOCK], preferred_element_type=jnp.float32)
        weights = soft_weights(cosines)
        alive = live[place, i : i + 1]
        parts = [weights[:, part * LANES : (part + 1) * LANES] for part in range(ROWS)]
        along_rows = along_rows + alive * sum(parts)
        for part, piece in enumerate(parts):
            row = i * ROWS + part
            new_totals[row : row + 1] = new_totals[row : row + 1] + alive * jnp.sum(piece, axis=0, keepdims=True)
    empty = [jnp.zeros((gap, LANES), jnp.float32) for gap in (first, BLOCK - first - rows)]
    along_rows = jnp.concatenate([part for part in (empty[0], along_rows, empty[1]) if part.shape[0]], axis=0)
    for part in range(ROWS):
        sums = jnp.sum(along_rows[part * LANES : (part + 1) * LANES].T, axis=0, keepdims=True)
        for i in range(count):
            row = i * ROWS + part
            back[row : row + 1] = sums + rest[-3][row : row + 1] if carries else sums


def work(place, slot, arrived, units, live, mine, totals, returned, carried):
    operands = [arrived, units, live, mine, totals] + [sums for _, sums in returned]
    operands += [] if carried is None else [carried]
    return pl.pallas_call(
        functools.partial(slot_kernel, place, *slot[2:], [one for one, _ in returned], carried is not None),
        out_shape=[jax.ShapeDtypeStruct(totals.shape, jnp.float32)] * 2,
        in_specs=[VMEM] * len(operands),
        out_specs=[VMEM] * 2,
        compiler_params=PARAMS,
    )(*operands)


BEHIND = 2
FIRST_CUT = 128


def plan_slots(sizes):
    slots = [("blk", 1, 0, BLOCK), ("sub", 2, 0, BLOCK), ("sub", sizes["sub"] - 1, 0, BLOCK)]
    slots += [("blk", k, 0, BLOCK) for k in range(2, sizes["blk"])]
    for k in (1, *range(3, sizes["sub"] - 1)):
        slots += [("sub", k, 0, FIRST_CUT), ("sub", k, FIRST_CUT, BLOCK - FIRST_CUT)]
    return slots


AT_ONCE = 2


def body(embeds, pick_blk, mask_blk, pick_sub, mask_sub):
    count = embeds.shape[0] // BLOCK
    sizes = {"sub": lax.axis_size("sub"), "blk": lax.axis_size("blk")}
    slots = plan_slots(sizes)

    def send(array, slot, back=False):
        axis, step, _, _ = slot
        there = pairs(axis, step, sizes[axis])
        return lax.ppermute(array, axis, [(b, a) for a, b in there] if back else there)

    outgoing = first_rows(slots[:AT_ONCE], pick_blk, pick_sub, embeds)
    outgoing += pick_rows(slots[AT_ONCE:], pick_blk, pick_sub, embeds)
    arrived = [send(rows, slot) for rows, slot in zip(outgoing, slots)]

    units, live, mine = prepare(slots, pick_blk, pick_sub, mask_blk, mask_sub, embeds)
    totals = jnp.zeros((count * ROWS, LANES), jnp.float32)
    carried = {}
    waiting, late = [], []
    for place, slot in enumerate(slots):
        axis, step, first, rows = slot
        last = place == len(slots) - 1
        ready = [one for one in waiting if last or one[0] <= place]
        waiting = [one for one in waiting if not last and one[0] > place]
        totals, back = work(
            place, slot, arrived[place], units, live, mine, totals, [one[1:] for one in ready], carried.pop(slot[:2], None)
        )
        if first + rows < BLOCK:
            carried[axis, step] = back
        elif axis == "blk":
            waiting.append((place + BEHIND, place, send(back, slot, back=True)))
        else:
            late.append((place, send(back, slot, back=True)))
    for place, sums in late:
        totals = totals + mine[place] * sums
    return (totals * (1.0 / BLOCK)).reshape(-1)


def solution(mesh):
    return jax.shard_map(
        body,
        mesh=mesh,
        in_specs=(
            P(("groups", "blk", "sub"), None),
            P(("groups", "blk", "sub"), None),
            P(("groups", "blk", "sub"), None),
            P(("groups", "blk"), None),
            P(("groups", "blk", "sub"), None),
        ),
        out_specs=P(("groups", "blk", "sub")),
        check_vma=False,
    )
```

```python
import functools
import math

import jax
import jax.numpy as jnp
from jax import lax
from jax.experimental import pallas as pl
from jax.experimental.pallas import tpu as pltpu
from jax.sharding import PartitionSpec as P

BLOCK = 256
LANES = 128
ROWS = BLOCK // LANES

cutoff = 0.05
sharpness = 100.0

SMEM = pl.BlockSpec(memory_space=pltpu.SMEM)
VMEM = pl.BlockSpec(memory_space=pltpu.VMEM)
HBM = pl.BlockSpec(memory_space=pltpu.HBM)
ANY = pl.BlockSpec(memory_space=pl.ANY)
PARAMS = pltpu.CompilerParams(vmem_limit_bytes=32 * 2**20)


def pairs(step, size):
    return [(i, i ^ step) for i in range(size)]


def rounded_units(rows):
    wide = rows.astype(jnp.float32)
    scale = lax.rsqrt(jnp.sum(wide * wide, axis=1, keepdims=True) + 1e-06)
    return (wide * scale).astype(jnp.bfloat16)


def soft_weights(cosines):
    rate = sharpness * math.log2(math.e)
    return pltpu.reciprocal(1.0 + jnp.exp2(cutoff * rate - cosines * rate), approx=True)


def take_pick(axis, step, pick_blk, pick_sub):
    target = lax.axis_index(axis) ^ step
    return pick_blk[0, target] if axis == "blk" else pick_sub[lax.axis_index("sub"), target]


def first_kernel(slots, pick_blk, pick_sub, embeds, *rest):
    outs, (blk_scalars, sub_scalars, staged, scalar_sems, in_sems, out_sems) = rest[: len(slots)], rest[len(slots) :]
    scalars = [
        pltpu.make_async_copy(pick_blk, blk_scalars, scalar_sems.at[0]),
        pltpu.make_async_copy(pick_sub, sub_scalars, scalar_sems.at[1]),
    ]
    for copy in scalars:
        copy.start()
    starts = range(0, BLOCK, PART)
    entering = []
    for start in starts:
        for top in range(start, embeds.shape[0], BLOCK):
            rows = pl.ds(top, PART)
            entering.append(pltpu.make_async_copy(embeds.at[rows], staged.at[rows], in_sems.at[len(entering)]))
            entering[-1].start()
    for copy in scalars:
        copy.wait()
    picks = [take_pick(axis, step, blk_scalars, sub_scalars) for axis, step, _, _ in slots]
    count = embeds.shape[0] // BLOCK
    leaving = []
    for turn, start in enumerate(starts):
        for copy in entering[turn * count : (turn + 1) * count]:
            copy.wait()
        for pick, out in zip(picks, outs):
            here = staged.at[pl.ds(pl.multiple_of(pick * BLOCK + start, PART), PART)]
            leaving.append(pltpu.make_async_copy(here, out.at[pl.ds(start, PART)], out_sems.at[len(leaving)]))
            leaving[-1].start()
    for copy in leaving:
        copy.wait()


PART = 128


def first_rows(slots, pick_blk, pick_sub, embeds):
    parts = BLOCK // PART
    return pl.pallas_call(
        functools.partial(first_kernel, slots),
        out_shape=[jax.ShapeDtypeStruct((BLOCK, embeds.shape[1]), embeds.dtype)] * len(slots),
        in_specs=[ANY] * 3,
        out_specs=[ANY] * len(slots),
        scratch_shapes=[
            pltpu.SMEM(pick_blk.shape, jnp.int32),
            pltpu.SMEM(pick_sub.shape, jnp.int32),
            pltpu.VMEM(embeds.shape, embeds.dtype),
            pltpu.SemaphoreType.DMA((2,)),
            pltpu.SemaphoreType.DMA((embeds.shape[0] // PART,)),
            pltpu.SemaphoreType.DMA((len(slots) * parts,)),
        ],
    )(pick_blk, pick_sub, embeds)


def pick_kernel(slots, pick_blk, pick_sub, embeds, *rest):
    outs, (blk_scalars, sub_scalars, scalar_sems, row_sems) = rest[: len(slots)], rest[len(slots) :]
    scalars = [
        pltpu.make_async_copy(pick_blk, blk_scalars, scalar_sems.at[0]),
        pltpu.make_async_copy(pick_sub, sub_scalars, scalar_sems.at[1]),
    ]
    for copy in scalars:
        copy.start()
    for copy in scalars:
        copy.wait()
    copies = []
    for place, (axis, step, first, rows) in enumerate(slots):
        pick = take_pick(axis, step, blk_scalars, sub_scalars)
        start = pl.multiple_of(pick * BLOCK + first, math.gcd(BLOCK, first))
        copies.append(pltpu.make_async_copy(embeds.at[pl.ds(start, rows)], outs[place], row_sems.at[place]))
        copies[-1].start()
    for copy in copies:
        copy.wait()


def pick_rows(slots, pick_blk, pick_sub, embeds):
    return pl.pallas_call(
        functools.partial(pick_kernel, slots),
        out_shape=[jax.ShapeDtypeStruct((rows, embeds.shape[1]), embeds.dtype) for _, _, _, rows in slots],
        in_specs=[HBM] * 3,
        out_specs=[VMEM] * len(slots),
        scratch_shapes=[
            pltpu.SMEM(pick_blk.shape, jnp.int32),
            pltpu.SMEM(pick_sub.shape, jnp.int32),
            pltpu.SemaphoreType.DMA((2,)),
            pltpu.SemaphoreType.DMA((len(slots),)),
        ],
        compiler_params=PARAMS,
    )(pick_blk, pick_sub, embeds)


def prepare_kernel(slots, pick_blk, pick_sub, mask_blk, mask_sub, embeds, units, live, mine):
    for start in range(0, embeds.shape[0], BLOCK):
        units[:, start : start + BLOCK] = rounded_units(embeds[start : start + BLOCK]).T
    count = live.shape[1]
    block_of = lax.broadcasted_iota(jnp.int32, mine.shape[1:], 0) // ROWS
    for place, (axis, step, _, _) in enumerate(slots):
        source = lax.axis_index(axis) ^ step
        mask = mask_blk if axis == "blk" else mask_sub
        for i in range(count):
            value = mask[0, source * count + i].astype(jnp.float32)
            live[place, i : i + 1] = jnp.full((1, LANES), value, jnp.float32)
        pick = take_pick(axis, step, pick_blk, pick_sub)
        mine[place] = (block_of == pick).astype(jnp.float32)


def prepare(slots, pick_blk, pick_sub, mask_blk, mask_sub, embeds):
    count = embeds.shape[0] // BLOCK
    return pl.pallas_call(
        functools.partial(prepare_kernel, slots),
        out_shape=[
            jax.ShapeDtypeStruct(embeds.shape[::-1], embeds.dtype),
            jax.ShapeDtypeStruct((len(slots), count, LANES), jnp.float32),
            jax.ShapeDtypeStruct((len(slots), count * ROWS, LANES), jnp.float32),
        ],
        in_specs=[SMEM] * 4 + [VMEM],
        out_specs=[VMEM] * 3,
        compiler_params=PARAMS,
    )(pick_blk, pick_sub, mask_blk, mask_sub, embeds)


def slot_kernel(place, first, rows, back_places, carries, arrived, units, live, mine, totals, *rest):
    new_totals, back = rest[-2:]
    count = live.shape[1]
    before = totals[...]
    for back_place, sums in zip(back_places, rest):
        before = before + mine[back_place] * sums[...]
    new_totals[...] = before
    x = rounded_units(arrived[...])
    along_rows = jnp.zeros((rows, LANES), jnp.float32)
    for i in range(count):
        cosines = jnp.dot(x, units[:, i * BLOCK : (i + 1) * BLOCK], preferred_element_type=jnp.float32)
        weights = soft_weights(cosines)
        alive = live[place, i : i + 1]
        parts = [weights[:, part * LANES : (part + 1) * LANES] for part in range(ROWS)]
        along_rows = along_rows + alive * sum(parts)
        for part, piece in enumerate(parts):
            row = i * ROWS + part
            new_totals[row : row + 1] = new_totals[row : row + 1] + alive * jnp.sum(piece, axis=0, keepdims=True)
    empty = [jnp.zeros((gap, LANES), jnp.float32) for gap in (first, BLOCK - first - rows)]
    along_rows = jnp.concatenate([part for part in (empty[0], along_rows, empty[1]) if part.shape[0]], axis=0)
    for part in range(ROWS):
        sums = jnp.sum(along_rows[part * LANES : (part + 1) * LANES].T, axis=0, keepdims=True)
        for i in range(count):
            row = i * ROWS + part
            back[row : row + 1] = sums + rest[-3][row : row + 1] if carries else sums


def work(place, slot, arrived, units, live, mine, totals, returned, carried):
    operands = [arrived, units, live, mine, totals] + [sums for _, sums in returned]
    operands += [] if carried is None else [carried]
    return pl.pallas_call(
        functools.partial(slot_kernel, place, *slot[2:], [one for one, _ in returned], carried is not None),
        out_shape=[jax.ShapeDtypeStruct(totals.shape, jnp.float32)] * 2,
        in_specs=[VMEM] * len(operands),
        out_specs=[VMEM] * 2,
        compiler_params=PARAMS,
    )(*operands)


BEHIND = 2
FIRST_CUT = 240


def plan_slots(sizes):
    slots = [("sub", 2, 0, BLOCK), ("sub", 1, 0, BLOCK), ("blk", 1, 0, BLOCK), ("blk", 2, 0, BLOCK)]
    for k in range(3, sizes["blk"]):
        slots += [("blk", k, 0, FIRST_CUT), ("blk", k, FIRST_CUT, BLOCK - FIRST_CUT)]
    return slots + [("sub", k, 0, BLOCK) for k in range(3, sizes["sub"])]


AT_ONCE = 1


def body(embeds, pick_blk, mask_blk, pick_sub, mask_sub):
    count = embeds.shape[0] // BLOCK
    sizes = {"sub": lax.axis_size("sub"), "blk": lax.axis_size("blk")}
    slots = plan_slots(sizes)

    def send(array, slot):
        return lax.ppermute(array, slot[0], pairs(slot[1], sizes[slot[0]]))

    outgoing = first_rows(slots[:AT_ONCE], pick_blk, pick_sub, embeds)
    outgoing += pick_rows(slots[AT_ONCE:], pick_blk, pick_sub, embeds)
    arrived = [send(rows, slot) for rows, slot in zip(outgoing, slots)]

    units, live, mine = prepare(slots, pick_blk, pick_sub, mask_blk, mask_sub, embeds)
    totals = jnp.zeros((count * ROWS, LANES), jnp.float32)
    carried = {}
    waiting, late = [], []
    for place, slot in enumerate(slots):
        axis, step, first, rows = slot
        last = place == len(slots) - 1
        ready = [one for one in waiting if last or one[0] <= place]
        waiting = [one for one in waiting if not last and one[0] > place]
        totals, back = work(
            place, slot, arrived[place], units, live, mine, totals, [one[1:] for one in ready], carried.pop(slot[:2], None)
        )
        if first + rows < BLOCK:
            carried[axis, step] = back
        elif axis == "blk":
            waiting.append((place + BEHIND, place, send(back, slot)))
        else:
            late.append((place, send(back, slot)))
    for place, sums in late:
        totals = totals + mine[place] * sums
    return (totals * (1.0 / BLOCK)).reshape(-1)


def solution(mesh):
    return jax.shard_map(
        body,
        mesh=mesh,
        in_specs=(
            P(("groups", "blk", "sub"), None),
            P(("groups", "blk", "sub"), None),
            P(("groups", "blk", "sub"), None),
            P(("groups", "blk"), None),
            P(("groups", "blk", "sub"), None),
        ),
        out_specs=P(("groups", "blk", "sub")),
        check_vma=False,
    )
```

```python
import functools
import math

import jax
import jax.numpy as jnp
from jax import lax
from jax.experimental import pallas as pl
from jax.experimental.pallas import tpu as pltpu
from jax.sharding import PartitionSpec as P

BLOCK = 256
LANES = 128
ROWS = BLOCK // LANES

cutoff = 0.05
sharpness = 100.0

SMEM = pl.BlockSpec(memory_space=pltpu.SMEM)
VMEM = pl.BlockSpec(memory_space=pltpu.VMEM)
HBM = pl.BlockSpec(memory_space=pltpu.HBM)
ANY = pl.BlockSpec(memory_space=pl.ANY)
PARAMS = pltpu.CompilerParams(vmem_limit_bytes=32 * 2**20)


def pairs(step, size):
    return [(i, i ^ step) for i in range(size)]


def rounded_units(rows):
    wide = rows.astype(jnp.float32)
    scale = lax.rsqrt(jnp.sum(wide * wide, axis=1, keepdims=True) + 1e-06)
    return (wide * scale).astype(jnp.bfloat16)


def soft_weights(cosines):
    rate = sharpness * math.log2(math.e)
    return pltpu.reciprocal(1.0 + jnp.exp2(cutoff * rate - cosines * rate), approx=True)


def take_pick(axis, step, pick_blk, pick_sub):
    target = lax.axis_index(axis) ^ step
    return pick_blk[0, target] if axis == "blk" else pick_sub[lax.axis_index("sub"), target]


def first_kernel(slots, pick_blk, pick_sub, embeds, *rest):
    outs, (blk_scalars, sub_scalars, staged, scalar_sems, in_sems, out_sems) = rest[: len(slots)], rest[len(slots) :]
    scalars = [
        pltpu.make_async_copy(pick_blk, blk_scalars, scalar_sems.at[0]),
        pltpu.make_async_copy(pick_sub, sub_scalars, scalar_sems.at[1]),
    ]
    for copy in scalars:
        copy.start()
    starts = range(0, BLOCK, PART)
    entering = []
    for start in starts:
        for top in range(start, embeds.shape[0], BLOCK):
            rows = pl.ds(top, PART)
            entering.append(pltpu.make_async_copy(embeds.at[rows], staged.at[rows], in_sems.at[len(entering)]))
            entering[-1].start()
    for copy in scalars:
        copy.wait()
    picks = [take_pick(axis, step, blk_scalars, sub_scalars) for axis, step, _, _ in slots]
    count = embeds.shape[0] // BLOCK
    leaving = []
    for turn, start in enumerate(starts):
        for copy in entering[turn * count : (turn + 1) * count]:
            copy.wait()
        for pick, out in zip(picks, outs):
            here = staged.at[pl.ds(pl.multiple_of(pick * BLOCK + start, PART), PART)]
            leaving.append(pltpu.make_async_copy(here, out.at[pl.ds(start, PART)], out_sems.at[len(leaving)]))
            leaving[-1].start()
    for copy in leaving:
        copy.wait()


PART = 128


def first_rows(slots, pick_blk, pick_sub, embeds):
    parts = BLOCK // PART
    return pl.pallas_call(
        functools.partial(first_kernel, slots),
        out_shape=[jax.ShapeDtypeStruct((BLOCK, embeds.shape[1]), embeds.dtype)] * len(slots),
        in_specs=[ANY] * 3,
        out_specs=[ANY] * len(slots),
        scratch_shapes=[
            pltpu.SMEM(pick_blk.shape, jnp.int32),
            pltpu.SMEM(pick_sub.shape, jnp.int32),
            pltpu.VMEM(embeds.shape, embeds.dtype),
            pltpu.SemaphoreType.DMA((2,)),
            pltpu.SemaphoreType.DMA((embeds.shape[0] // PART,)),
            pltpu.SemaphoreType.DMA((len(slots) * parts,)),
        ],
    )(pick_blk, pick_sub, embeds)


def pick_kernel(slots, pick_blk, pick_sub, embeds, *rest):
    outs, (blk_scalars, sub_scalars, scalar_sems, row_sems) = rest[: len(slots)], rest[len(slots) :]
    scalars = [
        pltpu.make_async_copy(pick_blk, blk_scalars, scalar_sems.at[0]),
        pltpu.make_async_copy(pick_sub, sub_scalars, scalar_sems.at[1]),
    ]
    for copy in scalars:
        copy.start()
    for copy in scalars:
        copy.wait()
    copies = []
    for place, (axis, step, first, rows) in enumerate(slots):
        pick = take_pick(axis, step, blk_scalars, sub_scalars)
        start = pl.multiple_of(pick * BLOCK + first, math.gcd(BLOCK, first))
        copies.append(pltpu.make_async_copy(embeds.at[pl.ds(start, rows)], outs[place], row_sems.at[place]))
        copies[-1].start()
    for copy in copies:
        copy.wait()


def pick_rows(slots, pick_blk, pick_sub, embeds):
    return pl.pallas_call(
        functools.partial(pick_kernel, slots),
        out_shape=[jax.ShapeDtypeStruct((rows, embeds.shape[1]), embeds.dtype) for _, _, _, rows in slots],
        in_specs=[HBM] * 3,
        out_specs=[VMEM] * len(slots),
        scratch_shapes=[
            pltpu.SMEM(pick_blk.shape, jnp.int32),
            pltpu.SMEM(pick_sub.shape, jnp.int32),
            pltpu.SemaphoreType.DMA((2,)),
            pltpu.SemaphoreType.DMA((len(slots),)),
        ],
        compiler_params=PARAMS,
    )(pick_blk, pick_sub, embeds)


def prepare_kernel(slots, pick_blk, pick_sub, mask_blk, mask_sub, embeds, units, live, mine):
    for start in range(0, embeds.shape[0], BLOCK):
        units[:, start : start + BLOCK] = rounded_units(embeds[start : start + BLOCK]).T
    count = live.shape[1]
    block_of = lax.broadcasted_iota(jnp.int32, mine.shape[1:], 0) // ROWS
    for place, (axis, step, _, _) in enumerate(slots):
        source = lax.axis_index(axis) ^ step
        mask = mask_blk if axis == "blk" else mask_sub
        for i in range(count):
            value = mask[0, source * count + i].astype(jnp.float32)
            live[place, i : i + 1] = jnp.full((1, LANES), value, jnp.float32)
        pick = take_pick(axis, step, pick_blk, pick_sub)
        mine[place] = (block_of == pick).astype(jnp.float32)


def prepare(slots, pick_blk, pick_sub, mask_blk, mask_sub, embeds):
    count = embeds.shape[0] // BLOCK
    return pl.pallas_call(
        functools.partial(prepare_kernel, slots),
        out_shape=[
            jax.ShapeDtypeStruct(embeds.shape[::-1], embeds.dtype),
            jax.ShapeDtypeStruct((len(slots), count, LANES), jnp.float32),
            jax.ShapeDtypeStruct((len(slots), count * ROWS, LANES), jnp.float32),
        ],
        in_specs=[SMEM] * 4 + [VMEM],
        out_specs=[VMEM] * 3,
        compiler_params=PARAMS,
    )(pick_blk, pick_sub, mask_blk, mask_sub, embeds)


def slot_kernel(place, first, rows, back_places, carries, arrived, units, live, mine, totals, *rest):
    new_totals, back = rest[-2:]
    count = live.shape[1]
    before = totals[...]
    for back_place, sums in zip(back_places, rest):
        before = before + mine[back_place] * sums[...]
    new_totals[...] = before
    x = rounded_units(arrived[...])
    along_rows = jnp.zeros((rows, LANES), jnp.float32)
    for i in range(count):
        cosines = jnp.dot(x, units[:, i * BLOCK : (i + 1) * BLOCK], preferred_element_type=jnp.float32)
        weights = soft_weights(cosines)
        alive = live[place, i : i + 1]
        parts = [weights[:, part * LANES : (part + 1) * LANES] for part in range(ROWS)]
        along_rows = along_rows + alive * sum(parts)
        for part, piece in enumerate(parts):
            row = i * ROWS + part
            new_totals[row : row + 1] = new_totals[row : row + 1] + alive * jnp.sum(piece, axis=0, keepdims=True)
    empty = [jnp.zeros((gap, LANES), jnp.float32) for gap in (first, BLOCK - first - rows)]
    along_rows = jnp.concatenate([part for part in (empty[0], along_rows, empty[1]) if part.shape[0]], axis=0)
    for part in range(ROWS):
        sums = jnp.sum(along_rows[part * LANES : (part + 1) * LANES].T, axis=0, keepdims=True)
        for i in range(count):
            row = i * ROWS + part
            back[row : row + 1] = sums + rest[-3][row : row + 1] if carries else sums


def work(place, slot, arrived, units, live, mine, totals, returned, carried):
    operands = [arrived, units, live, mine, totals] + [sums for _, sums in returned]
    operands += [] if carried is None else [carried]
    return pl.pallas_call(
        functools.partial(slot_kernel, place, *slot[2:], [one for one, _ in returned], carried is not None),
        out_shape=[jax.ShapeDtypeStruct(totals.shape, jnp.float32)] * 2,
        in_specs=[VMEM] * len(operands),
        out_specs=[VMEM] * 2,
        compiler_params=PARAMS,
    )(*operands)


BEHIND = 2
LAST_CUTS = ((0, 128), (128, 112), (240, 16))


def plan_slots(sizes):
    slots = [("blk", 1, 0, BLOCK), ("sub", 2, 0, BLOCK), ("sub", 1, 0, BLOCK)]
    slots += [("blk", k, 0, BLOCK) for k in range(2, sizes["blk"])]
    for k in range(3, sizes["sub"]):
        slots += [("sub", k, first, rows) for first, rows in LAST_CUTS]
    return slots


AT_ONCE = 2


def body(embeds, pick_blk, mask_blk, pick_sub, mask_sub):
    count = embeds.shape[0] // BLOCK
    sizes = {"sub": lax.axis_size("sub"), "blk": lax.axis_size("blk")}
    slots = plan_slots(sizes)

    def send(array, slot):
        return lax.ppermute(array, slot[0], pairs(slot[1], sizes[slot[0]]))

    outgoing = first_rows(slots[:AT_ONCE], pick_blk, pick_sub, embeds)
    outgoing += pick_rows(slots[AT_ONCE:], pick_blk, pick_sub, embeds)
    arrived = [send(rows, slot) for rows, slot in zip(outgoing, slots)]

    units, live, mine = prepare(slots, pick_blk, pick_sub, mask_blk, mask_sub, embeds)
    totals = jnp.zeros((count * ROWS, LANES), jnp.float32)
    carried = {}
    waiting, late = [], []
    for place, slot in enumerate(slots):
        axis, step, first, rows = slot
        last = place == len(slots) - 1
        ready = [one for one in waiting if last or one[0] <= place]
        waiting = [one for one in waiting if not last and one[0] > place]
        totals, back = work(
            place, slot, arrived[place], units, live, mine, totals, [one[1:] for one in ready], carried.pop(slot[:2], None)
        )
        if first + rows < BLOCK:
            carried[axis, step] = back
        elif axis == "blk":
            waiting.append((place + BEHIND, place, send(back, slot)))
        else:
            late.append((place, send(back, slot)))
    for place, sums in late:
        totals = totals + mine[place] * sums
    return (totals * (1.0 / BLOCK)).reshape(-1)


def solution(mesh):
    return jax.shard_map(
        body,
        mesh=mesh,
        in_specs=(
            P(("groups", "blk", "sub"), None),
            P(("groups", "blk", "sub"), None),
            P(("groups", "blk", "sub"), None),
            P(("groups", "blk"), None),
            P(("groups", "blk", "sub"), None),
        ),
        out_specs=P(("groups", "blk", "sub")),
        check_vma=False,
    )
```

```python
import functools
import math

import jax
import jax.numpy as jnp
from jax import lax
from jax.experimental import pallas as pl
from jax.experimental.pallas import tpu as pltpu
from jax.sharding import PartitionSpec as P

BLOCK = 256
LANES = 128
ROWS = BLOCK // LANES

cutoff = 0.05
sharpness = 100.0

SMEM = pl.BlockSpec(memory_space=pltpu.SMEM)
VMEM = pl.BlockSpec(memory_space=pltpu.VMEM)
HBM = pl.BlockSpec(memory_space=pltpu.HBM)
ANY = pl.BlockSpec(memory_space=pl.ANY)
PARAMS = pltpu.CompilerParams(vmem_limit_bytes=32 * 2**20)


def pairs(step, size):
    return [(i, i ^ step) for i in range(size)]


def rounded_units(rows):
    wide = rows.astype(jnp.float32)
    scale = lax.rsqrt(jnp.sum(wide * wide, axis=1, keepdims=True) + 1e-06)
    return (wide * scale).astype(jnp.bfloat16)


def soft_weights(cosines):
    rate = sharpness * math.log2(math.e)
    return pltpu.reciprocal(1.0 + jnp.exp2(cutoff * rate - cosines * rate), approx=True)


def take_pick(axis, step, pick_blk, pick_sub):
    target = lax.axis_index(axis) ^ step
    return pick_blk[0, target] if axis == "blk" else pick_sub[lax.axis_index("sub"), target]


def first_kernel(slots, pick_blk, pick_sub, embeds, *rest):
    outs, (blk_scalars, sub_scalars, staged, scalar_sems, in_sems, out_sems) = rest[: len(slots)], rest[len(slots) :]
    scalars = [
        pltpu.make_async_copy(pick_blk, blk_scalars, scalar_sems.at[0]),
        pltpu.make_async_copy(pick_sub, sub_scalars, scalar_sems.at[1]),
    ]
    for copy in scalars:
        copy.start()
    starts = range(0, BLOCK, PART)
    entering = []
    for start in starts:
        for top in range(start, embeds.shape[0], BLOCK):
            rows = pl.ds(top, PART)
            entering.append(pltpu.make_async_copy(embeds.at[rows], staged.at[rows], in_sems.at[len(entering)]))
            entering[-1].start()
    for copy in scalars:
        copy.wait()
    picks = [take_pick(axis, step, blk_scalars, sub_scalars) for axis, step, _, _ in slots]
    count = embeds.shape[0] // BLOCK
    leaving = []
    for turn, start in enumerate(starts):
        for copy in entering[turn * count : (turn + 1) * count]:
            copy.wait()
        for pick, out in zip(picks, outs):
            here = staged.at[pl.ds(pl.multiple_of(pick * BLOCK + start, PART), PART)]
            leaving.append(pltpu.make_async_copy(here, out.at[pl.ds(start, PART)], out_sems.at[len(leaving)]))
            leaving[-1].start()
    for copy in leaving:
        copy.wait()


PART = 128


def first_rows(slots, pick_blk, pick_sub, embeds):
    parts = BLOCK // PART
    return pl.pallas_call(
        functools.partial(first_kernel, slots),
        out_shape=[jax.ShapeDtypeStruct((BLOCK, embeds.shape[1]), embeds.dtype)] * len(slots),
        in_specs=[ANY] * 3,
        out_specs=[ANY] * len(slots),
        scratch_shapes=[
            pltpu.SMEM(pick_blk.shape, jnp.int32),
            pltpu.SMEM(pick_sub.shape, jnp.int32),
            pltpu.VMEM(embeds.shape, embeds.dtype),
            pltpu.SemaphoreType.DMA((2,)),
            pltpu.SemaphoreType.DMA((embeds.shape[0] // PART,)),
            pltpu.SemaphoreType.DMA((len(slots) * parts,)),
        ],
    )(pick_blk, pick_sub, embeds)


def pick_kernel(slots, pick_blk, pick_sub, embeds, *rest):
    outs, (blk_scalars, sub_scalars, scalar_sems, row_sems) = rest[: len(slots)], rest[len(slots) :]
    scalars = [
        pltpu.make_async_copy(pick_blk, blk_scalars, scalar_sems.at[0]),
        pltpu.make_async_copy(pick_sub, sub_scalars, scalar_sems.at[1]),
    ]
    for copy in scalars:
        copy.start()
    for copy in scalars:
        copy.wait()
    copies = []
    for place, (axis, step, first, rows) in enumerate(slots):
        pick = take_pick(axis, step, blk_scalars, sub_scalars)
        start = pl.multiple_of(pick * BLOCK + first, math.gcd(BLOCK, first))
        copies.append(pltpu.make_async_copy(embeds.at[pl.ds(start, rows)], outs[place], row_sems.at[place]))
        copies[-1].start()
    for copy in copies:
        copy.wait()


def pick_rows(slots, pick_blk, pick_sub, embeds):
    return pl.pallas_call(
        functools.partial(pick_kernel, slots),
        out_shape=[jax.ShapeDtypeStruct((rows, embeds.shape[1]), embeds.dtype) for _, _, _, rows in slots],
        in_specs=[HBM] * 3,
        out_specs=[VMEM] * len(slots),
        scratch_shapes=[
            pltpu.SMEM(pick_blk.shape, jnp.int32),
            pltpu.SMEM(pick_sub.shape, jnp.int32),
            pltpu.SemaphoreType.DMA((2,)),
            pltpu.SemaphoreType.DMA((len(slots),)),
        ],
        compiler_params=PARAMS,
    )(pick_blk, pick_sub, embeds)


def prepare_kernel(slots, pick_blk, pick_sub, mask_blk, mask_sub, embeds, units, live, mine):
    for start in range(0, embeds.shape[0], BLOCK):
        units[:, start : start + BLOCK] = rounded_units(embeds[start : start + BLOCK]).T
    count = live.shape[1]
    block_of = lax.broadcasted_iota(jnp.int32, mine.shape[1:], 0) // ROWS
    for place, (axis, step, _, _) in enumerate(slots):
        source = lax.axis_index(axis) ^ step
        mask = mask_blk if axis == "blk" else mask_sub
        for i in range(count):
            value = mask[0, source * count + i].astype(jnp.float32)
            live[place, i : i + 1] = jnp.full((1, LANES), value, jnp.float32)
        pick = take_pick(axis, step, pick_blk, pick_sub)
        mine[place] = (block_of == pick).astype(jnp.float32)


def prepare(slots, pick_blk, pick_sub, mask_blk, mask_sub, embeds):
    count = embeds.shape[0] // BLOCK
    return pl.pallas_call(
        functools.partial(prepare_kernel, slots),
        out_shape=[
            jax.ShapeDtypeStruct(embeds.shape[::-1], embeds.dtype),
            jax.ShapeDtypeStruct((len(slots), count, LANES), jnp.float32),
            jax.ShapeDtypeStruct((len(slots), count * ROWS, LANES), jnp.float32),
        ],
        in_specs=[SMEM] * 4 + [VMEM],
        out_specs=[VMEM] * 3,
        compiler_params=PARAMS,
    )(pick_blk, pick_sub, mask_blk, mask_sub, embeds)


def slot_kernel(place, first, rows, back_places, carries, arrived, units, live, mine, totals, *rest):
    new_totals, back = rest[-2:]
    count = live.shape[1]
    before = totals[...]
    for back_place, sums in zip(back_places, rest):
        before = before + mine[back_place] * sums[...]
    new_totals[...] = before
    x = rounded_units(arrived[...])
    along_rows = jnp.zeros((rows, LANES), jnp.float32)
    for i in range(count):
        cosines = jnp.dot(x, units[:, i * BLOCK : (i + 1) * BLOCK], preferred_element_type=jnp.float32)
        weights = soft_weights(cosines)
        alive = live[place, i : i + 1]
        parts = [weights[:, part * LANES : (part + 1) * LANES] for part in range(ROWS)]
        along_rows = along_rows + alive * sum(parts)
        for part, piece in enumerate(parts):
            row = i * ROWS + part
            new_totals[row : row + 1] = new_totals[row : row + 1] + alive * jnp.sum(piece, axis=0, keepdims=True)
    empty = [jnp.zeros((gap, LANES), jnp.float32) for gap in (first, BLOCK - first - rows)]
    along_rows = jnp.concatenate([part for part in (empty[0], along_rows, empty[1]) if part.shape[0]], axis=0)
    for part in range(ROWS):
        sums = jnp.sum(along_rows[part * LANES : (part + 1) * LANES].T, axis=0, keepdims=True)
        for i in range(count):
            row = i * ROWS + part
            back[row : row + 1] = sums + rest[-3][row : row + 1] if carries else sums


def work(place, slot, arrived, units, live, mine, totals, returned, carried):
    operands = [arrived, units, live, mine, totals] + [sums for _, sums in returned]
    operands += [] if carried is None else [carried]
    return pl.pallas_call(
        functools.partial(slot_kernel, place, *slot[2:], [one for one, _ in returned], carried is not None),
        out_shape=[jax.ShapeDtypeStruct(totals.shape, jnp.float32)] * 2,
        in_specs=[VMEM] * len(operands),
        out_specs=[VMEM] * 2,
        compiler_params=PARAMS,
    )(*operands)


BEHIND = 2
FIRST_CUT = 128


def plan_slots(sizes):
    slots = [("blk", 1, 0, BLOCK), ("sub", 2, 0, BLOCK), ("blk", 2, 0, BLOCK), ("sub", 1, 0, BLOCK)]
    slots += [("blk", k, 0, BLOCK) for k in range(3, sizes["blk"])]
    for k in range(3, sizes["sub"]):
        slots += [("sub", k, 0, FIRST_CUT), ("sub", k, FIRST_CUT, BLOCK - FIRST_CUT)]
    return slots


AT_ONCE = 2


def body(embeds, pick_blk, mask_blk, pick_sub, mask_sub):
    count = embeds.shape[0] // BLOCK
    sizes = {"sub": lax.axis_size("sub"), "blk": lax.axis_size("blk")}
    slots = plan_slots(sizes)

    def send(array, slot):
        return lax.ppermute(array, slot[0], pairs(slot[1], sizes[slot[0]]))

    outgoing = first_rows(slots[:AT_ONCE], pick_blk, pick_sub, embeds)
    outgoing += pick_rows(slots[AT_ONCE:], pick_blk, pick_sub, embeds)
    arrived = [send(rows, slot) for rows, slot in zip(outgoing, slots)]

    units, live, mine = prepare(slots, pick_blk, pick_sub, mask_blk, mask_sub, embeds)
    totals = jnp.zeros((count * ROWS, LANES), jnp.float32)
    carried = {}
    waiting, late = [], []
    for place, slot in enumerate(slots):
        axis, step, first, rows = slot
        last = place == len(slots) - 1
        ready = [one for one in waiting if last or one[0] <= place]
        waiting = [one for one in waiting if not last and one[0] > place]
        totals, back = work(
            place, slot, arrived[place], units, live, mine, totals, [one[1:] for one in ready], carried.pop(slot[:2], None)
        )
        if first + rows < BLOCK:
            carried[axis, step] = back
        elif axis == "blk":
            waiting.append((place + BEHIND, place, send(back, slot)))
        else:
            late.append((place, send(back, slot)))
    for place, sums in late:
        totals = totals + mine[place] * sums
    return (totals * (1.0 / BLOCK)).reshape(-1)


def solution(mesh):
    return jax.shard_map(
        body,
        mesh=mesh,
        in_specs=(
            P(("groups", "blk", "sub"), None),
            P(("groups", "blk", "sub"), None),
            P(("groups", "blk", "sub"), None),
            P(("groups", "blk"), None),
            P(("groups", "blk", "sub"), None),
        ),
        out_specs=P(("groups", "blk", "sub")),
        check_vma=False,
    )
```

```python
import functools
import math

import jax
import jax.numpy as jnp
from jax import lax
from jax.experimental import pallas as pl
from jax.experimental.pallas import tpu as pltpu
from jax.sharding import PartitionSpec as P

BLOCK = 256
LANES = 128
ROWS = BLOCK // LANES

cutoff = 0.05
sharpness = 100.0

SMEM = pl.BlockSpec(memory_space=pltpu.SMEM)
VMEM = pl.BlockSpec(memory_space=pltpu.VMEM)
HBM = pl.BlockSpec(memory_space=pltpu.HBM)
ANY = pl.BlockSpec(memory_space=pl.ANY)
PARAMS = pltpu.CompilerParams(vmem_limit_bytes=32 * 2**20)


def pairs(step, size):
    return [(i, i ^ step) for i in range(size)]


def rounded_units(rows):
    wide = rows.astype(jnp.float32)
    scale = lax.rsqrt(jnp.sum(wide * wide, axis=1, keepdims=True) + 1e-06)
    return (wide * scale).astype(jnp.bfloat16)


def soft_weights(cosines):
    rate = sharpness * math.log2(math.e)
    return pltpu.reciprocal(1.0 + jnp.exp2(cutoff * rate - cosines * rate), approx=True)


def take_pick(axis, step, pick_blk, pick_sub):
    target = lax.axis_index(axis) ^ step
    return pick_blk[0, target] if axis == "blk" else pick_sub[lax.axis_index("sub"), target]


def first_kernel(slots, pick_blk, pick_sub, embeds, *rest):
    outs, (blk_scalars, sub_scalars, staged, scalar_sems, in_sems, out_sems) = rest[: len(slots)], rest[len(slots) :]
    scalars = [
        pltpu.make_async_copy(pick_blk, blk_scalars, scalar_sems.at[0]),
        pltpu.make_async_copy(pick_sub, sub_scalars, scalar_sems.at[1]),
    ]
    for copy in scalars:
        copy.start()
    starts = range(0, BLOCK, PART)
    entering = []
    for start in starts:
        for top in range(start, embeds.shape[0], BLOCK):
            rows = pl.ds(top, PART)
            entering.append(pltpu.make_async_copy(embeds.at[rows], staged.at[rows], in_sems.at[len(entering)]))
            entering[-1].start()
    for copy in scalars:
        copy.wait()
    picks = [take_pick(axis, step, blk_scalars, sub_scalars) for axis, step, _, _ in slots]
    count = embeds.shape[0] // BLOCK
    leaving = []
    for turn, start in enumerate(starts):
        for copy in entering[turn * count : (turn + 1) * count]:
            copy.wait()
        for pick, out in zip(picks, outs):
            here = staged.at[pl.ds(pl.multiple_of(pick * BLOCK + start, PART), PART)]
            leaving.append(pltpu.make_async_copy(here, out.at[pl.ds(start, PART)], out_sems.at[len(leaving)]))
            leaving[-1].start()
    for copy in leaving:
        copy.wait()


PART = 128


def first_rows(slots, pick_blk, pick_sub, embeds):
    parts = BLOCK // PART
    return pl.pallas_call(
        functools.partial(first_kernel, slots),
        out_shape=[jax.ShapeDtypeStruct((BLOCK, embeds.shape[1]), embeds.dtype)] * len(slots),
        in_specs=[ANY] * 3,
        out_specs=[ANY] * len(slots),
        scratch_shapes=[
            pltpu.SMEM(pick_blk.shape, jnp.int32),
            pltpu.SMEM(pick_sub.shape, jnp.int32),
            pltpu.VMEM(embeds.shape, embeds.dtype),
            pltpu.SemaphoreType.DMA((2,)),
            pltpu.SemaphoreType.DMA((embeds.shape[0] // PART,)),
            pltpu.SemaphoreType.DMA((len(slots) * parts,)),
        ],
    )(pick_blk, pick_sub, embeds)


def pick_kernel(slots, pick_blk, pick_sub, embeds, *rest):
    outs, (blk_scalars, sub_scalars, scalar_sems, row_sems) = rest[: len(slots)], rest[len(slots) :]
    scalars = [
        pltpu.make_async_copy(pick_blk, blk_scalars, scalar_sems.at[0]),
        pltpu.make_async_copy(pick_sub, sub_scalars, scalar_sems.at[1]),
    ]
    for copy in scalars:
        copy.start()
    for copy in scalars:
        copy.wait()
    copies = []
    for place, (axis, step, first, rows) in enumerate(slots):
        pick = take_pick(axis, step, blk_scalars, sub_scalars)
        start = pl.multiple_of(pick * BLOCK + first, math.gcd(BLOCK, first))
        copies.append(pltpu.make_async_copy(embeds.at[pl.ds(start, rows)], outs[place], row_sems.at[place]))
        copies[-1].start()
    for copy in copies:
        copy.wait()


def pick_rows(slots, pick_blk, pick_sub, embeds):
    return pl.pallas_call(
        functools.partial(pick_kernel, slots),
        out_shape=[jax.ShapeDtypeStruct((rows, embeds.shape[1]), embeds.dtype) for _, _, _, rows in slots],
        in_specs=[HBM] * 3,
        out_specs=[VMEM] * len(slots),
        scratch_shapes=[
            pltpu.SMEM(pick_blk.shape, jnp.int32),
            pltpu.SMEM(pick_sub.shape, jnp.int32),
            pltpu.SemaphoreType.DMA((2,)),
            pltpu.SemaphoreType.DMA((len(slots),)),
        ],
        compiler_params=PARAMS,
    )(pick_blk, pick_sub, embeds)


def prepare_kernel(slots, pick_blk, pick_sub, mask_blk, mask_sub, embeds, units, live, mine):
    for start in range(0, embeds.shape[0], BLOCK):
        units[:, start : start + BLOCK] = rounded_units(embeds[start : start + BLOCK]).T
    count = live.shape[1]
    block_of = lax.broadcasted_iota(jnp.int32, mine.shape[1:], 0) // ROWS
    for place, (axis, step, _, _) in enumerate(slots):
        source = lax.axis_index(axis) ^ step
        mask = mask_blk if axis == "blk" else mask_sub
        for i in range(count):
            value = mask[0, source * count + i].astype(jnp.float32)
            live[place, i : i + 1] = jnp.full((1, LANES), value, jnp.float32)
        pick = take_pick(axis, step, pick_blk, pick_sub)
        mine[place] = (block_of == pick).astype(jnp.float32)


def prepare(slots, pick_blk, pick_sub, mask_blk, mask_sub, embeds):
    count = embeds.shape[0] // BLOCK
    return pl.pallas_call(
        functools.partial(prepare_kernel, slots),
        out_shape=[
            jax.ShapeDtypeStruct(embeds.shape[::-1], embeds.dtype),
            jax.ShapeDtypeStruct((len(slots), count, LANES), jnp.float32),
            jax.ShapeDtypeStruct((len(slots), count * ROWS, LANES), jnp.float32),
        ],
        in_specs=[SMEM] * 4 + [VMEM],
        out_specs=[VMEM] * 3,
        compiler_params=PARAMS,
    )(pick_blk, pick_sub, mask_blk, mask_sub, embeds)


def slot_kernel(place, first, rows, back_places, carries, arrived, units, live, mine, totals, *rest):
    new_totals, back = rest[-2:]
    count = live.shape[1]
    before = totals[...]
    for back_place, sums in zip(back_places, rest):
        before = before + mine[back_place] * sums[...]
    new_totals[...] = before
    x = rounded_units(arrived[...])
    along_rows = jnp.zeros((rows, LANES), jnp.float32)
    for i in range(count):
        cosines = jnp.dot(x, units[:, i * BLOCK : (i + 1) * BLOCK], preferred_element_type=jnp.float32)
        weights = soft_weights(cosines)
        alive = live[place, i : i + 1]
        parts = [weights[:, part * LANES : (part + 1) * LANES] for part in range(ROWS)]
        along_rows = along_rows + alive * sum(parts)
        for part, piece in enumerate(parts):
            row = i * ROWS + part
            new_totals[row : row + 1] = new_totals[row : row + 1] + alive * jnp.sum(piece, axis=0, keepdims=True)
    empty = [jnp.zeros((gap, LANES), jnp.float32) for gap in (first, BLOCK - first - rows)]
    along_rows = jnp.concatenate([part for part in (empty[0], along_rows, empty[1]) if part.shape[0]], axis=0)
    for part in range(ROWS):
        sums = jnp.sum(along_rows[part * LANES : (part + 1) * LANES].T, axis=0, keepdims=True)
        for i in range(count):
            row = i * ROWS + part
            back[row : row + 1] = sums + rest[-3][row : row + 1] if carries else sums


def work(place, slot, arrived, units, live, mine, totals, returned, carried):
    operands = [arrived, units, live, mine, totals] + [sums for _, sums in returned]
    operands += [] if carried is None else [carried]
    return pl.pallas_call(
        functools.partial(slot_kernel, place, *slot[2:], [one for one, _ in returned], carried is not None),
        out_shape=[jax.ShapeDtypeStruct(totals.shape, jnp.float32)] * 2,
        in_specs=[VMEM] * len(operands),
        out_specs=[VMEM] * 2,
        compiler_params=PARAMS,
    )(*operands)


BEHIND = 2
def plan_slots(sizes):
    slots = [("blk", 1, 0, BLOCK), ("sub", 2, 0, BLOCK), ("blk", 2, 0, BLOCK), ("sub", 1, 0, BLOCK)]
    slots += [("blk", k, 0, BLOCK) for k in range(3, sizes["blk"])]
    return slots + [("sub", k, 0, BLOCK) for k in range(3, sizes["sub"])]


AT_ONCE = 2


def body(embeds, pick_blk, mask_blk, pick_sub, mask_sub):
    count = embeds.shape[0] // BLOCK
    sizes = {"sub": lax.axis_size("sub"), "blk": lax.axis_size("blk")}
    slots = plan_slots(sizes)

    def send(array, slot):
        return lax.ppermute(array, slot[0], pairs(slot[1], sizes[slot[0]]))

    outgoing = first_rows(slots[:AT_ONCE], pick_blk, pick_sub, embeds)
    outgoing += pick_rows(slots[AT_ONCE:], pick_blk, pick_sub, embeds)
    arrived = [send(rows, slot) for rows, slot in zip(outgoing, slots)]

    units, live, mine = prepare(slots, pick_blk, pick_sub, mask_blk, mask_sub, embeds)
    totals = jnp.zeros((count * ROWS, LANES), jnp.float32)
    carried = {}
    waiting, late = [], []
    for place, slot in enumerate(slots):
        axis, step, first, rows = slot
        last = place == len(slots) - 1
        ready = [one for one in waiting if last or one[0] <= place]
        waiting = [one for one in waiting if not last and one[0] > place]
        totals, back = work(
            place, slot, arrived[place], units, live, mine, totals, [one[1:] for one in ready], carried.pop(slot[:2], None)
        )
        if first + rows < BLOCK:
            carried[axis, step] = back
        elif axis == "blk":
            waiting.append((place + BEHIND, place, send(back, slot)))
        else:
            late.append((place, send(back, slot)))
    for place, sums in late:
        totals = totals + mine[place] * sums
    return (totals * (1.0 / BLOCK)).reshape(-1)


def solution(mesh):
    return jax.shard_map(
        body,
        mesh=mesh,
        in_specs=(
            P(("groups", "blk", "sub"), None),
            P(("groups", "blk", "sub"), None),
            P(("groups", "blk", "sub"), None),
            P(("groups", "blk"), None),
            P(("groups", "blk", "sub"), None),
        ),
        out_specs=P(("groups", "blk", "sub")),
        check_vma=False,
    )
```

```python
import functools
import math

import jax
import jax.numpy as jnp
from jax import lax
from jax.experimental import pallas as pl
from jax.experimental.pallas import tpu as pltpu
from jax.sharding import PartitionSpec as P

BLOCK = 256
LANES = 128
ROWS = BLOCK // LANES

cutoff = 0.05
sharpness = 100.0

SMEM = pl.BlockSpec(memory_space=pltpu.SMEM)
VMEM = pl.BlockSpec(memory_space=pltpu.VMEM)
HBM = pl.BlockSpec(memory_space=pltpu.HBM)
ANY = pl.BlockSpec(memory_space=pl.ANY)
PARAMS = pltpu.CompilerParams(vmem_limit_bytes=32 * 2**20)


def pairs(step, size):
    return [(i, i ^ step) for i in range(size)]


def rounded_units(rows):
    wide = rows.astype(jnp.float32)
    scale = lax.rsqrt(jnp.sum(wide * wide, axis=1, keepdims=True) + 1e-06)
    return (wide * scale).astype(jnp.bfloat16)


def soft_weights(cosines):
    rate = sharpness * math.log2(math.e)
    return pltpu.reciprocal(1.0 + jnp.exp2(cutoff * rate - cosines * rate), approx=True)


def take_pick(axis, step, pick_blk, pick_sub):
    target = lax.axis_index(axis) ^ step
    return pick_blk[0, target] if axis == "blk" else pick_sub[lax.axis_index("sub"), target]


def first_kernel(slots, pick_blk, pick_sub, embeds, *rest):
    outs, (blk_scalars, sub_scalars, staged, scalar_sems, in_sems, out_sems) = rest[: len(slots)], rest[len(slots) :]
    scalars = [
        pltpu.make_async_copy(pick_blk, blk_scalars, scalar_sems.at[0]),
        pltpu.make_async_copy(pick_sub, sub_scalars, scalar_sems.at[1]),
    ]
    for copy in scalars:
        copy.start()
    starts = range(0, BLOCK, PART)
    entering = []
    for start in starts:
        for top in range(start, embeds.shape[0], BLOCK):
            rows = pl.ds(top, PART)
            entering.append(pltpu.make_async_copy(embeds.at[rows], staged.at[rows], in_sems.at[len(entering)]))
            entering[-1].start()
    for copy in scalars:
        copy.wait()
    picks = [take_pick(axis, step, blk_scalars, sub_scalars) for axis, step, _, _ in slots]
    count = embeds.shape[0] // BLOCK
    leaving = []
    for turn, start in enumerate(starts):
        for copy in entering[turn * count : (turn + 1) * count]:
            copy.wait()
        for pick, out in zip(picks, outs):
            here = staged.at[pl.ds(pl.multiple_of(pick * BLOCK + start, PART), PART)]
            leaving.append(pltpu.make_async_copy(here, out.at[pl.ds(start, PART)], out_sems.at[len(leaving)]))
            leaving[-1].start()
    for copy in leaving:
        copy.wait()


PART = 128


def first_rows(slots, pick_blk, pick_sub, embeds):
    parts = BLOCK // PART
    return pl.pallas_call(
        functools.partial(first_kernel, slots),
        out_shape=[jax.ShapeDtypeStruct((BLOCK, embeds.shape[1]), embeds.dtype)] * len(slots),
        in_specs=[ANY] * 3,
        out_specs=[ANY] * len(slots),
        scratch_shapes=[
            pltpu.SMEM(pick_blk.shape, jnp.int32),
            pltpu.SMEM(pick_sub.shape, jnp.int32),
            pltpu.VMEM(embeds.shape, embeds.dtype),
            pltpu.SemaphoreType.DMA((2,)),
            pltpu.SemaphoreType.DMA((embeds.shape[0] // PART,)),
            pltpu.SemaphoreType.DMA((len(slots) * parts,)),
        ],
    )(pick_blk, pick_sub, embeds)


def pick_kernel(slots, pick_blk, pick_sub, embeds, *rest):
    outs, (blk_scalars, sub_scalars, scalar_sems, row_sems) = rest[: len(slots)], rest[len(slots) :]
    scalars = [
        pltpu.make_async_copy(pick_blk, blk_scalars, scalar_sems.at[0]),
        pltpu.make_async_copy(pick_sub, sub_scalars, scalar_sems.at[1]),
    ]
    for copy in scalars:
        copy.start()
    for copy in scalars:
        copy.wait()
    copies = []
    for place, (axis, step, first, rows) in enumerate(slots):
        pick = take_pick(axis, step, blk_scalars, sub_scalars)
        start = pl.multiple_of(pick * BLOCK + first, math.gcd(BLOCK, first))
        copies.append(pltpu.make_async_copy(embeds.at[pl.ds(start, rows)], outs[place], row_sems.at[place]))
        copies[-1].start()
    for copy in copies:
        copy.wait()


def pick_rows(slots, pick_blk, pick_sub, embeds):
    return pl.pallas_call(
        functools.partial(pick_kernel, slots),
        out_shape=[jax.ShapeDtypeStruct((rows, embeds.shape[1]), embeds.dtype) for _, _, _, rows in slots],
        in_specs=[HBM] * 3,
        out_specs=[VMEM] * len(slots),
        scratch_shapes=[
            pltpu.SMEM(pick_blk.shape, jnp.int32),
            pltpu.SMEM(pick_sub.shape, jnp.int32),
            pltpu.SemaphoreType.DMA((2,)),
            pltpu.SemaphoreType.DMA((len(slots),)),
        ],
        compiler_params=PARAMS,
    )(pick_blk, pick_sub, embeds)


def prepare_kernel(slots, pick_blk, pick_sub, mask_blk, mask_sub, embeds, units, live, mine):
    for start in range(0, embeds.shape[0], BLOCK):
        units[:, start : start + BLOCK] = rounded_units(embeds[start : start + BLOCK]).T
    count = live.shape[1]
    block_of = lax.broadcasted_iota(jnp.int32, mine.shape[1:], 0) // ROWS
    for place, (axis, step, _, _) in enumerate(slots):
        source = lax.axis_index(axis) ^ step
        mask = mask_blk if axis == "blk" else mask_sub
        for i in range(count):
            value = mask[0, source * count + i].astype(jnp.float32)
            live[place, i : i + 1] = jnp.full((1, LANES), value, jnp.float32)
        pick = take_pick(axis, step, pick_blk, pick_sub)
        mine[place] = (block_of == pick).astype(jnp.float32)


def prepare(slots, pick_blk, pick_sub, mask_blk, mask_sub, embeds):
    count = embeds.shape[0] // BLOCK
    return pl.pallas_call(
        functools.partial(prepare_kernel, slots),
        out_shape=[
            jax.ShapeDtypeStruct(embeds.shape[::-1], embeds.dtype),
            jax.ShapeDtypeStruct((len(slots), count, LANES), jnp.float32),
            jax.ShapeDtypeStruct((len(slots), count * ROWS, LANES), jnp.float32),
        ],
        in_specs=[SMEM] * 4 + [VMEM],
        out_specs=[VMEM] * 3,
        compiler_params=PARAMS,
    )(pick_blk, pick_sub, mask_blk, mask_sub, embeds)


def slot_kernel(place, first, rows, back_places, carries, arrived, units, live, mine, totals, *rest):
    new_totals, back = rest[-2:]
    count = live.shape[1]
    before = totals[...]
    for back_place, sums in zip(back_places, rest):
        before = before + mine[back_place] * sums[...]
    new_totals[...] = before
    x = rounded_units(arrived[...])
    along_rows = jnp.zeros((rows, LANES), jnp.float32)
    for i in range(count):
        cosines = jnp.dot(x, units[:, i * BLOCK : (i + 1) * BLOCK], preferred_element_type=jnp.float32)
        weights = soft_weights(cosines)
        alive = live[place, i : i + 1]
        parts = [weights[:, part * LANES : (part + 1) * LANES] for part in range(ROWS)]
        along_rows = along_rows + alive * sum(parts)
        for part, piece in enumerate(parts):
            row = i * ROWS + part
            new_totals[row : row + 1] = new_totals[row : row + 1] + alive * jnp.sum(piece, axis=0, keepdims=True)
    empty = [jnp.zeros((gap, LANES), jnp.float32) for gap in (first, BLOCK - first - rows)]
    along_rows = jnp.concatenate([part for part in (empty[0], along_rows, empty[1]) if part.shape[0]], axis=0)
    for part in range(ROWS):
        sums = jnp.sum(along_rows[part * LANES : (part + 1) * LANES].T, axis=0, keepdims=True)
        for i in range(count):
            row = i * ROWS + part
            back[row : row + 1] = sums + rest[-3][row : row + 1] if carries else sums


def work(place, slot, arrived, units, live, mine, totals, returned, carried):
    operands = [arrived, units, live, mine, totals] + [sums for _, sums in returned]
    operands += [] if carried is None else [carried]
    return pl.pallas_call(
        functools.partial(slot_kernel, place, *slot[2:], [one for one, _ in returned], carried is not None),
        out_shape=[jax.ShapeDtypeStruct(totals.shape, jnp.float32)] * 2,
        in_specs=[VMEM] * len(operands),
        out_specs=[VMEM] * 2,
        compiler_params=PARAMS,
    )(*operands)


BEHIND = 2
FIRST_CUT = 192


def plan_slots(sizes):
    slots = [("blk", 1, 0, BLOCK), ("sub", 2, 0, BLOCK), ("blk", 2, 0, BLOCK), ("sub", 1, 0, BLOCK)]
    slots += [("blk", k, 0, BLOCK) for k in range(3, sizes["blk"])]
    for k in range(3, sizes["sub"]):
        slots += [("sub", k, 0, FIRST_CUT), ("sub", k, FIRST_CUT, BLOCK - FIRST_CUT)]
    return slots


AT_ONCE = 2


def body(embeds, pick_blk, mask_blk, pick_sub, mask_sub):
    count = embeds.shape[0] // BLOCK
    sizes = {"sub": lax.axis_size("sub"), "blk": lax.axis_size("blk")}
    slots = plan_slots(sizes)

    def send(array, slot):
        return lax.ppermute(array, slot[0], pairs(slot[1], sizes[slot[0]]))

    outgoing = first_rows(slots[:AT_ONCE], pick_blk, pick_sub, embeds)
    outgoing += pick_rows(slots[AT_ONCE:], pick_blk, pick_sub, embeds)
    arrived = [send(rows, slot) for rows, slot in zip(outgoing, slots)]

    units, live, mine = prepare(slots, pick_blk, pick_sub, mask_blk, mask_sub, embeds)
    totals = jnp.zeros((count * ROWS, LANES), jnp.float32)
    carried = {}
    waiting, late = [], []
    for place, slot in enumerate(slots):
        axis, step, first, rows = slot
        last = place == len(slots) - 1
        ready = [one for one in waiting if last or one[0] <= place]
        waiting = [one for one in waiting if not last and one[0] > place]
        totals, back = work(
            place, slot, arrived[place], units, live, mine, totals, [one[1:] for one in ready], carried.pop(slot[:2], None)
        )
        if first + rows < BLOCK:
            carried[axis, step] = back
        elif axis == "blk":
            waiting.append((place + BEHIND, place, send(back, slot)))
        else:
            late.append((place, send(back, slot)))
    for place, sums in late:
        totals = totals + mine[place] * sums
    return (totals * (1.0 / BLOCK)).reshape(-1)


def solution(mesh):
    return jax.shard_map(
        body,
        mesh=mesh,
        in_specs=(
            P(("groups", "blk", "sub"), None),
            P(("groups", "blk", "sub"), None),
            P(("groups", "blk", "sub"), None),
            P(("groups", "blk"), None),
            P(("groups", "blk", "sub"), None),
        ),
        out_specs=P(("groups", "blk", "sub")),
        check_vma=False,
    )
```

```python
import functools
import math

import jax
import jax.numpy as jnp
from jax import lax
from jax.experimental import pallas as pl
from jax.experimental.pallas import tpu as pltpu
from jax.sharding import PartitionSpec as P

BLOCK = 256
LANES = 128
ROWS = BLOCK // LANES

cutoff = 0.05
sharpness = 100.0

SMEM = pl.BlockSpec(memory_space=pltpu.SMEM)
VMEM = pl.BlockSpec(memory_space=pltpu.VMEM)
HBM = pl.BlockSpec(memory_space=pltpu.HBM)
ANY = pl.BlockSpec(memory_space=pl.ANY)
PARAMS = pltpu.CompilerParams(vmem_limit_bytes=32 * 2**20)


def pairs(step, size):
    return [(i, i ^ step) for i in range(size)]


def rounded_units(rows):
    wide = rows.astype(jnp.float32)
    scale = lax.rsqrt(jnp.sum(wide * wide, axis=1, keepdims=True) + 1e-06)
    return (wide * scale).astype(jnp.bfloat16)


def soft_weights(cosines):
    rate = sharpness * math.log2(math.e)
    return pltpu.reciprocal(1.0 + jnp.exp2(cutoff * rate - cosines * rate), approx=True)


def take_pick(axis, step, pick_blk, pick_sub):
    target = lax.axis_index(axis) ^ step
    return pick_blk[0, target] if axis == "blk" else pick_sub[lax.axis_index("sub"), target]


def first_kernel(slots, pick_blk, pick_sub, embeds, *rest):
    outs, (blk_scalars, sub_scalars, staged, scalar_sems, in_sems, out_sems) = rest[: len(slots)], rest[len(slots) :]
    scalars = [
        pltpu.make_async_copy(pick_blk, blk_scalars, scalar_sems.at[0]),
        pltpu.make_async_copy(pick_sub, sub_scalars, scalar_sems.at[1]),
    ]
    for copy in scalars:
        copy.start()
    starts = range(0, BLOCK, PART)
    entering = []
    for start in starts:
        for top in range(start, embeds.shape[0], BLOCK):
            rows = pl.ds(top, PART)
            entering.append(pltpu.make_async_copy(embeds.at[rows], staged.at[rows], in_sems.at[len(entering)]))
            entering[-1].start()
    for copy in scalars:
        copy.wait()
    picks = [take_pick(axis, step, blk_scalars, sub_scalars) for axis, step, _, _ in slots]
    count = embeds.shape[0] // BLOCK
    leaving = []
    for turn, start in enumerate(starts):
        for copy in entering[turn * count : (turn + 1) * count]:
            copy.wait()
        for pick, out in zip(picks, outs):
            here = staged.at[pl.ds(pl.multiple_of(pick * BLOCK + start, PART), PART)]
            leaving.append(pltpu.make_async_copy(here, out.at[pl.ds(start, PART)], out_sems.at[len(leaving)]))
            leaving[-1].start()
    for copy in leaving:
        copy.wait()


PART = 128


def first_rows(slots, pick_blk, pick_sub, embeds):
    parts = BLOCK // PART
    return pl.pallas_call(
        functools.partial(first_kernel, slots),
        out_shape=[jax.ShapeDtypeStruct((BLOCK, embeds.shape[1]), embeds.dtype)] * len(slots),
        in_specs=[ANY] * 3,
        out_specs=[ANY] * len(slots),
        scratch_shapes=[
            pltpu.SMEM(pick_blk.shape, jnp.int32),
            pltpu.SMEM(pick_sub.shape, jnp.int32),
            pltpu.VMEM(embeds.shape, embeds.dtype),
            pltpu.SemaphoreType.DMA((2,)),
            pltpu.SemaphoreType.DMA((embeds.shape[0] // PART,)),
            pltpu.SemaphoreType.DMA((len(slots) * parts,)),
        ],
    )(pick_blk, pick_sub, embeds)


def pick_kernel(slots, pick_blk, pick_sub, embeds, *rest):
    outs, (blk_scalars, sub_scalars, scalar_sems, row_sems) = rest[: len(slots)], rest[len(slots) :]
    scalars = [
        pltpu.make_async_copy(pick_blk, blk_scalars, scalar_sems.at[0]),
        pltpu.make_async_copy(pick_sub, sub_scalars, scalar_sems.at[1]),
    ]
    for copy in scalars:
        copy.start()
    for copy in scalars:
        copy.wait()
    copies = []
    for place, (axis, step, first, rows) in enumerate(slots):
        pick = take_pick(axis, step, blk_scalars, sub_scalars)
        start = pl.multiple_of(pick * BLOCK + first, math.gcd(BLOCK, first))
        copies.append(pltpu.make_async_copy(embeds.at[pl.ds(start, rows)], outs[place], row_sems.at[place]))
        copies[-1].start()
    for copy in copies:
        copy.wait()


def pick_rows(slots, pick_blk, pick_sub, embeds):
    return pl.pallas_call(
        functools.partial(pick_kernel, slots),
        out_shape=[jax.ShapeDtypeStruct((rows, embeds.shape[1]), embeds.dtype) for _, _, _, rows in slots],
        in_specs=[HBM] * 3,
        out_specs=[VMEM] * len(slots),
        scratch_shapes=[
            pltpu.SMEM(pick_blk.shape, jnp.int32),
            pltpu.SMEM(pick_sub.shape, jnp.int32),
            pltpu.SemaphoreType.DMA((2,)),
            pltpu.SemaphoreType.DMA((len(slots),)),
        ],
        compiler_params=PARAMS,
    )(pick_blk, pick_sub, embeds)


def prepare_kernel(slots, pick_blk, pick_sub, mask_blk, mask_sub, embeds, units, live, mine):
    for start in range(0, embeds.shape[0], BLOCK):
        units[:, start : start + BLOCK] = rounded_units(embeds[start : start + BLOCK]).T
    count = live.shape[1]
    block_of = lax.broadcasted_iota(jnp.int32, mine.shape[1:], 0) // ROWS
    for place, (axis, step, _, _) in enumerate(slots):
        source = lax.axis_index(axis) ^ step
        mask = mask_blk if axis == "blk" else mask_sub
        for i in range(count):
            value = mask[0, source * count + i].astype(jnp.float32)
            live[place, i : i + 1] = jnp.full((1, LANES), value, jnp.float32)
        pick = take_pick(axis, step, pick_blk, pick_sub)
        mine[place] = (block_of == pick).astype(jnp.float32)


def prepare(slots, pick_blk, pick_sub, mask_blk, mask_sub, embeds):
    count = embeds.shape[0] // BLOCK
    return pl.pallas_call(
        functools.partial(prepare_kernel, slots),
        out_shape=[
            jax.ShapeDtypeStruct(embeds.shape[::-1], embeds.dtype),
            jax.ShapeDtypeStruct((len(slots), count, LANES), jnp.float32),
            jax.ShapeDtypeStruct((len(slots), count * ROWS, LANES), jnp.float32),
        ],
        in_specs=[SMEM] * 4 + [VMEM],
        out_specs=[VMEM] * 3,
        compiler_params=PARAMS,
    )(pick_blk, pick_sub, mask_blk, mask_sub, embeds)


def slot_kernel(place, first, rows, back_places, carries, arrived, units, live, mine, totals, *rest):
    new_totals, back = rest[-2:]
    count = live.shape[1]
    before = totals[...]
    for back_place, sums in zip(back_places, rest):
        before = before + mine[back_place] * sums[...]
    new_totals[...] = before
    x = rounded_units(arrived[...])
    along_rows = jnp.zeros((rows, LANES), jnp.float32)
    for i in range(count):
        cosines = jnp.dot(x, units[:, i * BLOCK : (i + 1) * BLOCK], preferred_element_type=jnp.float32)
        weights = soft_weights(cosines)
        alive = live[place, i : i + 1]
        parts = [weights[:, part * LANES : (part + 1) * LANES] for part in range(ROWS)]
        along_rows = along_rows + alive * sum(parts)
        for part, piece in enumerate(parts):
            row = i * ROWS + part
            new_totals[row : row + 1] = new_totals[row : row + 1] + alive * jnp.sum(piece, axis=0, keepdims=True)
    empty = [jnp.zeros((gap, LANES), jnp.float32) for gap in (first, BLOCK - first - rows)]
    along_rows = jnp.concatenate([part for part in (empty[0], along_rows, empty[1]) if part.shape[0]], axis=0)
    for part in range(ROWS):
        sums = jnp.sum(along_rows[part * LANES : (part + 1) * LANES].T, axis=0, keepdims=True)
        for i in range(count):
            row = i * ROWS + part
            back[row : row + 1] = sums + rest[-3][row : row + 1] if carries else sums


def work(place, slot, arrived, units, live, mine, totals, returned, carried):
    operands = [arrived, units, live, mine, totals] + [sums for _, sums in returned]
    operands += [] if carried is None else [carried]
    return pl.pallas_call(
        functools.partial(slot_kernel, place, *slot[2:], [one for one, _ in returned], carried is not None),
        out_shape=[jax.ShapeDtypeStruct(totals.shape, jnp.float32)] * 2,
        in_specs=[VMEM] * len(operands),
        out_specs=[VMEM] * 2,
        compiler_params=PARAMS,
    )(*operands)


BEHIND = 3
FIRST_CUT = 128


def plan_slots(sizes):
    slots = [("blk", 1, 0, BLOCK), ("sub", 2, 0, BLOCK), ("blk", 2, 0, BLOCK), ("sub", 1, 0, BLOCK)]
    slots += [("blk", k, 0, BLOCK) for k in range(3, sizes["blk"])]
    for k in range(3, sizes["sub"]):
        slots += [("sub", k, 0, FIRST_CUT), ("sub", k, FIRST_CUT, BLOCK - FIRST_CUT)]
    return slots


AT_ONCE = 2


def body(embeds, pick_blk, mask_blk, pick_sub, mask_sub):
    count = embeds.shape[0] // BLOCK
    sizes = {"sub": lax.axis_size("sub"), "blk": lax.axis_size("blk")}
    slots = plan_slots(sizes)

    def send(array, slot):
        return lax.ppermute(array, slot[0], pairs(slot[1], sizes[slot[0]]))

    outgoing = first_rows(slots[:AT_ONCE], pick_blk, pick_sub, embeds)
    outgoing += pick_rows(slots[AT_ONCE:], pick_blk, pick_sub, embeds)
    arrived = [send(rows, slot) for rows, slot in zip(outgoing, slots)]

    units, live, mine = prepare(slots, pick_blk, pick_sub, mask_blk, mask_sub, embeds)
    totals = jnp.zeros((count * ROWS, LANES), jnp.float32)
    carried = {}
    waiting, late = [], []
    for place, slot in enumerate(slots):
        axis, step, first, rows = slot
        last = place == len(slots) - 1
        ready = [one for one in waiting if last or one[0] <= place]
        waiting = [one for one in waiting if not last and one[0] > place]
        totals, back = work(
            place, slot, arrived[place], units, live, mine, totals, [one[1:] for one in ready], carried.pop(slot[:2], None)
        )
        if first + rows < BLOCK:
            carried[axis, step] = back
        elif axis == "blk":
            waiting.append((place + BEHIND, place, send(back, slot)))
        else:
            late.append((place, send(back, slot)))
    for place, sums in late:
        totals = totals + mine[place] * sums
    return (totals * (1.0 / BLOCK)).reshape(-1)


def solution(mesh):
    return jax.shard_map(
        body,
        mesh=mesh,
        in_specs=(
            P(("groups", "blk", "sub"), None),
            P(("groups", "blk", "sub"), None),
            P(("groups", "blk", "sub"), None),
            P(("groups", "blk"), None),
            P(("groups", "blk", "sub"), None),
        ),
        out_specs=P(("groups", "blk", "sub")),
        check_vma=False,
    )
```

```python
import functools
import math

import jax
import jax.numpy as jnp
from jax import lax
from jax.experimental import pallas as pl
from jax.experimental.pallas import tpu as pltpu
from jax.sharding import PartitionSpec as P

BLOCK = 256
LANES = 128
ROWS = BLOCK // LANES

cutoff = 0.05
sharpness = 100.0

SMEM = pl.BlockSpec(memory_space=pltpu.SMEM)
VMEM = pl.BlockSpec(memory_space=pltpu.VMEM)
HBM = pl.BlockSpec(memory_space=pltpu.HBM)
ANY = pl.BlockSpec(memory_space=pl.ANY)
PARAMS = pltpu.CompilerParams(vmem_limit_bytes=32 * 2**20)


def pairs(step, size):
    return [(i, i ^ step) for i in range(size)]


def rounded_units(rows):
    wide = rows.astype(jnp.float32)
    scale = lax.rsqrt(jnp.sum(wide * wide, axis=1, keepdims=True) + 1e-06)
    return (wide * scale).astype(jnp.bfloat16)


def soft_weights(cosines):
    rate = sharpness * math.log2(math.e)
    return pltpu.reciprocal(1.0 + jnp.exp2(cutoff * rate - cosines * rate), approx=True)


def take_pick(axis, step, pick_blk, pick_sub):
    target = lax.axis_index(axis) ^ step
    return pick_blk[0, target] if axis == "blk" else pick_sub[lax.axis_index("sub"), target]


def first_kernel(slots, pick_blk, pick_sub, embeds, *rest):
    outs, (blk_scalars, sub_scalars, staged, scalar_sems, in_sems, out_sems) = rest[: len(slots)], rest[len(slots) :]
    scalars = [
        pltpu.make_async_copy(pick_blk, blk_scalars, scalar_sems.at[0]),
        pltpu.make_async_copy(pick_sub, sub_scalars, scalar_sems.at[1]),
    ]
    for copy in scalars:
        copy.start()
    starts = range(0, BLOCK, PART)
    entering = []
    for start in starts:
        for top in range(start, embeds.shape[0], BLOCK):
            rows = pl.ds(top, PART)
            entering.append(pltpu.make_async_copy(embeds.at[rows], staged.at[rows], in_sems.at[len(entering)]))
            entering[-1].start()
    for copy in scalars:
        copy.wait()
    picks = [take_pick(axis, step, blk_scalars, sub_scalars) for axis, step, _, _ in slots]
    count = embeds.shape[0] // BLOCK
    leaving = []
    for turn, start in enumerate(starts):
        for copy in entering[turn * count : (turn + 1) * count]:
            copy.wait()
        for pick, out in zip(picks, outs):
            here = staged.at[pl.ds(pl.multiple_of(pick * BLOCK + start, PART), PART)]
            leaving.append(pltpu.make_async_copy(here, out.at[pl.ds(start, PART)], out_sems.at[len(leaving)]))
            leaving[-1].start()
    for copy in leaving:
        copy.wait()


PART = 256


def first_rows(slots, pick_blk, pick_sub, embeds):
    parts = BLOCK // PART
    return pl.pallas_call(
        functools.partial(first_kernel, slots),
        out_shape=[jax.ShapeDtypeStruct((BLOCK, embeds.shape[1]), embeds.dtype)] * len(slots),
        in_specs=[ANY] * 3,
        out_specs=[ANY] * len(slots),
        scratch_shapes=[
            pltpu.SMEM(pick_blk.shape, jnp.int32),
            pltpu.SMEM(pick_sub.shape, jnp.int32),
            pltpu.VMEM(embeds.shape, embeds.dtype),
            pltpu.SemaphoreType.DMA((2,)),
            pltpu.SemaphoreType.DMA((embeds.shape[0] // PART,)),
            pltpu.SemaphoreType.DMA((len(slots) * parts,)),
        ],
    )(pick_blk, pick_sub, embeds)


def pick_kernel(slots, pick_blk, pick_sub, embeds, *rest):
    outs, (blk_scalars, sub_scalars, scalar_sems, row_sems) = rest[: len(slots)], rest[len(slots) :]
    scalars = [
        pltpu.make_async_copy(pick_blk, blk_scalars, scalar_sems.at[0]),
        pltpu.make_async_copy(pick_sub, sub_scalars, scalar_sems.at[1]),
    ]
    for copy in scalars:
        copy.start()
    for copy in scalars:
        copy.wait()
    copies = []
    for place, (axis, step, first, rows) in enumerate(slots):
        pick = take_pick(axis, step, blk_scalars, sub_scalars)
        start = pl.multiple_of(pick * BLOCK + first, math.gcd(BLOCK, first))
        copies.append(pltpu.make_async_copy(embeds.at[pl.ds(start, rows)], outs[place], row_sems.at[place]))
        copies[-1].start()
    for copy in copies:
        copy.wait()


def pick_rows(slots, pick_blk, pick_sub, embeds):
    return pl.pallas_call(
        functools.partial(pick_kernel, slots),
        out_shape=[jax.ShapeDtypeStruct((rows, embeds.shape[1]), embeds.dtype) for _, _, _, rows in slots],
        in_specs=[HBM] * 3,
        out_specs=[VMEM] * len(slots),
        scratch_shapes=[
            pltpu.SMEM(pick_blk.shape, jnp.int32),
            pltpu.SMEM(pick_sub.shape, jnp.int32),
            pltpu.SemaphoreType.DMA((2,)),
            pltpu.SemaphoreType.DMA((len(slots),)),
        ],
        compiler_params=PARAMS,
    )(pick_blk, pick_sub, embeds)


def prepare_kernel(slots, pick_blk, pick_sub, mask_blk, mask_sub, embeds, units, live, mine):
    for start in range(0, embeds.shape[0], BLOCK):
        units[:, start : start + BLOCK] = rounded_units(embeds[start : start + BLOCK]).T
    count = live.shape[1]
    block_of = lax.broadcasted_iota(jnp.int32, mine.shape[1:], 0) // ROWS
    for place, (axis, step, _, _) in enumerate(slots):
        source = lax.axis_index(axis) ^ step
        mask = mask_blk if axis == "blk" else mask_sub
        for i in range(count):
            value = mask[0, source * count + i].astype(jnp.float32)
            live[place, i : i + 1] = jnp.full((1, LANES), value, jnp.float32)
        pick = take_pick(axis, step, pick_blk, pick_sub)
        mine[place] = (block_of == pick).astype(jnp.float32)


def prepare(slots, pick_blk, pick_sub, mask_blk, mask_sub, embeds):
    count = embeds.shape[0] // BLOCK
    return pl.pallas_call(
        functools.partial(prepare_kernel, slots),
        out_shape=[
            jax.ShapeDtypeStruct(embeds.shape[::-1], embeds.dtype),
            jax.ShapeDtypeStruct((len(slots), count, LANES), jnp.float32),
            jax.ShapeDtypeStruct((len(slots), count * ROWS, LANES), jnp.float32),
        ],
        in_specs=[SMEM] * 4 + [VMEM],
        out_specs=[VMEM] * 3,
        compiler_params=PARAMS,
    )(pick_blk, pick_sub, mask_blk, mask_sub, embeds)


def slot_kernel(place, first, rows, back_places, carries, arrived, units, live, mine, totals, *rest):
    new_totals, back = rest[-2:]
    count = live.shape[1]
    before = totals[...]
    for back_place, sums in zip(back_places, rest):
        before = before + mine[back_place] * sums[...]
    new_totals[...] = before
    x = rounded_units(arrived[...])
    along_rows = jnp.zeros((rows, LANES), jnp.float32)
    for i in range(count):
        cosines = jnp.dot(x, units[:, i * BLOCK : (i + 1) * BLOCK], preferred_element_type=jnp.float32)
        weights = soft_weights(cosines)
        alive = live[place, i : i + 1]
        parts = [weights[:, part * LANES : (part + 1) * LANES] for part in range(ROWS)]
        along_rows = along_rows + alive * sum(parts)
        for part, piece in enumerate(parts):
            row = i * ROWS + part
            new_totals[row : row + 1] = new_totals[row : row + 1] + alive * jnp.sum(piece, axis=0, keepdims=True)
    empty = [jnp.zeros((gap, LANES), jnp.float32) for gap in (first, BLOCK - first - rows)]
    along_rows = jnp.concatenate([part for part in (empty[0], along_rows, empty[1]) if part.shape[0]], axis=0)
    for part in range(ROWS):
        sums = jnp.sum(along_rows[part * LANES : (part + 1) * LANES].T, axis=0, keepdims=True)
        for i in range(count):
            row = i * ROWS + part
            back[row : row + 1] = sums + rest[-3][row : row + 1] if carries else sums


def work(place, slot, arrived, units, live, mine, totals, returned, carried):
    operands = [arrived, units, live, mine, totals] + [sums for _, sums in returned]
    operands += [] if carried is None else [carried]
    return pl.pallas_call(
        functools.partial(slot_kernel, place, *slot[2:], [one for one, _ in returned], carried is not None),
        out_shape=[jax.ShapeDtypeStruct(totals.shape, jnp.float32)] * 2,
        in_specs=[VMEM] * len(operands),
        out_specs=[VMEM] * 2,
        compiler_params=PARAMS,
    )(*operands)


BEHIND = 2
FIRST_CUT = 128


def plan_slots(sizes):
    slots = [("blk", 1, 0, BLOCK), ("sub", 2, 0, BLOCK), ("sub", 1, 0, BLOCK)]
    slots += [("blk", k, 0, BLOCK) for k in range(2, sizes["blk"])]
    for k in range(3, sizes["sub"]):
        slots += [("sub", k, 0, FIRST_CUT), ("sub", k, FIRST_CUT, BLOCK - FIRST_CUT)]
    return slots


AT_ONCE = 2


def body(embeds, pick_blk, mask_blk, pick_sub, mask_sub):
    count = embeds.shape[0] // BLOCK
    sizes = {"sub": lax.axis_size("sub"), "blk": lax.axis_size("blk")}
    slots = plan_slots(sizes)

    def send(array, slot):
        return lax.ppermute(array, slot[0], pairs(slot[1], sizes[slot[0]]))

    outgoing = first_rows(slots[:AT_ONCE], pick_blk, pick_sub, embeds)
    outgoing += pick_rows(slots[AT_ONCE:], pick_blk, pick_sub, embeds)
    arrived = [send(rows, slot) for rows, slot in zip(outgoing, slots)]

    units, live, mine = prepare(slots, pick_blk, pick_sub, mask_blk, mask_sub, embeds)
    totals = jnp.zeros((count * ROWS, LANES), jnp.float32)
    carried = {}
    waiting, late = [], []
    for place, slot in enumerate(slots):
        axis, step, first, rows = slot
        last = place == len(slots) - 1
        ready = [one for one in waiting if last or one[0] <= place]
        waiting = [one for one in waiting if not last and one[0] > place]
        totals, back = work(
            place, slot, arrived[place], units, live, mine, totals, [one[1:] for one in ready], carried.pop(slot[:2], None)
        )
        if first + rows < BLOCK:
            carried[axis, step] = back
        elif axis == "blk":
            waiting.append((place + BEHIND, place, send(back, slot)))
        else:
            late.append((place, send(back, slot)))
    for place, sums in late:
        totals = totals + mine[place] * sums
    return (totals * (1.0 / BLOCK)).reshape(-1)


def solution(mesh):
    return jax.shard_map(
        body,
        mesh=mesh,
        in_specs=(
            P(("groups", "blk", "sub"), None),
            P(("groups", "blk", "sub"), None),
            P(("groups", "blk", "sub"), None),
            P(("groups", "blk"), None),
            P(("groups", "blk", "sub"), None),
        ),
        out_specs=P(("groups", "blk", "sub")),
        check_vma=False,
    )
```
